32 devices in a mesh: clip: 16 (over z, x, core), tile: 2 (over y).
Axes of the slice: x: 2, y: 2, z: 4, core: 2. Of those that a mesh axis runs over, the one named last changes fastest.
Arguments:
- latents: bfloat16 [32, 40, 64, 320], P('clip', 'tile'), may hold values from -64 to 64
- lengths: int32 [16], P('clip'), may hold values from 1 to 2, as said below
- context: int32 [8], replicated, may hold values from 0 to 31, as said below
- gain_first: float32 [320], replicated, may hold values from 0.25 to 1.75
- conv_first: bfloat16 [3, 3, 320, 320], replicated, may hold values from -0.109375 to 0.109375
- gain_second: float32 [320], replicated, may hold values from 0.25 to 1.75
- conv_second: bfloat16 [3, 3, 320, 320], replicated, may hold values from -0.109375 to 0.109375
- time_weight: bfloat16 [3, 320, 320], replicated, may hold values from -0.1875 to 0.1875
- attn_gain: float32 [320], replicated, may hold values from 0.25 to 1.75
- w_qkv: bfloat16 [320, 960], replicated, may hold values from -2 to 2
- w_out: bfloat16 [320, 320], replicated, may hold values from -0.3125 to 0.3125
Outputs:
- block_out: bfloat16 [32, 40, 64, 320], P('clip', 'tile')
The draws below stay inside these ranges and needn't reach their ends.
Inputs may be any that keep to these rules, and one draw needn't show every extreme that they name: `lengths`: the last clip is full with 2 live frames and some other clip has 1. The context frames lie in distinct clips; each names slot c * 2 + f of a live frame f < lengths[c].
All inputs are finite; a program needn't handle non-finite values.
Results may differ from the reference program's by a relative error of at most 0.011.
Values may be sent and summed in bfloat16 or wider, within the bound.
No kernel may reach another device: no remote copies, remote signals or barrier semaphores. Data moves between devices by JAX's collectives and lax.ppermute only.
A program may use at most 128 MiB of HBM per device.

```python
import math
import jax
import jax.numpy as jnp
from jax import lax

C = 320
HEAD_DIM = 64
GROUPS = 32
H = 40
W = 64
F_CAP = 2
NCTX = 8
CLIPS = 16
FRAMES = 32


def clip_plan(key):
    base_key = jax.random.fold_in(key, 101)
    key_len, key_half, key_clip, key_slot = jax.random.split(base_key, 4)
    half_cap = F_CAP // 2
    counts = half_cap + jax.random.randint(key_len, (CLIPS,), 0, F_CAP - half_cap + 1)
    half_clip = 1 + jax.random.randint(key_half, (), 0, CLIPS - 2)
    counts = counts.at[CLIPS - 1].set(F_CAP).at[half_clip].set(half_cap)
    middle = 1 + jax.random.permutation(key_clip, CLIPS - 2)[:NCTX - 2]
    chosen = jnp.concatenate([jnp.zeros((1,), jnp.int32), middle.astype(jnp.int32), jnp.full((1,), CLIPS - 1, jnp.int32)])
    offsets = jax.random.randint(key_slot, (NCTX,), 0, F_CAP) % counts[chosen]
    offsets = offsets.at[0].set(0).at[NCTX - 1].set(F_CAP - 1)
    return (counts.astype(jnp.int32), (chosen * F_CAP + offsets).astype(jnp.int32))


def draw_lengths(key, part):
    return clip_plan(key)[0]


def draw_context(key, part):
    return clip_plan(key)[1]


def draw_latents(key, part):
    key_noise, key_chan, key_row, key_frame = jax.random.split(jax.random.fold_in(key, 202), 4)
    shape_full = (FRAMES, H, W, C)
    noise = jnp.clip(jax.random.normal(key_noise, shape_full), -4.0, 4.0)
    channel_scale = jnp.exp(jax.random.uniform(key_chan, (C,), minval=math.log(0.3), maxval=math.log(3.0)))
    rising = 3.0 ** (jnp.arange(H).astype(jnp.float32) / (H - 1))
    row_scale = rising * jax.random.uniform(key_row, (H,), minval=0.7, maxval=1.4) / 1.7
    frame_scale = jnp.exp(jax.random.uniform(key_frame, (FRAMES,), minval=math.log(0.5), maxval=math.log(2.0)))
    values = noise * frame_scale[:, None, None, None] * row_scale[None, :, None, None] * channel_scale
    return jnp.clip(values, -64.0, 64.0).astype(jnp.bfloat16)


def draw_w_qkv(key, part):
    key_base = jax.random.fold_in(jax.random.fold_in(key, 303), 0)
    weights = jnp.clip(jax.random.normal(key_base, (C, 3 * C)), -6.0, 6.0) * C ** (-0.5)
    return jnp.clip(weights, -2.0, 2.0).astype(jnp.bfloat16)


def centred(key, extent, deviation, limit, held_as=jnp.bfloat16):
    values = deviation * jax.random.normal(key, extent, jnp.float32)
    return jnp.clip(values, min=-limit, max=limit).astype(held_as)


def setup_inputs(seed: int = 0) -> dict:
    seeds = jax.random.split(jax.random.key(seed), 12)
    latents = draw_latents(jax.random.fold_in(seeds[11], 71), 0)
    lengths = draw_lengths(jax.random.fold_in(seeds[11], 71), 0)
    context = draw_context(jax.random.fold_in(seeds[11], 71), 0)
    gain_first = jnp.clip(1.0 + 0.15 * jax.random.normal(seeds[3], (C,), jnp.float32), 0.25, 1.75)
    conv_first = centred(seeds[4], (3, 3, C, C), (9 * C) ** -0.5, 0.109375)
    gain_second = jnp.clip(1.0 + 0.15 * jax.random.normal(seeds[5], (C,), jnp.float32), 0.25, 1.75)
    conv_second = centred(seeds[6], (3, 3, C, C), (9 * C) ** -0.5, 0.109375)
    time_weight = centred(seeds[7], (3, C, C), (3 * C) ** -0.5, 0.1875)
    attn_gain = jnp.clip(1.0 + 0.15 * jax.random.normal(seeds[8], (C,), jnp.float32), 0.25, 1.75)
    w_qkv = draw_w_qkv(jax.random.fold_in(seeds[11], 71), 0)
    w_out = centred(seeds[10], (C, C), C ** -0.5, 0.3125)
    return {"latents": latents, "lengths": lengths, "context": context, "gain_first": gain_first, "conv_first": conv_first, "gain_second": gain_second, "conv_second": conv_second, "time_weight": time_weight, "attn_gain": attn_gain, "w_qkv": w_qkv, "w_out": w_out}


EPS = 1e-05
MASKED = -1e+30

def group_sums(source):
    frame_count, row_count, col_count, channels = source.shape
    group_width = channels // GROUPS
    values = source.astype(jnp.float32).reshape(frame_count, row_count * col_count, GROUPS, group_width)
    return (lax.optimization_barrier(jnp.sum(values, axis=(1, 3))), lax.optimization_barrier(jnp.sum(values * values, axis=(1, 3))))

def finish(total_sum, square_sum, gain):
    group_width = gain.shape[0] // GROUPS
    count = H * W * group_width
    centre = total_sum / count
    spread = square_sum / count - centre * centre
    inverse = lax.rsqrt(spread + EPS)
    scale = jnp.repeat(inverse, group_width, axis=1) * gain[None, :]
    shift = -jnp.repeat(centre, group_width, axis=1) * scale
    return (scale, shift)

def activate(source, scale, shift):
    return jax.nn.silu(source.astype(jnp.float32) * scale[:, None, None, :] + shift[:, None, None, :]).astype(jnp.bfloat16)

def convolve(padded, weights):
    wide = jnp.pad(padded, ((0, 0), (0, 0), (1, 1), (0, 0)))
    row_count = padded.shape[1] - 2
    col_count = padded.shape[2]
    result = jnp.zeros((padded.shape[0], row_count, col_count, weights.shape[-1]), jnp.float32)
    for row_step in range(3):
        for col_step in range(3):
            window = wide[:, row_step:row_step + row_count, col_step:col_step + col_count, :]
            result = result + jnp.dot(window, weights[row_step, col_step], preferred_element_type=jnp.float32)
    return result

def conv_clips(activated, weights):
    blocks = activated.reshape(CLIPS, F_CAP, H, W, C)

    def one_clip(block):
        return convolve(jnp.pad(block, ((0, 0), (1, 1), (0, 0), (0, 0))), weights)
    return lax.map(one_clip, blocks).reshape(FRAMES, H, W, C)

def layer_norm(source, gain):
    values = source.astype(jnp.float32)
    centre = lax.optimization_barrier(jnp.mean(values, axis=-1, keepdims=True))
    spread = lax.optimization_barrier(jnp.mean((values - centre) ** 2, axis=-1, keepdims=True))
    return ((values - centre) * lax.rsqrt(spread + EPS) * gain).astype(jnp.bfloat16)

def attend(packed, shared_kv, live_count):
    frame_count, cell_count, packed_width = packed.shape
    channels = packed_width // 3
    head_count = channels // HEAD_DIM
    shape_local = (frame_count, cell_count, head_count, HEAD_DIM)
    shape_shared = (shared_kv.shape[0], cell_count, head_count, HEAD_DIM)
    queries = packed[..., :channels].reshape(shape_local).astype(jnp.float32)
    keys_local = packed[..., channels:2 * channels].reshape(shape_local).astype(jnp.float32)
    values_local = packed[..., 2 * channels:].reshape(shape_local).astype(jnp.float32)
    keys_shared = shared_kv[..., :channels].reshape(shape_shared).astype(jnp.float32)
    values_shared = shared_kv[..., channels:].reshape(shape_shared).astype(jnp.float32)
    score_scale = HEAD_DIM ** (-0.5)
    near_scores = jnp.einsum('fnhd,gnhd->nhfg', queries, keys_local) * score_scale
    visible = jnp.arange(frame_count) < live_count
    near_scores = jnp.where(visible, near_scores, MASKED)
    far_scores = jnp.einsum('fnhd,jnhd->nhfj', queries, keys_shared) * score_scale
    ceiling = jnp.maximum(lax.optimization_barrier(jnp.max(near_scores, axis=-1)), lax.optimization_barrier(jnp.max(far_scores, axis=-1)))[..., None]
    near_exp = jnp.exp(near_scores - ceiling)
    far_exp = jnp.exp(far_scores - ceiling)
    normaliser = lax.optimization_barrier(jnp.sum(near_exp, axis=-1, keepdims=True)) + lax.optimization_barrier(jnp.sum(far_exp, axis=-1, keepdims=True))
    near_weight = (near_exp / normaliser).astype(jnp.bfloat16).astype(jnp.float32)
    far_weight = (far_exp / normaliser).astype(jnp.bfloat16).astype(jnp.float32)
    result = jnp.einsum('nhfg,gnhd->fnhd', near_weight, values_local)
    result = result + jnp.einsum('nhfj,jnhd->fnhd', far_weight, values_shared)
    return result.reshape(frame_count, cell_count, channels).astype(jnp.bfloat16)

def reference(latents, lengths, context, gain_first, conv_first, gain_second, conv_second, time_weight, attn_gain, w_qkv, w_out):
    total_sum, square_sum = group_sums(latents)
    scale, shift = finish(total_sum, square_sum, gain_first)
    hidden_one = conv_clips(activate(latents, scale, shift), conv_first).astype(jnp.bfloat16)
    total_sum, square_sum = group_sums(hidden_one)
    scale, shift = finish(total_sum, square_sum, gain_second)
    res_one = (latents.astype(jnp.float32) + conv_clips(activate(hidden_one, scale, shift), conv_second)).astype(jnp.bfloat16)
    res_one = res_one.reshape(CLIPS, F_CAP, H, W, C)
    moving = jax.nn.silu(res_one.astype(jnp.float32)).astype(jnp.bfloat16)
    clip_ids = jnp.arange(CLIPS).astype(jnp.int32)
    final_frames = moving[clip_ids, (lengths - 1).astype(jnp.int32)]
    prior = jnp.concatenate([jnp.zeros_like(final_frames[:1]), final_frames[:-1]], axis=0)
    later = jnp.concatenate([moving[1:, 0], jnp.zeros_like(final_frames[:1])], axis=0)
    backward = jnp.concatenate([prior[:, None], moving[:, :-1]], axis=1)
    forward = jnp.concatenate([moving[:, 1:], jnp.zeros_like(moving[:, :1])], axis=1)
    slots = jnp.arange(F_CAP).astype(jnp.int32)
    at_end = (slots[None, :] == lengths[:, None] - 1)[:, :, None, None, None]
    forward = jnp.where(at_end, later[:, None], forward)
    mixed = res_one.astype(jnp.float32) + jnp.dot(backward, time_weight[0], preferred_element_type=jnp.float32)
    mixed = mixed + jnp.dot(moving, time_weight[1], preferred_element_type=jnp.float32)
    mixed = mixed + jnp.dot(forward, time_weight[2], preferred_element_type=jnp.float32)
    res_two = mixed.astype(jnp.bfloat16)
    normed = layer_norm(res_two, attn_gain).reshape(CLIPS, F_CAP, H * W, C)

    def project_clip(block):
        return jnp.dot(block, w_qkv, preferred_element_type=jnp.float32).astype(jnp.bfloat16)
    packed = lax.map(project_clip, normed)
    pairs = packed[..., C:].reshape(FRAMES, H * W, 2 * C)
    shared_kv = jnp.take(pairs, context, axis=0)

    def attend_clip(item):
        return attend(item[0], shared_kv, item[1])
    attended = lax.map(attend_clip, (packed, lengths))
    result = res_two.astype(jnp.float32).reshape(CLIPS, F_CAP, H * W, C)
    result = result + jnp.dot(attended, w_out, preferred_element_type=jnp.float32)
    live = (slots[None, :] < lengths[:, None])[:, :, None, None]
    result = jnp.where(live, result, 0.0)
    return result.astype(jnp.bfloat16).reshape(FRAMES, H, W, C)
```

```python
import functools

import jax
import jax.numpy as jnp
from jax import lax
from jax.experimental import pallas as pl
from jax.experimental.pallas import tpu as pltpu
from jax.sharding import PartitionSpec as P

HEAD_DIM = 64
GROUPS = 32
H = 40
W = 64
EPS = 1e-05
MASKED = -1e30
LANES = 128
FLAG_ROWS = 16
F32 = jnp.float32
BF16 = jnp.bfloat16
VMEM_LIMIT = 48 * 1024 * 1024

SMEM = pl.BlockSpec(memory_space=pltpu.SMEM)
VMEM = pl.BlockSpec(memory_space=pltpu.VMEM)
ANY = pl.BlockSpec(memory_space=pl.ANY)


def call(kernel, out_shape, in_specs, args, scratch=(), flops=0, name=None):
    moved = sum(a.size * a.dtype.itemsize for a in args)
    moved += sum(o.size * o.dtype.itemsize for o in out_shape)
    return pl.pallas_call(
        kernel,
        out_shape=out_shape,
        in_specs=in_specs,
        out_specs=[VMEM] * len(out_shape),
        scratch_shapes=list(scratch),
        compiler_params=pltpu.CompilerParams(vmem_limit_bytes=VMEM_LIMIT),
        cost_estimate=pl.CostEstimate(flops=flops, bytes_accessed=moved, transcendentals=0),
        name=name,
    )(*args)


def struct(shape, dtype=BF16):
    return jax.ShapeDtypeStruct(shape, dtype)


def silu(x):
    return 0.5 * x * (1.0 + jnp.tanh(0.5 * x))


def column_sums(v):
    folded = v.reshape(v.shape[0] // 8, 8, v.shape[1])
    return jnp.sum(folded, axis=0), jnp.sum(folded * folded, axis=0)


def split3(x):
    high = x.astype(BF16)
    rest = x - high.astype(F32)
    mid = rest.astype(BF16)
    return high, mid, (rest - mid.astype(F32)).astype(BF16)


def put_stats(f, sums, stats_ref, msg_ref, cols):
    channels = sums.shape[1]
    stats_ref[f] = jnp.concatenate([sums, jnp.zeros((6, channels), F32)], axis=0)
    high, mid, low = split3(sums)
    parts = [high, mid, low, jnp.zeros((FLAG_ROWS - 6, channels), BF16)]
    packed = jnp.concatenate([p.astype(F32) for p in parts], axis=0)
    msg_ref[f, pl.ds(cols, FLAG_ROWS), :] = packed.astype(BF16)


def stats_kernel(cols, scalars, x_ref, stats_ref, msg_ref):
    frames, cells, channels = x_ref.shape
    step = 2 * cols if cells % (2 * cols) == 0 else cols
    for f in range(frames):

        def body(i, carry):
            v = x_ref[f, pl.ds(pl.multiple_of(i * step, step), step), :].astype(F32)
            s, q = column_sums(v)
            return carry[0] + s, carry[1] + q

        zero = jnp.zeros((8, channels), F32)
        s, q = lax.fori_loop(0, cells // step, body, (zero, zero))
        sums = jnp.concatenate(
            [jnp.sum(s, axis=0, keepdims=True), jnp.sum(q, axis=0, keepdims=True)], axis=0
        )
        put_stats(f, sums, stats_ref, msg_ref, cols)
        edge = pl.multiple_of(scalars[2], cols)
        msg_ref[f, pl.ds(0, cols), :] = x_ref[f, pl.ds(edge, cols), :]


def arrange(pieces):
    big = pieces[0].shape[1] // 256 * 256
    return jnp.concatenate([p[:, :big] for p in pieces] + [p[:, big:] for p in pieces], axis=1)


def place(total, w, index, count, channels, by_rows):
    pass


def conv_kernel(cols, total_cells, residual, scalars, x_ref, stats_ref, top_ref, bottom_ref, gain_ref, w_ref, *rest):
    if residual:
        (res_in_ref, res_ref, move_ref, one_ref, two_ref, wide_w, wide_x, wide_y) = rest
    else:
        (out_ref, out_stats_ref, msg_ref, wide_w, wide_x, wide_y) = rest
    frames, cells, channels = x_ref.shape
    big = channels // 256 * 256
    small = channels - big

    def spans(index):
        return ((index * big, big, 0), (3 * big + index * small, small, big))

    for a in range(3):
        for b in range(3):
            w = w_ref[3 * a + b]
            for row, height, from_row in spans(b):
                for col, width, from_col in spans(a):
                    wide_w[row : row + height, col : col + width] = w[
                        from_row : from_row + height, from_col : from_col + width
                    ]

    group_width = channels // GROUPS
    row_group = lax.broadcasted_iota(jnp.int32, (channels, channels), 0) // group_width
    col_group = lax.broadcasted_iota(jnp.int32, (channels, channels), 1) // group_width
    same = (row_group == col_group).astype(F32)
    step = cols * (4 if cells % (4 * cols) == 0 else 1)
    padded = cells + 2 * cols
    mm = padded // 4

    for f in range(frames):
        other = top_ref[f, pl.ds(cols, FLAG_ROWS), :].astype(F32)
        sums = stats_ref[f, 0:2, :] + other[0:2] + other[2:4] + other[4:6]
        sums = jnp.concatenate([sums, jnp.zeros((6, channels), F32)], axis=0)
        means = jnp.dot(
            sums, same, preferred_element_type=F32, precision=lax.Precision.HIGHEST
        ) / (total_cells * group_width)
        centre = means[0:1]
        inverse = lax.rsqrt(means[1:2] - centre * centre + EPS)
        scale = inverse * gain_ref[...]
        shift = -centre * scale

        def widen(raw, keep):
            length = raw.shape[0]
            y = silu(raw.astype(F32) * scale + shift)
            if keep is not None:
                y = jnp.where(keep, y, 0.0)
            column = lax.broadcasted_iota(jnp.int32, (length, 1), 0) % cols
            left = jnp.where(column == 0, 0.0, pltpu.roll(y, 1, 0))
            right = jnp.where(column == cols - 1, 0.0, pltpu.roll(y, length - 1, 0))
            return arrange([left, y, right]).astype(BF16)

        wide_x[0:cols] = widen(top_ref[f, 0:cols, :], scalars[0] > 0)
        wide_x[cells + cols : cells + 2 * cols] = widen(bottom_ref[f, 0:cols, :], scalars[1] > 0)

        def act_body(i, carry):
            start = pl.multiple_of(i * step, step)
            wide_x[pl.ds(start + cols, step), :] = widen(x_ref[f, pl.ds(start, step), :], None)
            return carry

        lax.fori_loop(0, cells // step, act_body, 0)

        def dot_body(i, carry):
            start = pl.multiple_of(i * mm, mm)
            wide_y[pl.ds(start, mm), :] = jnp.dot(
                wide_x[pl.ds(start, mm), :], wide_w[...], preferred_element_type=F32
            )
            return carry

        lax.fori_loop(0, padded // mm, dot_body, 0)

        def sum_rows(start):
            parts = []
            for base, width in ((0, big), (3 * big, small)):
                total = wide_y[pl.ds(start, step), base : base + width]
                total = total + wide_y[pl.ds(start + cols, step), base + width : base + 2 * width]
                total = total + wide_y[pl.ds(start + 2 * cols, step), base + 2 * width : base + 3 * width]
                parts.append(total)
            return jnp.concatenate(parts, axis=1)

        if residual:
            last = scalars[3] - 1
            odd = scalars[4] > 0

            def end_body(i, carry):
                start = pl.multiple_of(i * step, step)
                here = pl.ds(start, step)
                total = (res_in_ref[f, here, :].astype(F32) + sum_rows(start)).astype(BF16)
                res_ref[f, here, :] = total
                moving = silu(total.astype(F32)).astype(BF16)
                move_ref[f, here, :] = moving
                for ref, final in ((one_ref, jnp.logical_not(odd)), (two_ref, odd)):

                    @pl.when(jnp.where(final, f == last, f == 0))
                    def _():
                        ref[here, :] = moving

                return carry

            lax.fori_loop(0, cells // step, end_body, 0)
        else:

            def end_body(i, carry):
                start = pl.multiple_of(i * step, step)
                total = sum_rows(start).astype(BF16)
                out_ref[f, pl.ds(start, step), :] = total
                s, q = column_sums(total.astype(F32))
                return carry[0] + s, carry[1] + q

            zero = jnp.zeros((8, channels), F32)
            s, q = lax.fori_loop(0, cells // step, end_body, (zero, zero))
            sums = jnp.concatenate(
                [jnp.sum(s, axis=0, keepdims=True), jnp.sum(q, axis=0, keepdims=True)], axis=0
            )
            put_stats(f, sums, out_stats_ref, msg_ref, cols)
            edge = pl.multiple_of(scalars[2], cols)
            msg_ref[f, pl.ds(0, cols), :] = out_ref[f, pl.ds(edge, cols), :]


def time_kernel(group, scalars, res_ref, move_ref, one_ref, two_ref, w_ref, gain_ref, *rest):
    res_two_ref, shares, wide_w = rest[0], rest[1 : 1 + group], rest[1 + group]
    frames, cells, channels = res_ref.shape
    big = channels // 256 * 256
    small = channels - big
    share = cells // group
    live = scalars[3]
    odd = scalars[4] > 0
    for a in range(3):
        w = w_ref[a]
        wide_w[a * big : (a + 1) * big, :] = w[:big]
        wide_w[3 * big + a * small : 3 * big + (a + 1) * small, :] = w[big:]
    for d in range(group):
        start = pl.multiple_of(scalars[8 + d] * share, 16)
        here = pl.ds(start, share)
        one = one_ref[here, :].astype(F32)
        two = two_ref[here, :].astype(F32)
        prior = jnp.where(odd, one, two)
        later = jnp.where(odd, two, one)
        moving = [move_ref[f, here, :].astype(F32) for f in range(frames)]
        for f in range(frames):
            before = moving[f - 1] if f else prior
            after = moving[f + 1] if f + 1 < frames else jnp.zeros_like(prior)
            after = jnp.where(live == f + 1, later, after)
            x = arrange([before, moving[f], after]).astype(BF16)
            mixed = res_ref[f, here, :].astype(F32) + jnp.dot(
                x, wide_w[...], preferred_element_type=F32
            )
            res_two = mixed.astype(BF16)
            res_two_ref[f, here, :] = res_two
            v = res_two.astype(F32)
            centre = jnp.mean(v, axis=1, keepdims=True)
            v = v - centre
            spread = jnp.mean(v * v, axis=1, keepdims=True)
            normed = v * lax.rsqrt(spread + EPS) * gain_ref[...]
            shares[d][f, pl.ds(0, share), :] = normed.astype(BF16)
            flag = jnp.where(f < live, 1.0, 0.0)
            shares[d][f, pl.ds(share, FLAG_ROWS), :] = jnp.full(
                (FLAG_ROWS, channels), flag, F32
            ).astype(BF16)


def attend_kernel(group, buffers, contexts, scalars, *rest):
    own = rest[:group]
    sources = rest[group : group + buffers]
    w_ref = rest[group + buffers]
    outs = rest[group + buffers + 1 : 2 * group + buffers + 1]
    wide_w, context, packed, shared, sems = rest[2 * group + buffers + 1 :]
    frames, flagged, channels = own[0].shape
    share = flagged - FLAG_ROWS
    heads = channels // HEAD_DIM
    wide = (channels + LANES - 1) // LANES * LANES
    keys = frames + contexts

    for j in range(contexts):
        for b in range(buffers):

            @pl.when(scalars[8 + group + 2 * j] == b)
            def _():
                pltpu.make_async_copy(
                    sources[b].at[scalars[9 + group + 2 * j]], context.at[j], sems.at[j]
                ).start()

    wide_w[...] = jnp.zeros_like(wide_w)
    for part in range(3):
        wide_w[:, part * wide : part * wide + channels] = w_ref[:, part * channels : (part + 1) * channels]
    for d in range(group):
        for f in range(frames):
            packed[d, f] = jnp.dot(
                own[d][f, 0:share, :], wide_w[...], preferred_element_type=F32
            ).astype(BF16)
    for j in range(contexts):
        pltpu.make_async_copy(sources[0].at[0], context.at[j], sems.at[j]).wait()
    for j in range(contexts):
        shared[j] = jnp.dot(
            context[j], wide_w[:, wide:], preferred_element_type=F32
        ).astype(BF16)

    gather_row = lax.broadcasted_iota(jnp.int32, (keys * wide, LANES), 0)
    gather_lane = lax.broadcasted_iota(jnp.int32, (keys * wide, LANES), 1)
    gather = (gather_row // wide * 8 + gather_row % wide // HEAD_DIM == gather_lane).astype(F32)
    gather = (gather * HEAD_DIM ** (-0.5)).astype(BF16)
    spread_row = lax.broadcasted_iota(jnp.int32, (LANES, keys * wide), 0)
    spread_col = lax.broadcasted_iota(jnp.int32, (LANES, keys * wide), 1)
    spread = (spread_col // wide * 8 + spread_col % wide // HEAD_DIM == spread_row).astype(BF16)
    lane = lax.broadcasted_iota(jnp.int32, (1, LANES), 1)
    step = 80 if share % 80 == 0 else share
    for d in range(group):
        flags = own[d][:, pl.ds(share, FLAG_ROWS), 0:LANES].astype(F32)
        visible = jnp.logical_and(lane % 8 < heads, lane // 8 < keys)
        for f in range(frames):
            dead = jnp.logical_and(lane // 8 == f, flags[f, 0:1] < 0.5)
            visible = jnp.logical_and(visible, jnp.logical_not(dead))

        def body(i, carry, d=d, visible=visible):
            here = pl.ds(pl.multiple_of(i * step, 16), step)
            key = [packed[d, f, here, wide : 2 * wide] for f in range(frames)]
            key += [shared[j, here, 0:wide] for j in range(contexts)]
            value = [packed[d, f, here, 2 * wide : 3 * wide] for f in range(frames)]
            value += [shared[j, here, wide : 2 * wide] for j in range(contexts)]
            for f in range(frames):
                query = packed[d, f, here, 0:wide]
                products = jnp.concatenate([query * k for k in key], axis=1)
                scores = jnp.dot(products, gather, preferred_element_type=F32)
                scores = jnp.where(visible, scores, MASKED)
                top = scores
                for shift in (8, 16, 32, 64):
                    top = jnp.maximum(top, pltpu.roll(top, shift, 1))
                raised = jnp.exp(scores - top)
                total = raised
                for shift in (8, 16, 32, 64):
                    total = total + pltpu.roll(total, shift, 1)
                weights = (raised / total).astype(BF16)
                wide_weights = jnp.dot(weights, spread, preferred_element_type=F32)
                result = jnp.zeros((step, wide), F32)
                for j in range(keys):
                    result = result + wide_weights[:, j * wide : (j + 1) * wide] * value[j].astype(F32)
                outs[d][f, here, :] = result[:, :channels].astype(BF16)
            return carry

        lax.fori_loop(0, share // step, body, 0)


def final_kernel(group, scalars, res_ref, *rest):
    parts, w_ref, out_ref = rest[:group], rest[group], rest[group + 1]
    frames, cells, channels = res_ref.shape
    share = cells // group
    for d in range(group):
        here = pl.ds(pl.multiple_of(scalars[8 + d] * share, 16), share)
        for f in range(frames):
            total = res_ref[f, here, :].astype(F32) + jnp.dot(
                parts[d][f], w_ref[...], preferred_element_type=F32
            )
            out_ref[f, here, :] = jnp.where(f < scalars[3], total, 0.0).astype(BF16)


def share_tile(stats, msg, source, cols):
    tiles = lax.axis_size("tile")
    if tiles == 2:
        got = lax.ppermute(msg, "tile", [(0, 1), (1, 0)])
        return stats, got, got
    down = [(i, i + 1) for i in range(tiles - 1)]
    up = [(i + 1, i) for i in range(tiles - 1)]
    pad = ((0, 0), (0, FLAG_ROWS), (0, 0))
    top = lax.ppermute(source[:, -cols:], "tile", down)
    bottom = lax.ppermute(source[:, :cols], "tile", up)
    return lax.psum(stats, "tile"), jnp.pad(top, pad), jnp.pad(bottom, pad)


def local(
    latents,
    lengths,
    context,
    gain_first,
    conv_first,
    gain_second,
    conv_second,
    time_weight,
    attn_gain,
    w_qkv,
    w_out,
):
    frames, rows, cols, channels = latents.shape
    cells = rows * cols
    tiles, clips = lax.axis_size("tile"), lax.axis_size("clip")
    tile, clip = lax.axis_index("tile"), lax.axis_index("clip")
    group = 4
    levels = clips // group
    share = cells // group
    contexts = context.shape[0]
    member, level = clip % group, clip // group
    total_cells = cells * tiles

    owner = context // frames
    source_level = owner // group
    hop = level - source_level
    buffer = jnp.where(hop >= 0, hop, levels - 1 - hop)
    slot = (owner % group) ^ member
    scalars = jnp.concatenate(
        [
            jnp.stack(
                [
                    (tile > 0).astype(jnp.int32),
                    (tile < tiles - 1).astype(jnp.int32),
                    jnp.where(tile == 0, cells - cols, 0).astype(jnp.int32),
                    lengths[0],
                    clip % 2,
                    clip * 0,
                    clip * 0,
                    clip * 0,
                ]
            ),
            member ^ jnp.arange(group, dtype=jnp.int32),
            jnp.stack([buffer, slot], axis=1).reshape(-1),
        ]
    ).astype(jnp.int32)

    x = latents.reshape(frames, cells, channels)
    message = struct((frames, cols + FLAG_ROWS, channels))
    sums = struct((frames, 8, channels), F32)
    whole = struct((frames, cells, channels))
    stats, msg = call(
        functools.partial(stats_kernel, cols), [sums, message], [SMEM, VMEM], [scalars, x], name="first_sums"
    )

    conv_scratch = [
        pltpu.VMEM((3 * channels, 3 * channels), BF16),
        pltpu.VMEM((cells + 2 * cols, 3 * channels), BF16),
        pltpu.VMEM((cells + 2 * cols, 3 * channels), F32),
    ]
    conv_flops = 2 * frames * cells * 9 * channels * channels
    stats, top, bottom = share_tile(stats, msg, x, cols)
    hidden, stats, msg = call(
        functools.partial(conv_kernel, cols, total_cells, False),
        [whole, sums, message],
        [SMEM] + [VMEM] * 6,
        [scalars, x, stats, top, bottom, gain_first.reshape(1, channels), conv_first.reshape(9, channels, channels)],
        conv_scratch,
        conv_flops,
        name="conv_one",
    )
    stats, top, bottom = share_tile(stats, msg, hidden, cols)
    one_frame = struct((cells, channels))
    res_one, moving, one, two = call(
        functools.partial(conv_kernel, cols, total_cells, True),
        [whole, whole, one_frame, one_frame],
        [SMEM] + [VMEM] * 7,
        [scalars, hidden, stats, top, bottom, gain_second.reshape(1, channels), conv_second.reshape(9, channels, channels), x],
        conv_scratch,
        conv_flops,
        name="conv_two",
    )
    one = lax.ppermute(one, "clip", [(i, i ^ 1) for i in range(clips)])
    two = lax.ppermute(
        two, "clip", [(i, i + 1) for i in range(1, clips - 1, 2)] + [(i + 1, i) for i in range(1, clips - 1, 2)]
    )
    part = struct((frames, share + FLAG_ROWS, channels))
    res_two, *shares = call(
        functools.partial(time_kernel, group),
        [whole] + [part] * group,
        [SMEM] + [VMEM] * 6,
        [scalars, res_one, moving, one, two, time_weight, attn_gain.reshape(1, channels)],
        [pltpu.VMEM((3 * channels, channels), BF16)],
        2 * frames * cells * 3 * channels * channels,
        name="time_mix",
    )
    swaps = [[(i, i ^ d) for i in range(clips)] for d in range(group)]
    own = [shares[0]] + [lax.ppermute(shares[d], "clip", swaps[d]) for d in range(1, group)]

    picks = []
    for d in range(group):
        other = clip ^ d
        second = jnp.any(context == other * frames + 1)
        picks.append(jnp.where(second, own[d][1, :share], own[d][0, :share]))
    picked = jnp.stack(picks)
    rising = [(i, i + group) for i in range(clips - group)]
    falling = [(i + group, i) for i in range(clips - group)]
    below, above = [picked], [picked]
    for _ in range(levels - 1):
        below.append(lax.ppermute(below[-1], "clip", rising))
        above.append(lax.ppermute(above[-1], "clip", falling))
    sources = below + above[1:]

    wide = (channels + LANES - 1) // LANES * LANES
    attended = call(
        functools.partial(attend_kernel, group, len(sources), contexts),
        [struct((frames, share, channels))] * group,
        [SMEM] + [VMEM] * group + [ANY] * len(sources) + [VMEM],
        [scalars, *own, *sources, w_qkv],
        [
            pltpu.VMEM((channels, 3 * wide), BF16),
            pltpu.VMEM((contexts, share, channels), BF16),
            pltpu.VMEM((group, frames, share, 3 * wide), BF16),
            pltpu.VMEM((contexts, share, 2 * wide), BF16),
            pltpu.SemaphoreType.DMA((contexts,)),
        ],
        2 * frames * cells * channels * 10 * channels,
        name="attend",
    )
    parts = [attended[0]] + [lax.ppermute(attended[d], "clip", swaps[d]) for d in range(1, group)]
    (result,) = call(
        functools.partial(final_kernel, group),
        [whole],
        [SMEM] + [VMEM] * (group + 2),
        [scalars, res_two, *parts, w_out],
        flops=2 * frames * cells * channels * channels,
        name="project",
    )
    return result.reshape(frames, rows, cols, channels)


def solution(mesh):
    placed = (P("clip", "tile", None, None), P("clip"), P(), P(), P(), P(), P(), P(), P(), P(), P())
    return jax.shard_map(
        local, mesh=mesh, in_specs=placed, out_specs=P("clip", "tile", None, None), check_vma=False
    )
```

```python
import functools
import math

import jax
import jax.numpy as jnp
import ml_dtypes
import numpy as np
from jax import lax
from jax.experimental import pallas as pl
from jax.experimental.pallas import tpu as pltpu
from jax.sharding import PartitionSpec as P

HEAD_DIM = 64
GROUPS = 32
H = 40
W = 64
EPS = 1e-05
MASKED = -1e30
LANES = 128
FLAG_ROWS = 16
F32 = jnp.float32
BF16 = jnp.bfloat16

SMEM = pl.BlockSpec(memory_space=pltpu.SMEM)
VMEM = pl.BlockSpec(memory_space=pltpu.VMEM)
ANY = pl.BlockSpec(memory_space=pl.ANY)


def call(kernel, out_shape, in_specs, args, scratch=(), flops=0, name=None, mib=8):
    return pl.pallas_call(
        kernel,
        out_shape=out_shape,
        in_specs=in_specs,
        out_specs=[VMEM] * len(out_shape),
        scratch_shapes=list(scratch),
        compiler_params=pltpu.CompilerParams(vmem_limit_bytes=mib * 1024 * 1024),
        cost_estimate=pl.CostEstimate(flops=1, bytes_accessed=1, transcendentals=0),
        name=name,
    )(*args)


def struct(shape, dtype=BF16):
    return jax.ShapeDtypeStruct(shape, dtype)


def silu(x):
    return 0.5 * x * (1.0 + jnp.tanh(0.5 * x))


def column_sums(v):
    folded = v.reshape(v.shape[0] // 8, 8, v.shape[1])
    return jnp.sum(folded, axis=0), jnp.sum(folded * folded, axis=0)


def split3(x):
    high = x.astype(BF16)
    rest = x - high.astype(F32)
    mid = rest.astype(BF16)
    return high, mid, (rest - mid.astype(F32)).astype(BF16)


def put_stats(f, sums, stats_ref, msg_ref, cols):
    channels = sums.shape[1]
    stats_ref[f] = jnp.concatenate([sums, jnp.zeros((6, channels), F32)], axis=0)
    high, mid, low = split3(sums)
    parts = [high, mid, low, jnp.zeros((FLAG_ROWS - 6, channels), BF16)]
    packed = jnp.concatenate([p.astype(F32) for p in parts], axis=0)
    msg_ref[f, pl.ds(cols, FLAG_ROWS), :] = packed.astype(BF16)


def edge_start(cells, cols):
    return pl.multiple_of(jnp.where(lax.axis_index("tile") == 0, cells - cols, 0), cols)


def stats_kernel(cols, x_ref, stats_ref, msg_ref):
    frames, cells, channels = x_ref.shape
    step = 2 * cols if cells % (2 * cols) == 0 else cols
    for f in range(frames):

        def body(i, carry):
            v = x_ref[f, pl.ds(pl.multiple_of(i * step, step), step), :].astype(F32)
            s, q = column_sums(v)
            return carry[0] + s, carry[1] + q

        zero = jnp.zeros((8, channels), F32)
        s, q = lax.fori_loop(0, cells // step, body, (zero, zero))
        sums = jnp.concatenate(
            [jnp.sum(s, axis=0, keepdims=True), jnp.sum(q, axis=0, keepdims=True)], axis=0
        )
        put_stats(f, sums, stats_ref, msg_ref, cols)
        edge = edge_start(cells, cols)
        msg_ref[f, pl.ds(0, cols), :] = x_ref[f, pl.ds(edge, cols), :]


def arrange(pieces):
    big = pieces[0].shape[1] // 256 * 256
    return jnp.concatenate([p[:, :big] for p in pieces] + [p[:, big:] for p in pieces], axis=1)


def spans(index, channels):
    big = channels // 256 * 256
    return ((index * big, big, 0), (3 * big + index * (channels - big), channels - big, big))


def lay_conv(source, target):
    channels = source.shape[1]
    for a in range(3):
        for b in range(3):
            for row, height, from_row in spans(b, channels):
                for col, width, from_col in spans(a, channels):
                    target[row : row + height, col : col + width] = source[
                        3 * a + b, from_row : from_row + height, from_col : from_col + width
                    ]


def first_weights_kernel(first_ref, wide_first):
    lay_conv(first_ref, wide_first)


def weights_kernel(second_ref, time_ref, qkv_ref, out_ref, wide_second, wide_time, wide_q, wide_kv, wide_out):
    channels = out_ref.shape[0]
    lay_conv(second_ref, wide_second)
    for b in range(3):
        for row, height, from_row in spans(b, channels):
            wide_time[row : row + height, :] = time_ref[b, from_row : from_row + height, :]
    wide = wide_out.shape[0]
    wide_q[...] = jnp.zeros_like(wide_q)
    wide_kv[...] = jnp.zeros_like(wide_kv)
    wide_q[:, 0:channels] = qkv_ref[:, 0:channels]
    for part in range(2):
        wide_kv[:, part * wide : part * wide + channels] = qkv_ref[:, (part + 1) * channels : (part + 2) * channels]
    wide_out[...] = jnp.zeros_like(wide_out)
    wide_out[0:channels, :] = out_ref[...]


def conv_kernel(cols, total_cells, first_row, rows, residual, block_rows, x_ref, stats_ref, top_ref, bottom_ref, gain_ref, w_ref, *rest):
    if residual:
        res_in_ref, scalars, share_ref, wide_x, wide_y = rest
        share = share_ref.shape[2] - FLAG_ROWS
    else:
        out_ref, out_stats_ref, msg_ref, wide_x, wide_y = rest
    frames, cells, channels = x_ref.shape
    tile_rows = cells // cols
    big = channels // 256 * 256
    small = channels - big
    group_width = channels // GROUPS
    row_group = lax.broadcasted_iota(jnp.int32, (channels, channels), 0) // group_width
    col_group = lax.broadcasted_iota(jnp.int32, (channels, channels), 1) // group_width
    same = (row_group == col_group).astype(F32)
    column = lax.broadcasted_iota(jnp.int32, (cols, 1), 0)
    leftmost, rightmost = column == 0, column == cols - 1

    scales = []
    for f in range(frames):
        other = top_ref[f, pl.ds(cols, FLAG_ROWS), :].astype(F32)
        sums = stats_ref[f, 0:2, :] + other[0:2] + other[2:4] + other[4:6]
        sums = jnp.concatenate([sums, jnp.zeros((6, channels), F32)], axis=0)
        means = jnp.dot(
            sums, same, preferred_element_type=F32, precision=lax.Precision.HIGHEST
        ) / (total_cells * group_width)
        centre = means[0:1]
        scale = lax.rsqrt(means[1:2] - centre * centre + EPS) * gain_ref[...]
        scales.append((scale, -centre * scale))

    def widen(f, padded_row):
        row = first_row + padded_row - 1
        if row < 0:
            raw, keep = top_ref[f, 0:cols, :], lax.axis_index("tile") > 0
        elif row >= tile_rows:
            raw, keep = bottom_ref[f, 0:cols, :], lax.axis_index("tile") < lax.axis_size("tile") - 1
        else:
            raw, keep = x_ref[f, row * cols : (row + 1) * cols, :], None
        scale, shift = scales[f]
        y = silu(raw.astype(F32) * scale + shift)
        if keep is not None:
            y = jnp.where(keep, y, 0.0)
        left = jnp.where(leftmost, 0.0, pltpu.roll(y, 1, 0))
        right = jnp.where(rightmost, 0.0, pltpu.roll(y, cols - 1, 0))
        wide_x[f, padded_row * cols : (padded_row + 1) * cols, :] = arrange([left, y, right]).astype(BF16)

    def multiply(f, start, stop):
        here = slice(start * cols, stop * cols)
        wide_y[f, here, :] = jnp.dot(wide_x[f, here, :], w_ref[...], preferred_element_type=F32)

    totals = [[jnp.zeros((8, channels), F32)] * 2 for _ in range(frames)]

    def finish(f, r):
        parts = []
        for base, width in ((0, big), (3 * big, small)):
            parts.append(
                wide_y[f, r * cols : (r + 1) * cols, base : base + width]
                + wide_y[f, (r + 1) * cols : (r + 2) * cols, base + width : base + 2 * width]
                + wide_y[f, (r + 2) * cols : (r + 3) * cols, base + 2 * width : base + 3 * width]
            )
        total = jnp.concatenate(parts, axis=1)
        here = slice(r * cols, (r + 1) * cols)
        if residual:
            where = slice((first_row + r) * cols, (first_row + r + 1) * cols)
            total = (res_in_ref[f, where, :].astype(F32) + total).astype(BF16)
            put_share(scalars, share_ref, f, r * cols, total, share)
        else:
            total = total.astype(BF16)
            out_ref[f, here, :] = total
            s, q = column_sums(total.astype(F32))
            totals[f] = [totals[f][0] + s, totals[f][1] + q]

    blocks = []
    for f in range(frames):
        edges = list(range(0, rows + 2, block_rows)) + [rows + 2]
        blocks += [(f, edges[i], edges[i + 1]) for i in range(len(edges) - 1)]

    def act(block):
        for p in range(block[1], block[2]):
            widen(block[0], p)

    def end(block):
        for p in range(block[1], block[2]):
            if p >= 2:
                finish(block[0], p - 2)

    act(blocks[0])
    for i, block in enumerate(blocks):
        multiply(*block)
        if i + 1 < len(blocks):
            act(blocks[i + 1])
        if i > 0:
            end(blocks[i - 1])
    end(blocks[-1])
    if residual:
        for f in range(frames):
            flag = jnp.full((FLAG_ROWS, channels), jnp.where(f < scalars[3], 1.0, 0.0), F32)
            for d in range(share_ref.shape[0]):
                share_ref[d, f, share:, :] = flag.astype(BF16)
    else:
        for f in range(frames):
            sums = jnp.concatenate([jnp.sum(t, axis=0, keepdims=True) for t in totals[f]], axis=0)
            put_stats(f, sums, out_stats_ref, msg_ref, cols)
            edge = edge_start(cells, cols)
            msg_ref[f, pl.ds(0, cols), :] = out_ref[f, pl.ds(edge, cols), :]


def put_share(scalars, out_ref, f, start, total, share):
    piece = math.gcd(share, total.shape[0])
    for p in range(0, total.shape[0], piece):
        owner, inside = divmod(start + p, share)
        out_ref[scalars[8 + owner], f, inside : inside + piece, :] = total[p : p + piece]


def ends_kernel(group, scalars, *rest):
    own, (one_ref, two_ref) = rest[:group], rest[group:]
    share = one_ref.shape[0]
    odd = scalars[5] > 0
    for d in range(group):
        for ref, upper in ((one_ref, odd), (two_ref, jnp.logical_not(odd))):

            @pl.when(jnp.logical_and(jnp.logical_not(upper), scalars[4] ^ d == group - 1))
            def _():
                live = own[d][1, pl.ds(share, FLAG_ROWS), :].astype(F32)[0:1] > 0.5
                ref[...] = jnp.where(
                    live, own[d][1, 0:share, :].astype(F32), own[d][0, 0:share, :].astype(F32)
                ).astype(BF16)

            @pl.when(jnp.logical_and(upper, scalars[4] == d))
            def _():
                ref[...] = own[d][0, 0:share, :]


def time_kernel(group, scalars, *rest):
    own, (one_ref, two_ref, w_ref, gain_ref) = rest[:group], rest[group : group + 4]
    res_two_ref, normed_ref, pick_ref, ordered, moving = rest[group + 4 :]
    frames, flagged, channels = own[0].shape
    share = flagged - FLAG_ROWS
    for d in range(group):
        ordered[scalars[8 + d]] = own[d][...]
    step = 80 if share % 80 == 0 else share

    def lively(x):
        return silu(x.astype(F32)).astype(BF16)

    for m in range(group):
        for f in range(frames):
            for s in range(0, share, step):
                moving[m, f, s : s + step, :] = lively(ordered[m, f, s : s + step, :])
    odd = scalars[5] > 0
    live = [ordered[m, 1, share : share + FLAG_ROWS, :].astype(F32)[0:1] > 0.5 for m in range(group)]
    for m in range(group):
        for s in range(0, share, step):
            here = slice(s, s + step)
            first, second = moving[m, 0, here, :].astype(F32), moving[m, 1, here, :].astype(F32)
            if m:
                prior = jnp.where(
                    live[m - 1], moving[m - 1, 1, here, :].astype(F32), moving[m - 1, 0, here, :].astype(F32)
                )
            else:
                prior = jnp.where(odd, one_ref[here, :].astype(F32), two_ref[here, :].astype(F32))
                prior = lively(prior).astype(F32)
            if m + 1 < group:
                later = moving[m + 1, 0, here, :].astype(F32)
            else:
                later = jnp.where(odd, two_ref[here, :].astype(F32), one_ref[here, :].astype(F32))
                later = lively(later).astype(F32)
            rows = [
                arrange([prior, first, jnp.where(live[m], second, later)]),
                arrange([first, second, jnp.where(live[m], later, 0.0)]),
            ]
            mixed = jnp.dot(
                jnp.concatenate(rows, axis=0).astype(BF16), w_ref[...], preferred_element_type=F32
            )
            norms = []
            for f in range(frames):
                total = ordered[m, f, here, :].astype(F32) + mixed[f * step : (f + 1) * step]
                total = total.astype(BF16)
                res_two_ref[m, f, here, :] = total
                v = total.astype(F32)
                v = v - jnp.mean(v, axis=1, keepdims=True)
                spread = jnp.mean(v * v, axis=1, keepdims=True)
                normed = v * lax.rsqrt(spread + EPS) * gain_ref[...]
                norms.append(normed)
                normed_ref[m, f, here, :] = normed.astype(BF16)
            pick_ref[m, here, :] = jnp.where(scalars[8 + group + m] > 0, norms[1], norms[0]).astype(BF16)
        for f in range(frames):
            normed_ref[m, f, share : share + FLAG_ROWS, :] = ordered[m, f, share : share + FLAG_ROWS, :]


def pack_kernel(normed_ref, wq_ref, wkv_ref, packed_ref):
    group, frames, flagged, channels = normed_ref.shape
    share = flagged - FLAG_ROWS
    for m in range(group):
        rows = jnp.concatenate([normed_ref[m, f, 0:share, :] for f in range(frames)], axis=0)
        wide = wq_ref.shape[1]
        packed_ref[m, :, 0:wide] = jnp.dot(rows, wq_ref[...], preferred_element_type=F32).astype(BF16)
        packed_ref[m, :, wide:] = jnp.dot(rows, wkv_ref[...], preferred_element_type=F32).astype(BF16)


def head_maps(keys, channels, wide):
    column = np.arange(keys * wide)
    lane = column // wide * 8 + column % wide // HEAD_DIM
    hit = (lane[:, None] == np.arange(LANES)[None, :]) & (column % wide < channels)[:, None]
    return (hit * HEAD_DIM ** (-0.5)).astype(ml_dtypes.bfloat16), hit.T.astype(ml_dtypes.bfloat16)


def attend_kernel(buffers, contexts, scalars, *rest):
    sources = rest[:buffers]
    packed_ref, normed_ref, res_ref, wkv_ref, wout_ref, gather_ref, spread_ref, out_ref = rest[buffers : buffers + 8]
    context, shared, products, spreads, joined, sems = rest[buffers + 8 :]
    group, frames, share, channels = res_ref.shape
    heads = channels // HEAD_DIM
    wide = wout_ref.shape[0]
    keys = frames + contexts
    base = 8 + 2 * group

    for j in range(contexts):
        for b in range(buffers):

            @pl.when(scalars[base + 2 * j] == b)
            def _():
                pltpu.make_async_copy(
                    sources[b].at[scalars[base + 1 + 2 * j]], context.at[pl.ds(j * share, share)], sems.at[j]
                ).start()

    lane = lax.broadcasted_iota(jnp.int32, (1, LANES), 1)
    in_use = jnp.logical_and(lane % 8 < heads, lane // 8 < keys)

    for j in range(contexts):
        pltpu.make_async_copy(
            sources[0].at[0], context.at[pl.ds(j * share, share)], sems.at[j]
        ).wait()
    half = contexts // 2 * share
    for s in (0, half):
        shared[s : s + half, :] = jnp.dot(
            context[s : s + half, :], wkv_ref[...], preferred_element_type=F32
        ).astype(BF16)

    piece = 32 if share % 32 == 0 else 16

    def key_value(m, j, s, part):
        if j < frames:
            at = j * share + s
            return packed_ref[m, at : at + piece, (1 + part) * wide : (2 + part) * wide]
        at = (j - frames) * share + s
        return shared[at : at + piece, part * wide : (part + 1) * wide]

    def multiply(m):
        for s in range(0, share, piece):
            queries = [packed_ref[m, f * share + s : f * share + s + piece, 0:wide] for f in range(frames)]
            for j in range(keys):
                key = key_value(m, j, s, 0)
                for f in range(frames):
                    at = f * share + s
                    products[m, at : at + piece, j * wide : (j + 1) * wide] = queries[f] * key

    def weigh(m):
        flags = normed_ref[m, :, share : share + FLAG_ROWS, 0:LANES].astype(F32)
        visible = in_use
        for f in range(frames):
            dead = jnp.logical_and(lane // 8 == f, flags[f, 0:1] < 0.5)
            visible = jnp.logical_and(visible, jnp.logical_not(dead))
        scores = scored[m]
        scores = jnp.where(visible, scores, MASKED)
        top = scores
        for shift in (8, 16, 32, 64):
            top = jnp.maximum(top, pltpu.roll(top, shift, 1))
        raised = jnp.exp(scores - top)
        total = raised
        for shift in (8, 16, 32, 64):
            total = total + pltpu.roll(total, shift, 1)
        weights = (raised / total).astype(BF16)
        spreads[m % 2] = jnp.dot(weights, spread_ref[...], preferred_element_type=F32)

    def combine(m):
        for s in range(0, share, piece):
            results = [jnp.zeros((piece, wide), F32) for _ in range(frames)]
            for j in range(keys):
                value = key_value(m, j, s, 1).astype(F32)
                for f in range(frames):
                    at = f * share + s
                    results[f] = results[f] + spreads[m % 2, at : at + piece, j * wide : (j + 1) * wide] * value
            for f in range(frames):
                joined[f * share + s : f * share + s + piece, :] = results[f].astype(BF16)
        added = jnp.dot(joined[...], wout_ref[...], preferred_element_type=F32)
        for f in range(frames):
            live = normed_ref[m, f, share : share + FLAG_ROWS, :].astype(F32)[0:1] > 0.5
            total = res_ref[m, f].astype(F32) + added[f * share : (f + 1) * share]
            out_ref[scalars[8 + m], f] = jnp.where(live, total, 0.0).astype(BF16)

    for m in range(group):
        multiply(m)
    scored = [jnp.dot(products[m], gather_ref[...], preferred_element_type=F32) for m in range(group)]
    for m in range(group):
        weigh(m)
        if m > 0:
            combine(m - 1)
    combine(group - 1)


def assemble_kernel(group, chunks, scalars, *rest):
    parts, out_ref = rest[:-1], rest[-1]
    frames, cells, channels = out_ref.shape
    share = cells // (chunks * group)
    for c in range(chunks):
        for d in range(group):
            start = pl.multiple_of((c * group + scalars[8 + d]) * share, 16)
            for f in range(frames):
                out_ref[f, pl.ds(start, share), :] = parts[c * group + d][f]


def share_tile(stats, msg, source, cols):
    tiles = lax.axis_size("tile")
    if tiles == 2:
        got = lax.ppermute(msg, "tile", [(0, 1), (1, 0)])
        return stats, got, got
    down = [(i, i + 1) for i in range(tiles - 1)]
    up = [(i + 1, i) for i in range(tiles - 1)]
    pad = ((0, 0), (0, FLAG_ROWS), (0, 0))
    top = lax.ppermute(source[:, -cols:], "tile", down)
    bottom = lax.ppermute(source[:, :cols], "tile", up)
    return lax.psum(stats, "tile"), jnp.pad(top, pad), jnp.pad(bottom, pad)


def buffer_of(level, source, levels):
    if levels == 4:
        apart = level ^ source
        outermost = jnp.logical_or(level == 0, level == 3)
        return jnp.where(jnp.logical_and(apart == 3, outermost), 4, apart)
    hop = level - source
    return jnp.where(hop >= 0, hop, levels - 1 - hop)


def across_levels(own, levels, group):
    def send(x, pairs):
        return lax.ppermute(x, "clip", [(a * group + i, b * group + i) for a, b in pairs for i in range(group)])

    if levels == 4:
        far = send(own, [(0, 2), (2, 0), (1, 3), (3, 1)])
        near = send(own, [(0, 1), (1, 0), (2, 3), (3, 2)])
        middle = send(own, [(1, 2), (2, 1)])
        outer = send(far, [(1, 0), (2, 3)])
        return [own, near, far, middle, outer]
    lower, upper = [own], [own]
    for _ in range(levels - 1):
        lower.append(send(lower[-1], [(i, i + 1) for i in range(levels - 1)]))
        upper.append(send(upper[-1], [(i + 1, i) for i in range(levels - 1)]))
    return lower + upper[1:]


def local(
    latents,
    lengths,
    context,
    gain_first,
    conv_first,
    gain_second,
    conv_second,
    time_weight,
    attn_gain,
    w_qkv,
    w_out,
):
    frames, rows, cols, channels = latents.shape
    cells = rows * cols
    tiles, clips = lax.axis_size("tile"), lax.axis_size("clip")
    clip = lax.axis_index("clip")
    group = 4
    chunks = 2 if rows % 2 == 0 and cells % (2 * group * 16) == 0 else 1
    levels = clips // group
    share = cells // (group * chunks)
    contexts = context.shape[0]
    member, level = clip % group, clip // group
    total_cells = cells * tiles
    wide = (channels + LANES - 1) // LANES * LANES
    keys = frames + contexts

    owner = context // frames
    buffer = buffer_of(level, owner // group, levels)
    members = jnp.arange(group, dtype=jnp.int32)
    second = jnp.any(context[None, :] == ((level * group + members) * frames + 1)[:, None], axis=1)
    scalars = jnp.concatenate(
        [
            jnp.stack([level * 0, level * 0, level * 0, lengths[0], member]),
            jnp.stack([level % 2, level * 0, level * 0]),
            member ^ members,
            second,
            jnp.stack([buffer, owner % group], axis=1).reshape(-1),
        ]
    ).astype(jnp.int32)

    x = latents.reshape(frames, cells, channels)
    message = struct((frames, cols + FLAG_ROWS, channels))
    sums = struct((frames, 8, channels), F32)
    whole = struct((frames, cells, channels))
    stats, msg = call(
        functools.partial(stats_kernel, cols), [sums, message], [VMEM], [x], name="first_sums"
    )
    stats, top, bottom = share_tile(stats, msg, x, cols)
    square = struct((3 * channels, 3 * channels))
    (wide_first,) = call(
        first_weights_kernel, [square], [VMEM], [conv_first.reshape(9, channels, channels)], name="first_weights"
    )
    wide_second, wide_time, wide_q, wide_kv, wide_out = call(
        weights_kernel,
        [
            square,
            struct((3 * channels, channels)),
            struct((channels, wide)),
            struct((channels, 2 * wide)),
            struct((wide, channels)),
        ],
        [VMEM] * 4,
        [conv_second.reshape(9, channels, channels), time_weight, w_qkv, w_out],
        name="weights",
    )
    gather, spread = (jnp.asarray(a) for a in head_maps(keys, channels, wide))

    def conv(first_row, count, residual, outs, source, stats, top, bottom, gain, weight, *more):
        scratch = [
            pltpu.VMEM((frames, (count + 2) * cols, 3 * channels), BF16),
            pltpu.VMEM((frames, (count + 2) * cols, 3 * channels), F32),
        ]
        block_rows = 11 if count == 20 else 8
        return call(
            functools.partial(conv_kernel, cols, total_cells, first_row, count, residual, block_rows),
            outs,
            [VMEM] * 6 + [VMEM, SMEM][: len(more)],
            [source, stats, top, bottom, gain.reshape(1, channels), weight, *more],
            scratch,
            2 * frames * (count + 2) * cols * 9 * channels * channels,
            name="conv_two" if residual else "conv_one",
            mib=26,
        )

    hidden, stats, msg = conv(0, rows, False, [whole, sums, message], x, stats, top, bottom, gain_first, wide_first)
    stats, top, bottom = share_tile(stats, msg, hidden, cols)
    swaps = [[(i, i ^ d) for i in range(clips)] for d in range(group)]
    pairs = [[(i, i + 1) for i in range(a, levels - 1, 2)] for a in range(2)]
    beside = [
        [(u * group + i, v * group + i) for a, b in p for u, v in ((a, b), (b, a)) for i in range(group)] for p in pairs
    ]

    owns = []
    for c in range(chunks):
        (shares,) = conv(
            c * rows // chunks,
            rows // chunks,
            True,
            [struct((group, frames, share + FLAG_ROWS, channels))],
            hidden,
            stats,
            top,
            bottom,
            gain_second,
            wide_second,
            x,
            scalars,
        )
        owns.append([shares[0]] + [lax.ppermute(shares[d], "clip", swaps[d]) for d in range(1, group)])
    gathered = []
    for c in range(chunks):
        own = owns[c]
        end = struct((share, channels))
        one, two = call(
            functools.partial(ends_kernel, group), [end, end], [SMEM] + [VMEM] * group, [scalars, *own], name="ends"
        )
        one = lax.ppermute(one, "clip", beside[0])
        two = lax.ppermute(two, "clip", beside[1])
        both = (group, frames, share, channels)
        flagged = (group, frames, share + FLAG_ROWS, channels)
        res_two, normed, picked = call(
            functools.partial(time_kernel, group),
            [struct(both), struct(flagged), struct((group, share, channels))],
            [SMEM] + [VMEM] * (group + 4),
            [scalars, *own, one, two, wide_time, attn_gain.reshape(1, channels)],
            [pltpu.VMEM(flagged, BF16), pltpu.VMEM(both, BF16)],
            2 * frames * group * share * 3 * channels * channels,
            name="time_mix",
        )
        gathered.append((res_two, normed, across_levels(picked, levels, group)))
    parts = []
    for res_two, normed, sources in gathered:
        (packed,) = call(
            pack_kernel,
            [struct((group, frames * share, 3 * wide))],
            [VMEM] * 3,
            [normed, wide_q, wide_kv],
            flops=2 * group * frames * share * channels * 3 * wide,
            name="pack",
        )
        (outs,) = call(
            functools.partial(attend_kernel, len(sources), contexts),
            [struct((group, frames, share, channels))],
            [SMEM] + [ANY] * len(sources) + [VMEM] * 7,
            [scalars, *sources, packed, normed, res_two, wide_kv, wide_out, gather, spread],
            [
                pltpu.VMEM((contexts * share, channels), BF16),
                pltpu.VMEM((contexts * share, 2 * wide), BF16),
                pltpu.VMEM((group, frames * share, keys * wide), BF16),
                pltpu.VMEM((2, frames * share, keys * wide), F32),
                pltpu.VMEM((frames * share, wide), BF16),
                pltpu.SemaphoreType.DMA((contexts,)),
            ],
            2 * group * frames * share * channels * 20 * channels,
            name="attend",
            mib=34,
        )
        parts += [outs[0]] + [lax.ppermute(outs[d], "clip", swaps[d]) for d in range(1, group)]
    (result,) = call(
        functools.partial(assemble_kernel, group, chunks),
        [whole],
        [SMEM] + [VMEM] * len(parts),
        [scalars, *parts],
        name="assemble",
    )
    return result.reshape(frames, rows, cols, channels)


def solution(mesh):
    placed = (P("clip", "tile", None, None), P("clip"), P(), P(), P(), P(), P(), P(), P(), P(), P())
    return jax.shard_map(
        local, mesh=mesh, in_specs=placed, out_specs=P("clip", "tile", None, None), check_vma=False
    )
```

```python
import functools
import math

import jax
import jax.numpy as jnp
import ml_dtypes
import numpy as np
from jax import lax
from jax.experimental import pallas as pl
from jax.experimental.pallas import tpu as pltpu
from jax.sharding import PartitionSpec as P

HEAD_DIM = 64
GROUPS = 32
H = 40
W = 64
EPS = 1e-05
MASKED = -1e30
LANES = 128
FLAG_ROWS = 16
F32 = jnp.float32
BF16 = jnp.bfloat16

SMEM = pl.BlockSpec(memory_space=pltpu.SMEM)
VMEM = pl.BlockSpec(memory_space=pltpu.VMEM)
ANY = pl.BlockSpec(memory_space=pl.ANY)
HBM = pl.BlockSpec(memory_space=pltpu.HBM)


def call(kernel, out_shape, in_specs, args, scratch=(), flops=0, name=None, mib=8, wait=()):
    count = len(args)

    def body(*refs):
        kernel(*refs[:count], *refs[count + len(wait) :])

    return pl.pallas_call(
        body,
        out_shape=out_shape,
        in_specs=[*in_specs, *[ANY] * len(wait)],
        out_specs=[VMEM] * len(out_shape),
        scratch_shapes=list(scratch),
        compiler_params=pltpu.CompilerParams(vmem_limit_bytes=mib * 1024 * 1024),
        cost_estimate=pl.CostEstimate(flops=1, bytes_accessed=1, transcendentals=0),
        name=name,
    )(*args, *wait)


def struct(shape, dtype=BF16):
    return jax.ShapeDtypeStruct(shape, dtype)


def silu(x):
    return 0.5 * x * (1.0 + jnp.tanh(0.5 * x))


def column_sums(v):
    folded = v.reshape(v.shape[0] // 8, 8, v.shape[1])
    return jnp.sum(folded, axis=0), jnp.sum(folded * folded, axis=0)


def split3(x):
    high = x.astype(BF16)
    rest = x - high.astype(F32)
    mid = rest.astype(BF16)
    return high, mid, (rest - mid.astype(F32)).astype(BF16)


def put_stats(f, sums, stats_ref, msg_ref, cols):
    channels = sums.shape[1]
    stats_ref[f] = jnp.concatenate([sums, jnp.zeros((6, channels), F32)], axis=0)
    high, mid, low = split3(sums)
    parts = [high, mid, low, jnp.zeros((FLAG_ROWS - 6, channels), BF16)]
    packed = jnp.concatenate([p.astype(F32) for p in parts], axis=0)
    msg_ref[f, pl.ds(cols, FLAG_ROWS), :] = packed.astype(BF16)


def edge_start(cells, cols):
    return pl.multiple_of(jnp.where(lax.axis_index("tile") == 0, cells - cols, 0), cols)


def stats_kernel(cols, x_hbm, stats_ref, msg_ref, x_ref, sems):
    frames, cells, channels = x_ref.shape
    step = 2 * cols if cells % (2 * cols) == 0 else cols
    copies = [pltpu.make_async_copy(x_hbm.at[f], x_ref.at[f], sems.at[f]) for f in range(frames)]
    for copy in copies:
        copy.start()
    for f in range(frames):
        copies[f].wait()

        def body(i, carry):
            v = x_ref[f, pl.ds(pl.multiple_of(i * step, step), step), :].astype(F32)
            s, q = column_sums(v)
            return carry[0] + s, carry[1] + q

        zero = jnp.zeros((8, channels), F32)
        s, q = lax.fori_loop(0, cells // step, body, (zero, zero))
        sums = jnp.concatenate(
            [jnp.sum(s, axis=0, keepdims=True), jnp.sum(q, axis=0, keepdims=True)], axis=0
        )
        put_stats(f, sums, stats_ref, msg_ref, cols)
        edge = edge_start(cells, cols)
        msg_ref[f, pl.ds(0, cols), :] = x_ref[f, pl.ds(edge, cols), :]


def arrange(pieces):
    big = pieces[0].shape[1] // 256 * 256
    return jnp.concatenate([p[:, :big] for p in pieces] + [p[:, big:] for p in pieces], axis=1)


def spans(index, channels):
    big = channels // 256 * 256
    return ((index * big, big, 0), (3 * big + index * (channels - big), channels - big, big))


def lay_conv(source, target):
    channels = source.shape[1]
    for a in range(3):
        for b in range(3):
            for row, height, from_row in spans(b, channels):
                for col, width, from_col in spans(a, channels):
                    target[row : row + height, col : col + width] = source[
                        3 * a + b, from_row : from_row + height, from_col : from_col + width
                    ]


def first_weights_kernel(first_ref, wide_first):
    lay_conv(first_ref, wide_first)


def weights_kernel(second_ref, time_ref, qkv_ref, out_ref, wide_second, wide_time, wide_q, wide_kv, wide_out):
    channels = out_ref.shape[0]
    lay_conv(second_ref, wide_second)
    for b in range(3):
        for row, height, from_row in spans(b, channels):
            wide_time[row : row + height, :] = time_ref[b, from_row : from_row + height, :]
    wide = wide_out.shape[0]
    wide_q[...] = jnp.zeros_like(wide_q)
    wide_kv[...] = jnp.zeros_like(wide_kv)
    wide_q[:, 0:channels] = qkv_ref[:, 0:channels]
    for part in range(2):
        wide_kv[:, part * wide : part * wide + channels] = qkv_ref[:, (part + 1) * channels : (part + 2) * channels]
    wide_out[...] = jnp.zeros_like(wide_out)
    wide_out[0:channels, :] = out_ref[...]


def conv_kernel(cols, total_cells, first_row, rows, residual, block_rows, x_ref, stats_ref, top_ref, bottom_ref, gain_ref, w_ref, *rest):
    if residual:
        res_in_ref, scalars, *share_refs, wide_x, wide_y, res_rows, res_sem, share_ref = rest
        here = pl.ds(first_row * cols, rows * cols)
        res_copy = pltpu.make_async_copy(res_in_ref.at[:, here], res_rows, res_sem)
        res_copy.start()
        share = cols * rows // share_ref.shape[0]
    else:
        out_ref, out_stats_ref, msg_ref, wide_x, wide_y = rest
    frames, cells, channels = x_ref.shape
    tile_rows = cells // cols
    big = channels // 256 * 256
    small = channels - big
    group_width = channels // GROUPS
    row_group = lax.broadcasted_iota(jnp.int32, (channels, channels), 0) // group_width
    col_group = lax.broadcasted_iota(jnp.int32, (channels, channels), 1) // group_width
    same = (row_group == col_group).astype(F32)
    column = lax.broadcasted_iota(jnp.int32, (cols, 1), 0)
    leftmost, rightmost = column == 0, column == cols - 1

    scales = []
    for f in range(frames):
        other = top_ref[f, pl.ds(cols, FLAG_ROWS), :].astype(F32)
        sums = stats_ref[f, 0:2, :] + other[0:2] + other[2:4] + other[4:6]
        sums = jnp.concatenate([sums, jnp.zeros((6, channels), F32)], axis=0)
        means = jnp.dot(
            sums, same, preferred_element_type=F32, precision=lax.Precision.HIGHEST
        ) / (total_cells * group_width)
        centre = means[0:1]
        scale = lax.rsqrt(means[1:2] - centre * centre + EPS) * gain_ref[...]
        scales.append((scale, -centre * scale))

    def widen(f, padded_row):
        row = first_row + padded_row - 1
        if row < 0:
            raw, keep = top_ref[f, 0:cols, :], lax.axis_index("tile") > 0
        elif row >= tile_rows:
            raw, keep = bottom_ref[f, 0:cols, :], lax.axis_index("tile") < lax.axis_size("tile") - 1
        else:
            raw, keep = x_ref[f, row * cols : (row + 1) * cols, :], None
        scale, shift = scales[f]
        y = silu(raw.astype(F32) * scale + shift)
        if keep is not None:
            y = jnp.where(keep, y, 0.0)
        left = jnp.where(leftmost, 0.0, pltpu.roll(y, 1, 0))
        right = jnp.where(rightmost, 0.0, pltpu.roll(y, cols - 1, 0))
        wide_x[f, padded_row * cols : (padded_row + 1) * cols, :] = arrange([left, y, right]).astype(BF16)

    def multiply(f, start, stop):
        here = slice(start * cols, stop * cols)
        wide_y[f, here, :] = jnp.dot(wide_x[f, here, :], w_ref[...], preferred_element_type=F32)

    totals = [[jnp.zeros((8, channels), F32)] * 2 for _ in range(frames)]

    def finish(f, r):
        parts = []
        for base, width in ((0, big), (3 * big, small)):
            parts.append(
                wide_y[f, r * cols : (r + 1) * cols, base : base + width]
                + wide_y[f, (r + 1) * cols : (r + 2) * cols, base + width : base + 2 * width]
                + wide_y[f, (r + 2) * cols : (r + 3) * cols, base + 2 * width : base + 3 * width]
            )
        total = jnp.concatenate(parts, axis=1)
        here = slice(r * cols, (r + 1) * cols)
        if residual:
            total = (res_rows[f, here, :].astype(F32) + total).astype(BF16)
            put_share(scalars, share_ref, f, r * cols, total, share)
        else:
            total = total.astype(BF16)
            out_ref[f, here, :] = total
            s, q = column_sums(total.astype(F32))
            totals[f] = [totals[f][0] + s, totals[f][1] + q]

    blocks = []
    for f in range(frames):
        edges = list(range(0, rows + 2, block_rows)) + [rows + 2]
        blocks += [(f, edges[i], edges[i + 1]) for i in range(len(edges) - 1)]

    def act(block):
        for p in range(block[1], block[2]):
            widen(block[0], p)

    def end(block):
        for p in range(block[1], block[2]):
            if p >= 2:
                finish(block[0], p - 2)

    act(blocks[0])
    if residual:
        res_copy.wait()
    for i, block in enumerate(blocks):
        multiply(*block)
        if i + 1 < len(blocks):
            act(blocks[i + 1])
        if i > 0:
            end(blocks[i - 1])
    end(blocks[-1])
    if residual:
        for f in range(frames):
            flag = jnp.full((FLAG_ROWS, LANES), jnp.where(f < scalars[3], 1.0, 0.0), F32)
            for d in range(share_ref.shape[0]):
                share_ref[d, f, pl.ds(dense_rows(share)[0], FLAG_ROWS), :] = flag.astype(BF16)
        for d, ref in enumerate(share_refs):
            ref[...] = share_ref[d]
    else:
        for f in range(frames):
            sums = jnp.concatenate([jnp.sum(t, axis=0, keepdims=True) for t in totals[f]], axis=0)
            put_stats(f, sums, out_stats_ref, msg_ref, cols)
            edge = edge_start(cells, cols)
            msg_ref[f, pl.ds(0, cols), :] = out_ref[f, pl.ds(edge, cols), :]


def dense_rows(share):
    half = (share // 2 + 15) // 16 * 16
    return 2 * share + half, half


def put_dense(ref, where, start, x, share):
    _, half = dense_rows(share)
    count = x.shape[0]
    ref[(*where, slice(start, start + count), slice(None))] = x[:, 0:LANES]
    ref[(*where, slice(share + start, share + start + count), slice(None))] = x[:, LANES : 2 * LANES]
    rest = x.shape[1] - 2 * LANES
    side, row = (0, start) if start < half else (1, start - half)
    row += 2 * share
    ref[(*where, slice(row, row + count), slice(side * rest, (side + 1) * rest))] = x[:, 2 * LANES :]


def get_dense(ref, where, start, count, share, channels):
    _, half = dense_rows(share)
    rest = channels - 2 * LANES
    side, row = (0, start) if start < half else (1, start - half)
    row += 2 * share
    third = ref[(*where, slice(row, row + count), slice(None))]
    return jnp.concatenate(
        [
            ref[(*where, slice(start, start + count), slice(None))],
            ref[(*where, slice(share + start, share + start + count), slice(None))],
            third[:, side * rest : (side + 1) * rest],
        ],
        axis=1,
    )


def halves(share):
    _, half = dense_rows(share)
    return ((0, half), (half, share - half))


def put_share(scalars, out_ref, f, start, total, share):
    piece = math.gcd(math.gcd(share, total.shape[0]), dense_rows(share)[1])
    for p in range(0, total.shape[0], piece):
        owner, inside = divmod(start + p, share)
        put_dense(out_ref, (scalars[8 + owner], f), inside, total[p : p + piece], share)


def ends_kernel(group, scalars, *rest):
    own, (one_ref, two_ref) = rest[:group], rest[group:]
    dense = one_ref.shape[0]
    odd = scalars[5] > 0
    for d in range(group):
        for ref, upper in ((one_ref, odd), (two_ref, jnp.logical_not(odd))):

            @pl.when(jnp.logical_and(jnp.logical_not(upper), scalars[4] ^ d == group - 1))
            def _():
                live = own[d][1, pl.ds(dense, FLAG_ROWS), :].astype(F32)[0:1] > 0.5
                ref[...] = jnp.where(
                    live, own[d][1, 0:dense, :].astype(F32), own[d][0, 0:dense, :].astype(F32)
                ).astype(BF16)

            @pl.when(jnp.logical_and(upper, scalars[4] == d))
            def _():
                ref[...] = own[d][0, 0:dense, :]


def time_kernel(group, scalars, *rest):
    own, (one_ref, two_ref, w_ref, gain_ref) = rest[:group], rest[group : group + 4]
    res_two_ref, normed_ref, *pick_refs, ordered, moving, edge, picks = rest[group + 4 :]
    _, frames, share, channels = res_two_ref.shape
    dense = one_ref.shape[0]
    odd = scalars[5] > 0
    for d in range(group):
        ordered[scalars[8 + d]] = own[d][...]

    def lively(x):
        return silu(x.astype(F32)).astype(BF16)

    for m in range(group):
        for f in range(frames):
            moving[m, f] = lively(ordered[m, f, 0:dense, :])
    one, two = one_ref[...].astype(F32), two_ref[...].astype(F32)
    edge[0] = lively(jnp.where(odd, one, two))
    edge[1] = lively(jnp.where(odd, two, one))
    live = [ordered[m, 1, dense : dense + FLAG_ROWS, :].astype(F32)[0:1, 0:1] > 0.5 for m in range(group)]
    for m in range(group):
        for start, step in halves(share):

            def cells(ref, *where):
                return get_dense(ref, where, start, step, share, channels).astype(F32)

            here = slice(start, start + step)
            first, second = cells(moving, m, 0), cells(moving, m, 1)
            if m:
                prior = jnp.where(live[m - 1], cells(moving, m - 1, 1), cells(moving, m - 1, 0))
            else:
                prior = cells(edge, 0)
            later = cells(moving, m + 1, 0) if m + 1 < group else cells(edge, 1)
            rows = [
                arrange([prior, first, jnp.where(live[m], second, later)]),
                arrange([first, second, jnp.where(live[m], later, 0.0)]),
            ]
            mixed = jnp.dot(
                jnp.concatenate(rows, axis=0).astype(BF16), w_ref[...], preferred_element_type=F32
            )
            norms = []
            for f in range(frames):
                total = (cells(ordered, m, f) + mixed[f * step : (f + 1) * step]).astype(BF16)
                res_two_ref[m, f, here, :] = total
                v = total.astype(F32)
                v = v - jnp.mean(v, axis=1, keepdims=True)
                spread = jnp.mean(v * v, axis=1, keepdims=True)
                normed = v * lax.rsqrt(spread + EPS) * gain_ref[...]
                norms.append(normed)
                normed_ref[m, f, here, :] = normed.astype(BF16)
            picked = jnp.where(scalars[8 + group + m] > 0, norms[1], norms[0]).astype(BF16)
            put_dense(picks, (scalars[8 + 2 * group + m],), start, picked, share)
        for f in range(frames):
            flag = ordered[m, f, dense : dense + FLAG_ROWS, :].astype(F32)[:, 0:1]
            normed_ref[m, f, share : share + FLAG_ROWS, :] = jnp.broadcast_to(flag, (FLAG_ROWS, channels)).astype(BF16)
    both_ref, *part_refs = pick_refs
    both_ref[...] = picks[...]
    for i, ref in enumerate(part_refs):
        ref[...] = picks[2 * i : 2 * i + 2]


def pack_kernel(normed_ref, wq_ref, wkv_ref, packed_ref):
    group, frames, flagged, channels = normed_ref.shape
    share = flagged - FLAG_ROWS
    for m in range(group):
        rows = jnp.concatenate([normed_ref[m, f, 0:share, :] for f in range(frames)], axis=0)
        wide = wq_ref.shape[1]
        packed_ref[m, :, 0:wide] = jnp.dot(rows, wq_ref[...], preferred_element_type=F32).astype(BF16)
        packed_ref[m, :, wide:] = jnp.dot(rows, wkv_ref[...], preferred_element_type=F32).astype(BF16)


def head_maps(keys, channels, wide):
    column = np.arange(keys * wide)
    lane = column // wide * 8 + column % wide // HEAD_DIM
    hit = (lane[:, None] == np.arange(LANES)[None, :]) & (column % wide < channels)[:, None]
    return (hit * HEAD_DIM ** (-0.5)).astype(ml_dtypes.bfloat16), hit.T.astype(ml_dtypes.bfloat16)


def shared_kernel(buffers, contexts, base, share, scalars, *rest):
    sources, (wkv_ref, shared_ref, dense_context, context, sems) = rest[:buffers], rest[buffers:]
    channels = context.shape[1]
    for j in range(contexts):
        for b in range(buffers):

            @pl.when(scalars[base + 2 * j] == b)
            def _():
                pltpu.make_async_copy(
                    sources[b].at[scalars[base + 1 + 2 * j]], dense_context.at[j], sems.at[j]
                ).start()

    for j in range(contexts):
        pltpu.make_async_copy(sources[0].at[0], dense_context.at[j], sems.at[j]).wait()
        for start, count in halves(share):
            at = j * share + start
            context[at : at + count, :] = get_dense(dense_context, (j,), start, count, share, channels)
    half = contexts // 2 * share
    for s in (0, half):
        shared_ref[s : s + half, :] = jnp.dot(
            context[s : s + half, :], wkv_ref[...], preferred_element_type=F32
        ).astype(BF16)


def attend_kernel(contexts, who, scalars, shared, packed_ref, normed_ref, res_ref, wout_ref, gather_hbm, spread_hbm, *rest):
    out_refs = rest[: len(who)]
    products, spreads, joined, gather_ref, spread_ref, sems = rest[len(who) :]
    group, frames, share, channels = res_ref.shape
    heads = channels // HEAD_DIM
    wide = wout_ref.shape[0]
    keys = frames + contexts
    gather_copy = pltpu.make_async_copy(gather_hbm, gather_ref, sems.at[0])
    spread_copy = pltpu.make_async_copy(spread_hbm, spread_ref, sems.at[1])
    gather_copy.start()
    spread_copy.start()
    at_member = [scalars[8 + d] for d in who]
    lane = lax.broadcasted_iota(jnp.int32, (1, LANES), 1)
    in_use = jnp.logical_and(lane % 8 < heads, lane // 8 < keys)

    piece = 32 if share % 32 == 0 else 16

    def key_value(m, j, s, part):
        if j < frames:
            at = j * share + s
            return packed_ref[at_member[m], at : at + piece, (1 + part) * wide : (2 + part) * wide]
        at = (j - frames) * share + s
        return shared[at : at + piece, part * wide : (part + 1) * wide]

    def multiply(m):
        for s in range(0, share, piece):
            queries = [packed_ref[at_member[m], f * share + s : f * share + s + piece, 0:wide] for f in range(frames)]
            for j in range(keys):
                key = key_value(m, j, s, 0)
                for f in range(frames):
                    at = f * share + s
                    products[m, at : at + piece, j * wide : (j + 1) * wide] = queries[f] * key

    def weigh(m):
        flags = normed_ref[at_member[m], :, share : share + FLAG_ROWS, 0:LANES].astype(F32)
        visible = in_use
        for f in range(frames):
            dead = jnp.logical_and(lane // 8 == f, flags[f, 0:1] < 0.5)
            visible = jnp.logical_and(visible, jnp.logical_not(dead))
        scores = scored[m]
        scores = jnp.where(visible, scores, MASKED)
        top = scores
        for shift in (8, 16, 32, 64):
            top = jnp.maximum(top, pltpu.roll(top, shift, 1))
        raised = jnp.exp(scores - top)
        total = raised
        for shift in (8, 16, 32, 64):
            total = total + pltpu.roll(total, shift, 1)
        weights = (raised / total).astype(BF16)
        spreads[m % 2] = jnp.dot(weights, spread_ref[...], preferred_element_type=F32)

    def combine(m):
        for s in range(0, share, piece):
            results = [jnp.zeros((piece, wide), F32) for _ in range(frames)]
            for j in range(keys):
                value = key_value(m, j, s, 1).astype(F32)
                for f in range(frames):
                    at = f * share + s
                    results[f] = results[f] + spreads[m % 2, at : at + piece, j * wide : (j + 1) * wide] * value
            for f in range(frames):
                joined[f * share + s : f * share + s + piece, :] = results[f].astype(BF16)
        added = jnp.dot(joined[...], wout_ref[...], preferred_element_type=F32)
        for f in range(frames):
            live = normed_ref[at_member[m], f, share : share + FLAG_ROWS, :].astype(F32)[0:1] > 0.5
            total = res_ref[at_member[m], f].astype(F32) + added[f * share : (f + 1) * share]
            total = jnp.where(live, total, 0.0).astype(BF16)
            for start, count in halves(share):
                put_dense(out_refs[m], (f,), start, total[start : start + count], share)

    count = len(who)
    for m in range(count):
        multiply(m)
    gather_copy.wait()
    scored = [jnp.dot(products[m], gather_ref[...], preferred_element_type=F32) for m in range(count)]
    spread_copy.wait()
    for m in range(count):
        weigh(m)
        if m > 0:
            combine(m - 1)
    combine(count - 1)


def assemble_kernel(group, chunks, scalars, *rest):
    parts, out_ref = rest[:-1], rest[-1]
    frames, cells, channels = out_ref.shape
    share = cells // (chunks * group)
    for c in range(chunks):
        for d in range(group):
            place = (c * group + scalars[8 + d]) * share
            for f in range(frames):
                for start, count in halves(share):
                    out_ref[f, pl.ds(pl.multiple_of(place + start, 16), count), :] = get_dense(
                        parts[c * group + d], (f,), start, count, share, channels
                    )


def share_tile(stats, msg, source, cols):
    tiles = lax.axis_size("tile")
    if tiles == 2:
        got = lax.ppermute(msg, "tile", [(0, 1), (1, 0)])
        return stats, got, got
    down = [(i, i + 1) for i in range(tiles - 1)]
    up = [(i + 1, i) for i in range(tiles - 1)]
    pad = ((0, 0), (0, FLAG_ROWS), (0, 0))
    top = lax.ppermute(source[:, -cols:], "tile", down)
    bottom = lax.ppermute(source[:, :cols], "tile", up)
    return lax.psum(stats, "tile"), jnp.pad(top, pad), jnp.pad(bottom, pad)


def place_of(level, source, slot, levels):
    if levels != 4:
        hop = level - source
        return jnp.where(hop >= 0, hop, levels - 1 - hop), slot
    apart = level ^ source
    late = slot > 1
    outer = jnp.logical_or(level == 0, level == 3)
    from_outer = jnp.logical_or(source == 0, source == 3)
    whole = jnp.logical_or(apart < 2, jnp.logical_and(apart == 3, outer))
    two = jnp.where(late, jnp.where(from_outer, 5, 7), 4)
    three = jnp.where(outer, 2, jnp.where(late, 6, 3))
    buffer = jnp.where(apart < 2, apart, jnp.where(apart == 2, two, three))
    return buffer, jnp.where(jnp.logical_or(whole, jnp.logical_not(late)), slot, slot - 2)


def plan_kernel(group, frames, length, lengths_ref, context_ref, out_ref):
    contexts = context_ref.shape[0]
    levels = lax.axis_size("clip") // group
    clip = lax.axis_index("clip")
    level, member = lax.div(clip, group), lax.rem(clip, group)
    for i in range(length):
        out_ref[i] = 0
    out_ref[3] = lengths_ref[0]
    out_ref[4] = member
    out_ref[5] = lax.rem(level, 2)
    frame = [context_ref[j] for j in range(contexts)]
    owner = [lax.div(c, frames) for c in frame]
    source = [lax.div(c, group) for c in owner]

    def one(flag):
        return jnp.where(flag, 1, 0)

    crowded = 0
    for j in range(contexts):
        slot = 0
        for i in range(contexts):
            if i != j:
                slot = slot + one(jnp.logical_and(source[i] == source[j], owner[i] < owner[j]))
        inner = jnp.logical_and(source[j] > 0, source[j] < levels - 1)
        crowded = jnp.maximum(crowded, one(jnp.logical_and(slot > 1, inner)))
        buffer, place = place_of(level, source[j], slot, levels)
        out_ref[8 + 3 * group + 2 * j] = buffer
        out_ref[9 + 3 * group + 2 * j] = place
    out_ref[6] = crowded
    named, second = [], []
    for m in range(group):
        mine = level * group + m
        hit, late = 0, 0
        for j in range(contexts):
            hit = jnp.maximum(hit, one(owner[j] == mine))
            late = jnp.maximum(late, one(frame[j] == mine * frames + 1))
        named.append(hit)
        second.append(late)
    before, empty = 0, sum(named)
    for m in range(group):
        out_ref[8 + m] = member ^ m
        out_ref[8 + group + m] = second[m]
        out_ref[8 + 2 * group + m] = jnp.where(named[m] > 0, before, empty)
        before, empty = before + named[m], empty + 1 - named[m]


def send(x, pairs, group):
    return lax.ppermute(x, "clip", [(a * group + i, b * group + i) for a, b in pairs for i in range(group)])


SWAP = [(0, 1), (1, 0), (2, 3), (3, 2)]


def turn_kernel(far_ref, far_high_ref, on_ref):
    on_ref[0:2] = far_ref[...]
    on_ref[2:4] = far_high_ref[...]


def send_near(both, low, high, levels, group):
    if levels != 4:
        return (both,)
    return (
        send(low, [(0, 2), (2, 0), (1, 3), (3, 1)], group),
        send(high, [(0, 2), (3, 1)], group),
        send(low, [(1, 2), (2, 1)], group),
        send(both, [(0, 1), (1, 0), (2, 3), (3, 2)], group),
    )


def empty_kernel(_, *refs):
    for ref in refs:
        ref[...] = jnp.zeros_like(ref)


def send_crowd(high, crowded, group):
    def crowd(high):
        return send(high, [(1, 2), (2, 1)], group), send(high, [(1, 3), (2, 0)], group)

    return lax.cond(crowded, crowd, lambda high: tuple(call(empty_kernel, [struct(high.shape)] * 2, [ANY], [high])), high)


def send_on(both, high, got, crowded, levels, group, wait):
    if levels != 4:
        lower, upper = [both], [both]
        for _ in range(levels - 1):
            lower.append(send(lower[-1], [(i, i + 1) for i in range(levels - 1)], group))
            upper.append(send(upper[-1], [(i + 1, i) for i in range(levels - 1)], group))
        return lower + upper[1:], got
    far, far_high, middle, near = got
    crowd = send_crowd(high, crowded, group)
    (on,) = call(
        turn_kernel,
        [struct(both.shape)],
        [VMEM] * 2,
        [far, far_high],
        name="turn",
        wait=(near, middle, *crowd, *wait),
    )
    outer = send(on, [(1, 0), (2, 3)], group)
    return [both, near, outer, middle, far, far_high, *crowd], (on,)


def local(
    latents,
    lengths,
    context,
    gain_first,
    conv_first,
    gain_second,
    conv_second,
    time_weight,
    attn_gain,
    w_qkv,
    w_out,
):
    frames, rows, cols, channels = latents.shape
    cells = rows * cols
    tiles, clips = lax.axis_size("tile"), lax.axis_size("clip")
    group = 4
    chunks = 2 if rows % 2 == 0 and cells % (2 * group * 16) == 0 else 1
    levels = clips // group
    share = cells // (group * chunks)
    dense, _ = dense_rows(share)
    contexts = context.shape[0]
    total_cells = cells * tiles
    wide = (channels + LANES - 1) // LANES * LANES
    keys = frames + contexts

    length = 8 + 3 * group + 2 * contexts
    scalars = pl.pallas_call(
        functools.partial(plan_kernel, group, frames, length),
        out_shape=struct((length,), jnp.int32),
        in_specs=[SMEM] * 2,
        out_specs=SMEM,
        name="plan",
    )(lengths, context)
    crowded = scalars[6] > 0

    x = latents.reshape(frames, cells, channels)
    message = struct((frames, cols + FLAG_ROWS, channels))
    sums = struct((frames, 8, channels), F32)
    whole = struct((frames, cells, channels))
    x_scratch = [pltpu.SemaphoreType.DMA((frames,))]
    stats, msg, near_x = call(
        functools.partial(stats_kernel, cols), [sums, message, whole], [HBM], [x], x_scratch, name="first_sums"
    )
    stats, top, bottom = share_tile(stats, msg, x, cols)
    square = struct((3 * channels, 3 * channels))
    (wide_first,) = call(
        first_weights_kernel, [square], [VMEM], [conv_first.reshape(9, channels, channels)], name="first_weights"
    )
    gather, spread = (jnp.asarray(a) for a in head_maps(keys, channels, wide))

    part = struct((frames, dense + FLAG_ROWS, LANES))

    def conv(first_row, count, residual, outs, source, stats, top, bottom, gain, weight, *more):
        scratch = [
            pltpu.VMEM((frames, (count + 2) * cols, 3 * channels), BF16),
            pltpu.VMEM((frames, (count + 2) * cols, 3 * channels), F32),
        ]
        if residual:
            scratch += [
                pltpu.VMEM((frames, count * cols, channels), BF16),
                pltpu.SemaphoreType.DMA,
                pltpu.VMEM((group, *part.shape), BF16),
            ]
        block_rows = 11 if count == 20 else 8
        return call(
            functools.partial(conv_kernel, cols, total_cells, first_row, count, residual, block_rows),
            outs,
            [VMEM] * 6 + [HBM, SMEM][: len(more)],
            [source, stats, top, bottom, gain.reshape(1, channels), weight, *more],
            scratch,
            2 * frames * (count + 2) * cols * 9 * channels * channels,
            name="conv_two" if residual else "conv_one",
            mib=26,
        )

    hidden, stats, msg = conv(0, rows, False, [whole, sums, message], near_x, stats, top, bottom, gain_first, wide_first)
    wide_second, wide_time, wide_q, wide_kv, wide_out = call(
        weights_kernel,
        [
            square,
            struct((3 * channels, channels)),
            struct((channels, wide)),
            struct((channels, 2 * wide)),
            struct((wide, channels)),
        ],
        [VMEM] * 4,
        [conv_second.reshape(9, channels, channels), time_weight, w_qkv, w_out],
        name="weights",
        wait=(stats,),
    )
    stats, top, bottom = share_tile(stats, msg, hidden, cols)
    swaps = [[(i, i ^ d) for i in range(clips)] for d in range(group)]
    pairs = [[(i, i + 1) for i in range(a, levels - 1, 2)] for a in range(2)]
    beside = [
        [(u * group + i, v * group + i) for a, b in p for u, v in ((a, b), (b, a)) for i in range(group)] for p in pairs
    ]

    shares_of = []
    for c in range(chunks):
        shares = conv(
            c * rows // chunks,
            rows // chunks,
            True,
            [part] * group,
            hidden,
            stats,
            top,
            bottom,
            gain_second,
            wide_second,
            x,
            scalars,
        )
        shares_of.append(shares)

    def mix(own, *before):
        end = struct((dense, LANES))
        one, two = call(
            functools.partial(ends_kernel, group), [end, end], [SMEM] + [VMEM] * group, [scalars, *own], name="ends",
            wait=shares_of[-1][:1],
        )
        one = lax.ppermute(one, "clip", beside[0])
        two = lax.ppermute(two, "clip", beside[1])
        both = (group, frames, share, channels)
        flagged = (group, frames, share + FLAG_ROWS, channels)
        res_two, normed, *picked = call(
            functools.partial(time_kernel, group),
            [struct(both), struct(flagged), struct((group, dense, LANES))] + [struct((2, dense, LANES))] * (group // 2),
            [SMEM] + [VMEM] * (group + 4),
            [scalars, *own, one, two, wide_time, attn_gain.reshape(1, channels)],
            [
                pltpu.VMEM((group, frames, dense + FLAG_ROWS, LANES), BF16),
                pltpu.VMEM((group, frames, dense, LANES), BF16),
                pltpu.VMEM((2, dense, LANES), BF16),
                pltpu.VMEM((group, dense, LANES), BF16),
            ],
            2 * frames * group * share * 3 * channels * channels,
            name="time_mix",
            wait=before,
        )
        return res_two, normed, *picked

    def exchange(shares):
        return [shares[0]] + [lax.ppermute(shares[d], "clip", swaps[d]) for d in range(1, group)]

    def shared_kv(sources):
        (shared,) = call(
            functools.partial(shared_kernel, len(sources), contexts, 8 + 3 * group, share),
            [struct((contexts * share, 2 * wide))],
            [SMEM] + [ANY] * len(sources) + [VMEM],
            [scalars, *sources, wide_kv],
            [
                pltpu.VMEM((contexts, dense, LANES), BF16),
                pltpu.VMEM((contexts * share, channels), BF16),
                pltpu.SemaphoreType.DMA((contexts,)),
            ],
            name="shared",
        )
        return shared

    def attention(res_two, normed, shared, calls):
        (packed,) = call(
            pack_kernel,
            [struct((group, frames * share, 3 * wide))],
            [VMEM] * 3,
            [normed, wide_q, wide_kv],
            flops=2 * group * frames * share * channels * 3 * wide,
            name="pack",
        )
        parts = [None] * group
        for who, wait in calls:
            outs = call(
                functools.partial(attend_kernel, contexts, who),
                [struct((frames, dense, LANES))] * len(who),
                [SMEM] + [VMEM] * 5 + [HBM] * 2,
                [scalars, shared, packed, normed, res_two, wide_out, gather, spread],
                [
                    pltpu.VMEM((len(who), frames * share, keys * wide), BF16),
                    pltpu.VMEM((2, frames * share, keys * wide), F32),
                    pltpu.VMEM((frames * share, wide), BF16),
                    pltpu.VMEM((keys * wide, LANES), BF16),
                    pltpu.VMEM((LANES, keys * wide), BF16),
                    pltpu.SemaphoreType.DMA((2,)),
                ],
                name="attend",
                mib=26,
                wait=wait,
            )
            for i, d in enumerate(who):
                parts[d] = lax.ppermute(outs[i], "clip", swaps[d]) if d else outs[i]
        return parts

    def across(both, low, high, wait=()):
        got = send_near(both, low, high, levels, group)
        return send_on(both, high, got, crowded, levels, group, wait)

    own = exchange(shares_of[0])
    later = [exchange(shares) for shares in shares_of[1:]]
    res_two, normed, *picked = mix(own)
    buffers, turned = across(*picked)
    parts = []
    for own in later:
        next_res_two, next_normed, *picked = mix(own, *turned)
        shared = shared_kv(buffers)
        buffers, turned = across(*picked, (shared,))
        parts += attention(res_two, normed, shared, (((2, 3), turned), ((0, 1), buffers[2:3])))
        res_two, normed = next_res_two, next_normed
    parts += attention(res_two, normed, shared_kv(buffers), (((2, 3, 1), ()), ((0,), ())))
    (result,) = call(
        functools.partial(assemble_kernel, group, chunks),
        [whole],
        [SMEM] + [VMEM] * len(parts),
        [scalars, *parts],
        name="assemble",
    )
    return result.reshape(frames, rows, cols, channels)


def solution(mesh):
    placed = (P("clip", "tile", None, None), P("clip"), P(), P(), P(), P(), P(), P(), P(), P(), P())
    return jax.shard_map(
        local, mesh=mesh, in_specs=placed, out_specs=P("clip", "tile", None, None), check_vma=False
    )
```

```python
import functools
import math

import jax
import jax.numpy as jnp
import ml_dtypes
import numpy as np
from jax import lax
from jax.experimental import pallas as pl
from jax.experimental.pallas import tpu as pltpu
from jax.sharding import PartitionSpec as P

HEAD_DIM = 64
GROUPS = 32
H = 40
W = 64
EPS = 1e-05
MASKED = -1e30
LANES = 128
FLAG_ROWS = 16
F32 = jnp.float32
BF16 = jnp.bfloat16

SMEM = pl.BlockSpec(memory_space=pltpu.SMEM)
VMEM = pl.BlockSpec(memory_space=pltpu.VMEM)
ANY = pl.BlockSpec(memory_space=pl.ANY)
HBM = pl.BlockSpec(memory_space=pltpu.HBM)


def call(kernel, out_shape, in_specs, args, scratch=(), flops=0, name=None, mib=8, wait=()):
    count = len(args)

    def body(*refs):
        kernel(*refs[:count], *refs[count + len(wait) :])

    return pl.pallas_call(
        body,
        out_shape=out_shape,
        in_specs=[*in_specs, *[ANY] * len(wait)],
        out_specs=[VMEM] * len(out_shape),
        scratch_shapes=list(scratch),
        compiler_params=pltpu.CompilerParams(vmem_limit_bytes=mib * 1024 * 1024),
        cost_estimate=pl.CostEstimate(flops=1, bytes_accessed=1, transcendentals=0),
        name=name,
    )(*args, *wait)


def struct(shape, dtype=BF16):
    return jax.ShapeDtypeStruct(shape, dtype)


def silu(x):
    return 0.5 * x * (1.0 + jnp.tanh(0.5 * x))


def column_sums(v):
    folded = v.reshape(v.shape[0] // 8, 8, v.shape[1])
    return jnp.sum(folded, axis=0), jnp.sum(folded * folded, axis=0)


def split3(x):
    high = x.astype(BF16)
    rest = x - high.astype(F32)
    mid = rest.astype(BF16)
    return high, mid, (rest - mid.astype(F32)).astype(BF16)


def put_stats(f, sums, stats_ref, msg_ref, cols):
    channels = sums.shape[1]
    stats_ref[f] = jnp.concatenate([sums, jnp.zeros((6, channels), F32)], axis=0)
    high, mid, low = split3(sums)
    parts = [high, mid, low, jnp.zeros((FLAG_ROWS - 6, channels), BF16)]
    packed = jnp.concatenate([p.astype(F32) for p in parts], axis=0)
    msg_ref[f, pl.ds(cols, FLAG_ROWS), :] = packed.astype(BF16)


def edge_start(cells, cols):
    return pl.multiple_of(jnp.where(lax.axis_index("tile") == 0, cells - cols, 0), cols)


def stats_kernel(cols, x_hbm, stats_ref, msg_ref, x_ref, sems):
    frames, cells, channels = x_ref.shape
    step = 2 * cols if cells % (2 * cols) == 0 else cols
    copies = [pltpu.make_async_copy(x_hbm.at[f], x_ref.at[f], sems.at[f]) for f in range(frames)]
    for copy in copies:
        copy.start()
    for f in range(frames):
        copies[f].wait()

        def body(i, carry):
            v = x_ref[f, pl.ds(pl.multiple_of(i * step, step), step), :].astype(F32)
            s, q = column_sums(v)
            return carry[0] + s, carry[1] + q

        zero = jnp.zeros((8, channels), F32)
        s, q = lax.fori_loop(0, cells // step, body, (zero, zero))
        sums = jnp.concatenate(
            [jnp.sum(s, axis=0, keepdims=True), jnp.sum(q, axis=0, keepdims=True)], axis=0
        )
        put_stats(f, sums, stats_ref, msg_ref, cols)
        edge = edge_start(cells, cols)
        msg_ref[f, pl.ds(0, cols), :] = x_ref[f, pl.ds(edge, cols), :]


def arrange(pieces):
    big = pieces[0].shape[1] // 256 * 256
    return jnp.concatenate([p[:, :big] for p in pieces] + [p[:, big:] for p in pieces], axis=1)


def spans(index, channels):
    big = channels // 256 * 256
    return ((index * big, big, 0), (3 * big + index * (channels - big), channels - big, big))


def lay_conv(source, target):
    channels = source.shape[1]
    for a in range(3):
        for b in range(3):
            for row, height, from_row in spans(b, channels):
                for col, width, from_col in spans(a, channels):
                    target[row : row + height, col : col + width] = source[
                        3 * a + b, from_row : from_row + height, from_col : from_col + width
                    ]


def first_weights_kernel(first_ref, wide_first):
    lay_conv(first_ref, wide_first)


def weights_kernel(second_ref, time_ref, qkv_ref, out_ref, wide_second, wide_time, wide_q, wide_kv, wide_out):
    channels = out_ref.shape[0]
    lay_conv(second_ref, wide_second)
    for b in range(3):
        for row, height, from_row in spans(b, channels):
            wide_time[row : row + height, :] = time_ref[b, from_row : from_row + height, :]
    wide = wide_out.shape[0]
    wide_q[...] = jnp.zeros_like(wide_q)
    wide_kv[...] = jnp.zeros_like(wide_kv)
    wide_q[:, 0:channels] = qkv_ref[:, 0:channels]
    for part in range(2):
        wide_kv[:, part * wide : part * wide + channels] = qkv_ref[:, (part + 1) * channels : (part + 2) * channels]
    wide_out[...] = jnp.zeros_like(wide_out)
    wide_out[0:channels, :] = out_ref[...]


def conv_kernel(cols, total_cells, first_row, rows, residual, block_rows, x_ref, stats_ref, top_ref, bottom_ref, gain_ref, w_ref, *rest):
    if residual:
        res_in_ref, scalars, *share_refs, wide_x, wide_y, res_rows, res_sem, share_ref = rest
        here = pl.ds(first_row * cols, rows * cols)
        res_copy = pltpu.make_async_copy(res_in_ref.at[:, here], res_rows, res_sem)
        res_copy.start()
        share = cols * rows // share_ref.shape[0]
    else:
        out_ref, out_stats_ref, msg_ref, wide_x, wide_y = rest
    frames, cells, channels = x_ref.shape
    tile_rows = cells // cols
    big = channels // 256 * 256
    small = channels - big
    group_width = channels // GROUPS
    row_group = lax.broadcasted_iota(jnp.int32, (channels, channels), 0) // group_width
    col_group = lax.broadcasted_iota(jnp.int32, (channels, channels), 1) // group_width
    same = (row_group == col_group).astype(F32)
    column = lax.broadcasted_iota(jnp.int32, (cols, 1), 0)
    leftmost, rightmost = column == 0, column == cols - 1

    scales = []
    for f in range(frames):
        other = top_ref[f, pl.ds(cols, FLAG_ROWS), :].astype(F32)
        sums = stats_ref[f, 0:2, :] + other[0:2] + other[2:4] + other[4:6]
        sums = jnp.concatenate([sums, jnp.zeros((6, channels), F32)], axis=0)
        means = jnp.dot(
            sums, same, preferred_element_type=F32, precision=lax.Precision.HIGHEST
        ) / (total_cells * group_width)
        centre = means[0:1]
        scale = lax.rsqrt(means[1:2] - centre * centre + EPS) * gain_ref[...]
        scales.append((scale, -centre * scale))

    def widen(f, padded_row):
        row = first_row + padded_row - 1
        if row < 0:
            raw, keep = top_ref[f, 0:cols, :], lax.axis_index("tile") > 0
        elif row >= tile_rows:
            raw, keep = bottom_ref[f, 0:cols, :], lax.axis_index("tile") < lax.axis_size("tile") - 1
        else:
            raw, keep = x_ref[f, row * cols : (row + 1) * cols, :], None
        scale, shift = scales[f]
        y = silu(raw.astype(F32) * scale + shift)
        if keep is not None:
            y = jnp.where(keep, y, 0.0)
        left = jnp.where(leftmost, 0.0, pltpu.roll(y, 1, 0))
        right = jnp.where(rightmost, 0.0, pltpu.roll(y, cols - 1, 0))
        wide_x[f, padded_row * cols : (padded_row + 1) * cols, :] = arrange([left, y, right]).astype(BF16)

    def multiply(f, start, stop):
        here = slice(start * cols, stop * cols)
        wide_y[f, here, :] = jnp.dot(wide_x[f, here, :], w_ref[...], preferred_element_type=F32)

    totals = [[jnp.zeros((8, channels), F32)] * 2 for _ in range(frames)]

    def finish(f, r):
        parts = []
        for base, width in ((0, big), (3 * big, small)):
            parts.append(
                wide_y[f, r * cols : (r + 1) * cols, base : base + width]
                + wide_y[f, (r + 1) * cols : (r + 2) * cols, base + width : base + 2 * width]
                + wide_y[f, (r + 2) * cols : (r + 3) * cols, base + 2 * width : base + 3 * width]
            )
        total = jnp.concatenate(parts, axis=1)
        here = slice(r * cols, (r + 1) * cols)
        if residual:
            total = (res_rows[f, here, :].astype(F32) + total).astype(BF16)
            put_share(scalars, share_ref, f, r * cols, total, share)
        else:
            total = total.astype(BF16)
            out_ref[f, here, :] = total
            s, q = column_sums(total.astype(F32))
            totals[f] = [totals[f][0] + s, totals[f][1] + q]

    blocks = []
    for f in range(frames):
        edges = list(range(0, rows + 2, block_rows)) + [rows + 2]
        blocks += [(f, edges[i], edges[i + 1]) for i in range(len(edges) - 1)]

    def act(block):
        for p in range(block[1], block[2]):
            widen(block[0], p)

    def end(block):
        for p in range(block[1], block[2]):
            if p >= 2:
                finish(block[0], p - 2)

    act(blocks[0])
    if residual:
        res_copy.wait()
    for i, block in enumerate(blocks):
        multiply(*block)
        if i + 1 < len(blocks):
            act(blocks[i + 1])
        if i > 0:
            end(blocks[i - 1])
    end(blocks[-1])
    if residual:
        for f in range(frames):
            flag = jnp.full((FLAG_ROWS, LANES), jnp.where(f < scalars[3], 1.0, 0.0), F32)
            for d in range(share_ref.shape[0]):
                share_ref[d, f, pl.ds(dense_rows(share)[0], FLAG_ROWS), :] = flag.astype(BF16)
        for d, ref in enumerate(share_refs):
            ref[...] = share_ref[d]
    else:
        for f in range(frames):
            sums = jnp.concatenate([jnp.sum(t, axis=0, keepdims=True) for t in totals[f]], axis=0)
            put_stats(f, sums, out_stats_ref, msg_ref, cols)
            edge = edge_start(cells, cols)
            msg_ref[f, pl.ds(0, cols), :] = out_ref[f, pl.ds(edge, cols), :]


def dense_rows(share):
    half = (share // 2 + 15) // 16 * 16
    return 2 * share + half, half


def put_dense(ref, where, start, x, share):
    _, half = dense_rows(share)
    count = x.shape[0]
    ref[(*where, slice(start, start + count), slice(None))] = x[:, 0:LANES]
    ref[(*where, slice(share + start, share + start + count), slice(None))] = x[:, LANES : 2 * LANES]
    rest = x.shape[1] - 2 * LANES
    side, row = (0, start) if start < half else (1, start - half)
    row += 2 * share
    ref[(*where, slice(row, row + count), slice(side * rest, (side + 1) * rest))] = x[:, 2 * LANES :]


def get_dense(ref, where, start, count, share, channels):
    _, half = dense_rows(share)
    rest = channels - 2 * LANES
    side, row = (0, start) if start < half else (1, start - half)
    row += 2 * share
    third = ref[(*where, slice(row, row + count), slice(None))]
    return jnp.concatenate(
        [
            ref[(*where, slice(start, start + count), slice(None))],
            ref[(*where, slice(share + start, share + start + count), slice(None))],
            third[:, side * rest : (side + 1) * rest],
        ],
        axis=1,
    )


def halves(share):
    _, half = dense_rows(share)
    return ((0, half), (half, share - half))


def put_share(scalars, out_ref, f, start, total, share):
    piece = math.gcd(math.gcd(share, total.shape[0]), dense_rows(share)[1])
    for p in range(0, total.shape[0], piece):
        owner, inside = divmod(start + p, share)
        put_dense(out_ref, (scalars[8 + owner], f), inside, total[p : p + piece], share)


def ends_kernel(group, scalars, *rest):
    own, (one_ref, two_ref) = rest[:group], rest[group:]
    dense = one_ref.shape[0]
    odd = scalars[5] > 0
    for d in range(group):
        for ref, upper in ((one_ref, odd), (two_ref, jnp.logical_not(odd))):

            @pl.when(jnp.logical_and(jnp.logical_not(upper), scalars[4] ^ d == group - 1))
            def _():
                live = own[d][1, pl.ds(dense, FLAG_ROWS), :].astype(F32)[0:1] > 0.5
                ref[...] = jnp.where(
                    live, own[d][1, 0:dense, :].astype(F32), own[d][0, 0:dense, :].astype(F32)
                ).astype(BF16)

            @pl.when(jnp.logical_and(upper, scalars[4] == d))
            def _():
                ref[...] = own[d][0, 0:dense, :]


def time_kernel(group, scalars, *rest):
    own, (one_ref, two_ref, w_ref, gain_ref) = rest[:group], rest[group : group + 4]
    res_two_ref, normed_ref, flag_ref, *pick_refs, ordered, moving, edge, picks = rest[group + 4 :]
    _, frames, share, channels = res_two_ref.shape
    dense = one_ref.shape[0]
    odd = scalars[5] > 0
    for d in range(group):
        ordered[scalars[8 + d]] = own[d][...]

    def lively(x):
        return silu(x.astype(F32)).astype(BF16)

    for m in range(group):
        for f in range(frames):
            moving[m, f] = lively(ordered[m, f, 0:dense, :])
    one, two = one_ref[...].astype(F32), two_ref[...].astype(F32)
    edge[0] = lively(jnp.where(odd, one, two))
    edge[1] = lively(jnp.where(odd, two, one))
    live = [ordered[m, 1, dense : dense + FLAG_ROWS, :].astype(F32)[0:1, 0:1] > 0.5 for m in range(group)]
    for m in range(group):
        for start, step in halves(share):

            def cells(ref, *where):
                return get_dense(ref, where, start, step, share, channels).astype(F32)

            here = slice(start, start + step)
            first, second = cells(moving, m, 0), cells(moving, m, 1)
            if m:
                prior = jnp.where(live[m - 1], cells(moving, m - 1, 1), cells(moving, m - 1, 0))
            else:
                prior = cells(edge, 0)
            later = cells(moving, m + 1, 0) if m + 1 < group else cells(edge, 1)
            rows = [
                arrange([prior, first, jnp.where(live[m], second, later)]),
                arrange([first, second, jnp.where(live[m], later, 0.0)]),
            ]
            mixed = jnp.dot(
                jnp.concatenate(rows, axis=0).astype(BF16), w_ref[...], preferred_element_type=F32
            )
            norms = []
            for f in range(frames):
                total = (cells(ordered, m, f) + mixed[f * step : (f + 1) * step]).astype(BF16)
                res_two_ref[m, f, here, :] = total
                v = total.astype(F32)
                v = v - jnp.mean(v, axis=1, keepdims=True)
                spread = jnp.mean(v * v, axis=1, keepdims=True)
                normed = v * lax.rsqrt(spread + EPS) * gain_ref[...]
                norms.append(normed)
                normed_ref[m, f, here, :] = normed.astype(BF16)
            picked = jnp.where(scalars[8 + group + m] > 0, norms[1], norms[0]).astype(BF16)
            put_dense(picks, (scalars[8 + 2 * group + m],), start, picked, share)
        for f in range(frames):
            flag_ref[m, f] = ordered[m, f, dense : dense + FLAG_ROWS, :].astype(F32)[0:8]
    both_ref, *part_refs = pick_refs
    both_ref[...] = picks[...]
    for i, ref in enumerate(part_refs):
        ref[...] = picks[2 * i : 2 * i + 2]


def pack_kernel(normed_ref, wq_ref, wkv_ref, packed_ref):
    group, frames, _, _ = normed_ref.shape
    wide = wq_ref.shape[1]
    for m in range(group):
        rows = jnp.concatenate([normed_ref[m, f] for f in range(frames)], axis=0)
        packed_ref[m, :, 0:wide] = jnp.dot(rows, wq_ref[...], preferred_element_type=F32).astype(BF16)
        packed_ref[m, :, wide:] = jnp.dot(rows, wkv_ref[...], preferred_element_type=F32).astype(BF16)


def head_maps(keys, channels, wide):
    column = np.arange(keys * wide)
    lane = column // wide * 8 + column % wide // HEAD_DIM
    hit = (lane[:, None] == np.arange(LANES)[None, :]) & (column % wide < channels)[:, None]
    return (hit * HEAD_DIM ** (-0.5)).astype(ml_dtypes.bfloat16), hit.T.astype(ml_dtypes.bfloat16)


def shared_kernel(buffers, contexts, base, share, scalars, *rest):
    sources, (wkv_ref, shared_ref, dense_context, context, sems) = rest[:buffers], rest[buffers:]
    channels = context.shape[1]
    for j in range(contexts):
        for b in range(buffers):

            @pl.when(scalars[base + 2 * j] == b)
            def _():
                pltpu.make_async_copy(
                    sources[b].at[scalars[base + 1 + 2 * j]], dense_context.at[j], sems.at[j]
                ).start()

    for j in range(contexts):
        pltpu.make_async_copy(sources[0].at[0], dense_context.at[j], sems.at[j]).wait()
        for start, count in halves(share):
            at = j * share + start
            context[at : at + count, :] = get_dense(dense_context, (j,), start, count, share, channels)
    half = contexts // 2 * share
    for s in (0, half):
        shared_ref[s : s + half, :] = jnp.dot(
            context[s : s + half, :], wkv_ref[...], preferred_element_type=F32
        ).astype(BF16)


def attend_kernel(contexts, who, scalars, shared, packed_ref, flag_ref, wout_ref, gather_hbm, spread_hbm, res_hbm, *rest):
    out_refs = rest[: len(who)]
    products, spreads, joined, gather_ref, spread_ref, res_ref, sems, res_sems = rest[len(who) :]
    _, frames, share, channels = res_ref.shape
    heads = channels // HEAD_DIM
    wide = wout_ref.shape[0]
    keys = frames + contexts
    gather_copy = pltpu.make_async_copy(gather_hbm, gather_ref, sems.at[0])
    spread_copy = pltpu.make_async_copy(spread_hbm, spread_ref, sems.at[1])
    gather_copy.start()
    spread_copy.start()
    at_member = [scalars[8 + d] for d in who]
    res_copies = [
        pltpu.make_async_copy(res_hbm.at[at], res_ref.at[i], res_sems.at[i]) for i, at in enumerate(at_member)
    ]
    for copy in res_copies:
        copy.start()
    lane = lax.broadcasted_iota(jnp.int32, (1, LANES), 1)
    in_use = jnp.logical_and(lane % 8 < heads, lane // 8 < keys)

    piece = 32 if share % 32 == 0 else 16

    def key_value(m, j, s, part):
        if j < frames:
            at = j * share + s
            return packed_ref[at_member[m], at : at + piece, (1 + part) * wide : (2 + part) * wide]
        at = (j - frames) * share + s
        return shared[at : at + piece, part * wide : (part + 1) * wide]

    def multiply(m):
        for s in range(0, share, piece):
            queries = [packed_ref[at_member[m], f * share + s : f * share + s + piece, 0:wide] for f in range(frames)]
            for j in range(keys):
                key = key_value(m, j, s, 0)
                for f in range(frames):
                    at = f * share + s
                    products[m, at : at + piece, j * wide : (j + 1) * wide] = queries[f] * key

    def weigh(m):
        flags = flag_ref[at_member[m]]
        visible = in_use
        for f in range(frames):
            dead = jnp.logical_and(lane // 8 == f, flags[f, 0:1] < 0.5)
            visible = jnp.logical_and(visible, jnp.logical_not(dead))
        scores = scored[m]
        scores = jnp.where(visible, scores, MASKED)
        top = scores
        for shift in (8, 16, 32, 64):
            top = jnp.maximum(top, pltpu.roll(top, shift, 1))
        raised = jnp.exp(scores - top)
        total = raised
        for shift in (8, 16, 32, 64):
            total = total + pltpu.roll(total, shift, 1)
        weights = (raised / total).astype(BF16)
        spreads[m % 2] = jnp.dot(weights, spread_ref[...], preferred_element_type=F32)

    def combine(m):
        for s in range(0, share, piece):
            results = [jnp.zeros((piece, wide), F32) for _ in range(frames)]
            for j in range(keys):
                value = key_value(m, j, s, 1).astype(F32)
                for f in range(frames):
                    at = f * share + s
                    results[f] = results[f] + spreads[m % 2, at : at + piece, j * wide : (j + 1) * wide] * value
            for f in range(frames):
                joined[f * share + s : f * share + s + piece, :] = results[f].astype(BF16)
        added = jnp.dot(joined[...], wout_ref[...], preferred_element_type=F32)
        for f in range(frames):
            live = flag_ref[at_member[m], f, 0:1, 0:1] > 0.5
            total = res_ref[m, f].astype(F32) + added[f * share : (f + 1) * share]
            total = jnp.where(live, total, 0.0).astype(BF16)
            for start, count in halves(share):
                put_dense(out_refs[m], (f,), start, total[start : start + count], share)

    count = len(who)
    for m in range(count):
        multiply(m)
    gather_copy.wait()
    scored = [jnp.dot(products[m], gather_ref[...], preferred_element_type=F32) for m in range(count)]
    spread_copy.wait()
    for copy in res_copies:
        copy.wait()
    for m in range(count):
        weigh(m)
        if m > 0:
            combine(m - 1)
    combine(count - 1)


def assemble_kernel(group, chunks, scalars, *rest):
    parts, out_ref = rest[:-1], rest[-1]
    frames, cells, channels = out_ref.shape
    share = cells // (chunks * group)
    for c in range(chunks):
        for d in range(group):
            place = (c * group + scalars[8 + d]) * share
            for f in range(frames):
                for start, count in halves(share):
                    out_ref[f, pl.ds(pl.multiple_of(place + start, 16), count), :] = get_dense(
                        parts[c * group + d], (f,), start, count, share, channels
                    )


def share_tile(stats, msg, source, cols):
    tiles = lax.axis_size("tile")
    if tiles == 2:
        got = lax.ppermute(msg, "tile", [(0, 1), (1, 0)])
        return stats, got, got
    down = [(i, i + 1) for i in range(tiles - 1)]
    up = [(i + 1, i) for i in range(tiles - 1)]
    pad = ((0, 0), (0, FLAG_ROWS), (0, 0))
    top = lax.ppermute(source[:, -cols:], "tile", down)
    bottom = lax.ppermute(source[:, :cols], "tile", up)
    return lax.psum(stats, "tile"), jnp.pad(top, pad), jnp.pad(bottom, pad)


def place_of(level, source, slot, levels):
    if levels != 4:
        hop = level - source
        return jnp.where(hop >= 0, hop, levels - 1 - hop), slot
    apart = level ^ source
    late = slot > 1
    outer = jnp.logical_or(level == 0, level == 3)
    from_outer = jnp.logical_or(source == 0, source == 3)
    whole = jnp.logical_or(apart < 2, jnp.logical_and(apart == 3, outer))
    two = jnp.where(late, jnp.where(from_outer, 5, 7), 4)
    three = jnp.where(outer, 2, jnp.where(late, 6, 3))
    buffer = jnp.where(apart < 2, apart, jnp.where(apart == 2, two, three))
    return buffer, jnp.where(jnp.logical_or(whole, jnp.logical_not(late)), slot, slot - 2)


def plan_kernel(group, frames, length, lengths_ref, context_ref, out_ref):
    contexts = context_ref.shape[0]
    levels = lax.axis_size("clip") // group
    clip = lax.axis_index("clip")
    level, member = lax.div(clip, group), lax.rem(clip, group)
    for i in range(length):
        out_ref[i] = 0
    out_ref[3] = lengths_ref[0]
    out_ref[4] = member
    out_ref[5] = lax.rem(level, 2)
    frame = [context_ref[j] for j in range(contexts)]
    owner = [lax.div(c, frames) for c in frame]
    source = [lax.div(c, group) for c in owner]

    def one(flag):
        return jnp.where(flag, 1, 0)

    for j in range(contexts):
        slot = 0
        for i in range(contexts):
            if i != j:
                slot = slot + one(jnp.logical_and(source[i] == source[j], owner[i] < owner[j]))
        buffer, place = place_of(level, source[j], slot, levels)
        out_ref[8 + 3 * group + 2 * j] = buffer
        out_ref[9 + 3 * group + 2 * j] = place
    named, second = [], []
    for m in range(group):
        mine = level * group + m
        hit, late = 0, 0
        for j in range(contexts):
            hit = jnp.maximum(hit, one(owner[j] == mine))
            late = jnp.maximum(late, one(frame[j] == mine * frames + 1))
        named.append(hit)
        second.append(late)
    before, empty = 0, sum(named)
    for m in range(group):
        out_ref[8 + m] = member ^ m
        out_ref[8 + group + m] = second[m]
        out_ref[8 + 2 * group + m] = jnp.where(named[m] > 0, before, empty)
        before, empty = before + named[m], empty + 1 - named[m]


def send(x, pairs, group):
    return lax.ppermute(x, "clip", [(a * group + i, b * group + i) for a, b in pairs for i in range(group)])


SWAP = [(0, 1), (1, 0), (2, 3), (3, 2)]


def turn_kernel(far_ref, far_high_ref, high_ref, on_ref, late_ref):
    on_ref[0:2] = far_ref[...]
    on_ref[2:4] = far_high_ref[...]
    late_ref[...] = high_ref[...]


def send_near(both, low, high, levels, group):
    if levels != 4:
        return (both,)
    return (
        send(low, [(0, 2), (2, 0), (1, 3), (3, 1)], group),
        send(high, [(0, 2), (3, 1)], group),
        send(low, [(1, 2), (2, 1)], group),
        send(both, [(0, 1), (1, 0), (2, 3), (3, 2)], group),
    )


def send_on(both, high, got, levels, group, wait):
    if levels != 4:
        lower, upper = [both], [both]
        for _ in range(levels - 1):
            lower.append(send(lower[-1], [(i, i + 1) for i in range(levels - 1)], group))
            upper.append(send(upper[-1], [(i + 1, i) for i in range(levels - 1)], group))
        return lower + upper[1:], got
    far, far_high, middle, near = got
    on, late = call(
        turn_kernel,
        [struct(both.shape), struct(high.shape)],
        [VMEM] * 3,
        [far, far_high, high],
        name="turn",
        wait=(near, middle, *wait),
    )
    outer = send(on, [(1, 0), (2, 3)], group)
    middle_late = send(late, [(1, 2), (2, 1)], group)
    far_late = send(late, [(1, 3), (2, 0)], group)
    return [both, near, outer, middle, far, far_high, middle_late, far_late], (on,)


def local(
    latents,
    lengths,
    context,
    gain_first,
    conv_first,
    gain_second,
    conv_second,
    time_weight,
    attn_gain,
    w_qkv,
    w_out,
):
    frames, rows, cols, channels = latents.shape
    cells = rows * cols
    tiles, clips = lax.axis_size("tile"), lax.axis_size("clip")
    group = 4
    chunks = 2 if rows % 2 == 0 and cells % (2 * group * 16) == 0 else 1
    levels = clips // group
    share = cells // (group * chunks)
    dense, _ = dense_rows(share)
    contexts = context.shape[0]
    total_cells = cells * tiles
    wide = (channels + LANES - 1) // LANES * LANES
    keys = frames + contexts

    length = 8 + 3 * group + 2 * contexts
    scalars = pl.pallas_call(
        functools.partial(plan_kernel, group, frames, length),
        out_shape=struct((length,), jnp.int32),
        in_specs=[SMEM] * 2,
        out_specs=SMEM,
        name="plan",
    )(lengths, context)

    x = latents.reshape(frames, cells, channels)
    message = struct((frames, cols + FLAG_ROWS, channels))
    sums = struct((frames, 8, channels), F32)
    whole = struct((frames, cells, channels))
    x_scratch = [pltpu.SemaphoreType.DMA((frames,))]
    stats, msg, near_x = call(
        functools.partial(stats_kernel, cols), [sums, message, whole], [HBM], [x], x_scratch, name="first_sums"
    )
    stats, top, bottom = share_tile(stats, msg, x, cols)
    square = struct((3 * channels, 3 * channels))
    (wide_first,) = call(
        first_weights_kernel, [square], [VMEM], [conv_first.reshape(9, channels, channels)], name="first_weights"
    )
    gather, spread = (jnp.asarray(a) for a in head_maps(keys, channels, wide))

    part = struct((frames, dense + FLAG_ROWS, LANES))

    def conv(first_row, count, residual, outs, source, stats, top, bottom, gain, weight, *more):
        scratch = [
            pltpu.VMEM((frames, (count + 2) * cols, 3 * channels), BF16),
            pltpu.VMEM((frames, (count + 2) * cols, 3 * channels), F32),
        ]
        if residual:
            scratch += [
                pltpu.VMEM((frames, count * cols, channels), BF16),
                pltpu.SemaphoreType.DMA,
                pltpu.VMEM((group, *part.shape), BF16),
            ]
        block_rows = 11 if count == 20 else 8
        return call(
            functools.partial(conv_kernel, cols, total_cells, first_row, count, residual, block_rows),
            outs,
            [VMEM] * 6 + [HBM, SMEM][: len(more)],
            [source, stats, top, bottom, gain.reshape(1, channels), weight, *more],
            scratch,
            2 * frames * (count + 2) * cols * 9 * channels * channels,
            name="conv_two" if residual else "conv_one",
            mib=26,
        )

    hidden, stats, msg = conv(0, rows, False, [whole, sums, message], near_x, stats, top, bottom, gain_first, wide_first)
    wide_second, wide_time, wide_q, wide_kv, wide_out = call(
        weights_kernel,
        [
            square,
            struct((3 * channels, channels)),
            struct((channels, wide)),
            struct((channels, 2 * wide)),
            struct((wide, channels)),
        ],
        [VMEM] * 4,
        [conv_second.reshape(9, channels, channels), time_weight, w_qkv, w_out],
        name="weights",
        wait=(stats,),
    )
    stats, top, bottom = share_tile(stats, msg, hidden, cols)
    swaps = [[(i, i ^ d) for i in range(clips)] for d in range(group)]
    pairs = [[(i, i + 1) for i in range(a, levels - 1, 2)] for a in range(2)]
    beside = [
        [(u * group + i, v * group + i) for a, b in p for u, v in ((a, b), (b, a)) for i in range(group)] for p in pairs
    ]

    shares_of = []
    for c in range(chunks):
        shares = conv(
            c * rows // chunks,
            rows // chunks,
            True,
            [part] * group,
            hidden,
            stats,
            top,
            bottom,
            gain_second,
            wide_second,
            x,
            scalars,
        )
        shares_of.append(shares)

    def mix(own, *before):
        end = struct((dense, LANES))
        one, two = call(
            functools.partial(ends_kernel, group), [end, end], [SMEM] + [VMEM] * group, [scalars, *own], name="ends",
            wait=shares_of[-1][:1],
        )
        one = lax.ppermute(one, "clip", beside[0])
        two = lax.ppermute(two, "clip", beside[1])
        both = (group, frames, share, channels)
        res_two, normed, flags, *picked = call(
            functools.partial(time_kernel, group),
            [struct(both), struct(both), struct((group, frames, 8, LANES), F32), struct((group, dense, LANES))] + [struct((2, dense, LANES))] * (group // 2),
            [SMEM] + [VMEM] * (group + 4),
            [scalars, *own, one, two, wide_time, attn_gain.reshape(1, channels)],
            [
                pltpu.VMEM((group, frames, dense + FLAG_ROWS, LANES), BF16),
                pltpu.VMEM((group, frames, dense, LANES), BF16),
                pltpu.VMEM((2, dense, LANES), BF16),
                pltpu.VMEM((group, dense, LANES), BF16),
            ],
            2 * frames * group * share * 3 * channels * channels,
            name="time_mix",
            wait=before,
        )
        return res_two, normed, flags, *picked

    def exchange(shares):
        return [shares[0]] + [lax.ppermute(shares[d], "clip", swaps[d]) for d in range(1, group)]

    def shared_kv(sources):
        (shared,) = call(
            functools.partial(shared_kernel, len(sources), contexts, 8 + 3 * group, share),
            [struct((contexts * share, 2 * wide))],
            [SMEM] + [HBM] * len(sources) + [VMEM],
            [scalars, *sources, wide_kv],
            [
                pltpu.VMEM((contexts, dense, LANES), BF16),
                pltpu.VMEM((contexts * share, channels), BF16),
                pltpu.SemaphoreType.DMA((contexts,)),
            ],
            name="shared",
        )
        return shared

    def pack(normed):
        (packed,) = call(
            pack_kernel,
            [struct((group, frames * share, 3 * wide))],
            [VMEM] * 3,
            [normed, wide_q, wide_kv],
            name="pack",
        )
        return packed

    def attention(res_two, flags, packed, shared, who, wait=()):
        return call(
            functools.partial(attend_kernel, contexts, who),
            [struct((frames, dense, LANES))] * len(who),
            [SMEM] + [VMEM] * 4 + [HBM] * 3,
            [scalars, shared, packed, flags, wide_out, gather, spread, res_two],
            [
                pltpu.VMEM((len(who), frames * share, keys * wide), BF16),
                pltpu.VMEM((2, frames * share, keys * wide), F32),
                pltpu.VMEM((frames * share, wide), BF16),
                pltpu.VMEM((keys * wide, LANES), BF16),
                pltpu.VMEM((LANES, keys * wide), BF16),
                pltpu.VMEM((len(who), frames, share, channels), BF16),
                pltpu.SemaphoreType.DMA((2,)),
                pltpu.SemaphoreType.DMA((len(who),)),
            ],
            name="attend",
            mib=26,
            wait=wait,
        )

    def give_back(who, outs):
        return [lax.ppermute(out, "clip", swaps[d]) if d else out for d, out in zip(who, outs, strict=True)]

    def across(normed, both, low, high, wait=()):
        got = send_near(both, low, high, levels, group)
        packed = pack(normed)
        return packed, *send_on(both, high, got, levels, group, (packed, *wait))

    own = exchange(shares_of[0])
    later = [exchange(shares) for shares in shares_of[1:]]
    res_two, normed, flags, *picked = mix(own)
    packed, buffers, turned = across(normed, *picked)
    parts = []
    for own in later:
        shared = shared_kv(buffers)
        next_res_two, normed, next_flags, *picked = mix(own, *turned)
        next_packed, buffers, turned = across(normed, *picked, (shared,))
        outs = attention(res_two, flags, packed, shared, range(group), turned)
        parts += give_back(range(group), outs)
        res_two, flags, packed = next_res_two, next_flags, next_packed
    shared = shared_kv(buffers)
    most = attention(res_two, flags, packed, shared, (1, 2, 3))
    parts += attention(res_two, flags, packed, shared, (0,), most[:1])
    parts += give_back((1, 2, 3), most)
    (result,) = call(
        functools.partial(assemble_kernel, group, chunks),
        [whole],
        [SMEM] + [VMEM] * len(parts),
        [scalars, *parts],
        name="assemble",
    )
    return result.reshape(frames, rows, cols, channels)


def solution(mesh):
    placed = (P("clip", "tile", None, None), P("clip"), P(), P(), P(), P(), P(), P(), P(), P(), P())
    return jax.shard_map(
        local, mesh=mesh, in_specs=placed, out_specs=P("clip", "tile", None, None), check_vma=False
    )
```

```python
import functools
import math

import jax
import jax.numpy as jnp
import ml_dtypes
import numpy as np
from jax import lax
from jax.experimental import pallas as pl
from jax.experimental.pallas import tpu as pltpu
from jax.sharding import PartitionSpec as P

HEAD_DIM = 64
GROUPS = 32
H = 40
W = 64
EPS = 1e-05
MASKED = -1e30
LANES = 128
FLAG_ROWS = 16
F32 = jnp.float32
BF16 = jnp.bfloat16

SMEM = pl.BlockSpec(memory_space=pltpu.SMEM)
VMEM = pl.BlockSpec(memory_space=pltpu.VMEM)
ANY = pl.BlockSpec(memory_space=pl.ANY)
HBM = pl.BlockSpec(memory_space=pltpu.HBM)


def call(kernel, out_shape, in_specs, args, scratch=(), flops=0, name=None, mib=8, wait=()):
    count = len(args)

    def body(*refs):
        kernel(*refs[:count], *refs[count + len(wait) :])

    return pl.pallas_call(
        body,
        out_shape=out_shape,
        in_specs=[*in_specs, *[ANY] * len(wait)],
        out_specs=[VMEM] * len(out_shape),
        scratch_shapes=list(scratch),
        compiler_params=pltpu.CompilerParams(vmem_limit_bytes=mib * 1024 * 1024),
        cost_estimate=pl.CostEstimate(flops=1, bytes_accessed=1, transcendentals=0),
        name=name,
    )(*args, *wait)


def struct(shape, dtype=BF16):
    return jax.ShapeDtypeStruct(shape, dtype)


def silu(x):
    return 0.5 * x * (1.0 + jnp.tanh(0.5 * x))


def column_sums(v):
    folded = v.reshape(v.shape[0] // 8, 8, v.shape[1])
    return jnp.sum(folded, axis=0), jnp.sum(folded * folded, axis=0)


def split3(x):
    high = x.astype(BF16)
    rest = x - high.astype(F32)
    mid = rest.astype(BF16)
    return high, mid, (rest - mid.astype(F32)).astype(BF16)


def put_stats(f, sums, stats_ref, msg_ref, cols):
    channels = sums.shape[1]
    stats_ref[f] = jnp.concatenate([sums, jnp.zeros((6, channels), F32)], axis=0)
    high, mid, low = split3(sums)
    parts = [high, mid, low, jnp.zeros((FLAG_ROWS - 6, channels), BF16)]
    packed = jnp.concatenate([p.astype(F32) for p in parts], axis=0)
    msg_ref[f, pl.ds(cols, FLAG_ROWS), :] = packed.astype(BF16)


def edge_start(cells, cols):
    return pl.multiple_of(jnp.where(lax.axis_index("tile") == 0, cells - cols, 0), cols)


def stats_kernel(cols, x_ref, stats_ref, msg_ref):
    frames, cells, channels = x_ref.shape
    step = 2 * cols if cells % (2 * cols) == 0 else cols
    for f in range(frames):

        def body(i, carry):
            v = x_ref[f, pl.ds(pl.multiple_of(i * step, step), step), :].astype(F32)
            s, q = column_sums(v)
            return carry[0] + s, carry[1] + q

        zero = jnp.zeros((8, channels), F32)
        s, q = lax.fori_loop(0, cells // step, body, (zero, zero))
        sums = jnp.concatenate(
            [jnp.sum(s, axis=0, keepdims=True), jnp.sum(q, axis=0, keepdims=True)], axis=0
        )
        put_stats(f, sums, stats_ref, msg_ref, cols)
        edge = edge_start(cells, cols)
        msg_ref[f, pl.ds(0, cols), :] = x_ref[f, pl.ds(edge, cols), :]


def arrange(pieces):
    big = pieces[0].shape[1] // 256 * 256
    return jnp.concatenate([p[:, :big] for p in pieces] + [p[:, big:] for p in pieces], axis=1)


def spans(index, channels):
    big = channels // 256 * 256
    return ((index * big, big, 0), (3 * big + index * (channels - big), channels - big, big))


def lay_conv(source, target):
    channels = source.shape[1]
    for a in range(3):
        for b in range(3):
            for row, height, from_row in spans(b, channels):
                for col, width, from_col in spans(a, channels):
                    target[row : row + height, col : col + width] = source[
                        3 * a + b, from_row : from_row + height, from_col : from_col + width
                    ]


def first_weights_kernel(first_ref, wide_first):
    lay_conv(first_ref, wide_first)


def weights_kernel(second_ref, time_ref, qkv_ref, out_ref, wide_second, wide_time, wide_q, wide_kv, wide_out):
    channels = out_ref.shape[0]
    lay_conv(second_ref, wide_second)
    for b in range(3):
        for row, height, from_row in spans(b, channels):
            wide_time[row : row + height, :] = time_ref[b, from_row : from_row + height, :]
    wide = wide_out.shape[0]
    wide_q[...] = jnp.zeros_like(wide_q)
    wide_kv[...] = jnp.zeros_like(wide_kv)
    wide_q[:, 0:channels] = qkv_ref[:, 0:channels]
    for part in range(2):
        wide_kv[:, part * wide : part * wide + channels] = qkv_ref[:, (part + 1) * channels : (part + 2) * channels]
    wide_out[...] = jnp.zeros_like(wide_out)
    wide_out[0:channels, :] = out_ref[...]


def conv_kernel(cols, total_cells, first_row, rows, residual, block_rows, x_ref, stats_ref, top_ref, bottom_ref, gain_ref, w_ref, *rest):
    if residual:
        res_in_ref, scalars, *share_refs, wide_x, wide_y, res_rows, res_sem, share_ref = rest
        here = pl.ds(first_row * cols, rows * cols)
        res_copy = pltpu.make_async_copy(res_in_ref.at[:, here], res_rows, res_sem)
        res_copy.start()
        share = cols * rows // share_ref.shape[0]
    else:
        out_ref, out_stats_ref, msg_ref, wide_x, wide_y = rest
    frames, cells, channels = x_ref.shape
    tile_rows = cells // cols
    big = channels // 256 * 256
    small = channels - big
    group_width = channels // GROUPS
    row_group = lax.broadcasted_iota(jnp.int32, (channels, channels), 0) // group_width
    col_group = lax.broadcasted_iota(jnp.int32, (channels, channels), 1) // group_width
    same = (row_group == col_group).astype(F32)
    column = lax.broadcasted_iota(jnp.int32, (cols, 1), 0)
    leftmost, rightmost = column == 0, column == cols - 1

    scales = []
    for f in range(frames):
        other = top_ref[f, pl.ds(cols, FLAG_ROWS), :].astype(F32)
        sums = stats_ref[f, 0:2, :] + other[0:2] + other[2:4] + other[4:6]
        sums = jnp.concatenate([sums, jnp.zeros((6, channels), F32)], axis=0)
        means = jnp.dot(
            sums, same, preferred_element_type=F32, precision=lax.Precision.HIGHEST
        ) / (total_cells * group_width)
        centre = means[0:1]
        scale = lax.rsqrt(means[1:2] - centre * centre + EPS) * gain_ref[...]
        scales.append((scale, -centre * scale))

    def widen(f, padded_row):
        row = first_row + padded_row - 1
        if row < 0:
            raw, keep = top_ref[f, 0:cols, :], lax.axis_index("tile") > 0
        elif row >= tile_rows:
            raw, keep = bottom_ref[f, 0:cols, :], lax.axis_index("tile") < lax.axis_size("tile") - 1
        else:
            raw, keep = x_ref[f, row * cols : (row + 1) * cols, :], None
        scale, shift = scales[f]
        y = silu(raw.astype(F32) * scale + shift)
        if keep is not None:
            y = jnp.where(keep, y, 0.0)
        left = jnp.where(leftmost, 0.0, pltpu.roll(y, 1, 0))
        right = jnp.where(rightmost, 0.0, pltpu.roll(y, cols - 1, 0))
        wide_x[f, padded_row * cols : (padded_row + 1) * cols, :] = arrange([left, y, right]).astype(BF16)

    def multiply(f, start, stop):
        here = slice(start * cols, stop * cols)
        wide_y[f, here, :] = jnp.dot(wide_x[f, here, :], w_ref[...], preferred_element_type=F32)

    totals = [[jnp.zeros((8, channels), F32)] * 2 for _ in range(frames)]

    def finish(f, r):
        parts = []
        for base, width in ((0, big), (3 * big, small)):
            parts.append(
                wide_y[f, r * cols : (r + 1) * cols, base : base + width]
                + wide_y[f, (r + 1) * cols : (r + 2) * cols, base + width : base + 2 * width]
                + wide_y[f, (r + 2) * cols : (r + 3) * cols, base + 2 * width : base + 3 * width]
            )
        total = jnp.concatenate(parts, axis=1)
        here = slice(r * cols, (r + 1) * cols)
        if residual:
            total = (res_rows[f, here, :].astype(F32) + total).astype(BF16)
            put_share(scalars, share_ref, f, r * cols, total, share)
        else:
            total = total.astype(BF16)
            out_ref[f, here, :] = total
            s, q = column_sums(total.astype(F32))
            totals[f] = [totals[f][0] + s, totals[f][1] + q]

    blocks = []
    for f in range(frames):
        edges = list(range(0, rows + 2, block_rows)) + [rows + 2]
        blocks += [(f, edges[i], edges[i + 1]) for i in range(len(edges) - 1)]

    def act(block):
        for p in range(block[1], block[2]):
            widen(block[0], p)

    def end(block):
        for p in range(block[1], block[2]):
            if p >= 2:
                finish(block[0], p - 2)

    act(blocks[0])
    if residual:
        res_copy.wait()
    for i, block in enumerate(blocks):
        multiply(*block)
        if i + 1 < len(blocks):
            act(blocks[i + 1])
        if i > 0:
            end(blocks[i - 1])
    end(blocks[-1])
    if residual:
        for f in range(frames):
            flag = jnp.full((FLAG_ROWS, LANES), jnp.where(f < scalars[3], 1.0, 0.0), F32)
            for d in range(share_ref.shape[0]):
                share_ref[d, f, pl.ds(dense_rows(share)[0], FLAG_ROWS), :] = flag.astype(BF16)
        for d, ref in enumerate(share_refs):
            ref[...] = share_ref[d]
    else:
        for f in range(frames):
            sums = jnp.concatenate([jnp.sum(t, axis=0, keepdims=True) for t in totals[f]], axis=0)
            put_stats(f, sums, out_stats_ref, msg_ref, cols)
            edge = edge_start(cells, cols)
            msg_ref[f, pl.ds(0, cols), :] = out_ref[f, pl.ds(edge, cols), :]


def dense_rows(share):
    half = (share // 2 + 15) // 16 * 16
    return 2 * share + half, half


def put_dense(ref, where, start, x, share):
    _, half = dense_rows(share)
    count = x.shape[0]
    ref[(*where, slice(start, start + count), slice(None))] = x[:, 0:LANES]
    ref[(*where, slice(share + start, share + start + count), slice(None))] = x[:, LANES : 2 * LANES]
    rest = x.shape[1] - 2 * LANES
    side, row = (0, start) if start < half else (1, start - half)
    row += 2 * share
    ref[(*where, slice(row, row + count), slice(side * rest, (side + 1) * rest))] = x[:, 2 * LANES :]


def get_dense(ref, where, start, count, share, channels):
    _, half = dense_rows(share)
    rest = channels - 2 * LANES
    side, row = (0, start) if start < half else (1, start - half)
    row += 2 * share
    third = ref[(*where, slice(row, row + count), slice(None))]
    return jnp.concatenate(
        [
            ref[(*where, slice(start, start + count), slice(None))],
            ref[(*where, slice(share + start, share + start + count), slice(None))],
            third[:, side * rest : (side + 1) * rest],
        ],
        axis=1,
    )


def halves(share):
    _, half = dense_rows(share)
    return ((0, half), (half, share - half))


def put_share(scalars, out_ref, f, start, total, share):
    piece = math.gcd(math.gcd(share, total.shape[0]), dense_rows(share)[1])
    for p in range(0, total.shape[0], piece):
        owner, inside = divmod(start + p, share)
        put_dense(out_ref, (scalars[8 + owner], f), inside, total[p : p + piece], share)


def ends_kernel(group, scalars, *rest):
    own, (one_ref, two_ref) = rest[:group], rest[group:]
    dense = one_ref.shape[0]
    odd = scalars[5] > 0
    for d in range(group):
        for ref, upper in ((one_ref, odd), (two_ref, jnp.logical_not(odd))):

            @pl.when(jnp.logical_and(jnp.logical_not(upper), scalars[4] ^ d == group - 1))
            def _():
                live = own[d][1, pl.ds(dense, FLAG_ROWS), :].astype(F32)[0:1] > 0.5
                ref[...] = jnp.where(
                    live, own[d][1, 0:dense, :].astype(F32), own[d][0, 0:dense, :].astype(F32)
                ).astype(BF16)

            @pl.when(jnp.logical_and(upper, scalars[4] == d))
            def _():
                ref[...] = own[d][0, 0:dense, :]


def time_kernel(group, scalars, *rest):
    own, (one_ref, two_ref, w_ref, gain_ref) = rest[:group], rest[group : group + 4]
    res_two_ref, normed_ref, flag_ref, *pick_refs, ordered, moving, edge, picks = rest[group + 4 :]
    _, frames, share, channels = res_two_ref.shape
    dense = one_ref.shape[0]
    odd = scalars[5] > 0
    for d in range(group):
        ordered[scalars[8 + d]] = own[d][...]

    def lively(x):
        return silu(x.astype(F32)).astype(BF16)

    for m in range(group):
        for f in range(frames):
            moving[m, f] = lively(ordered[m, f, 0:dense, :])
    one, two = one_ref[...].astype(F32), two_ref[...].astype(F32)
    edge[0] = lively(jnp.where(odd, one, two))
    edge[1] = lively(jnp.where(odd, two, one))
    live = [ordered[m, 1, dense : dense + FLAG_ROWS, :].astype(F32)[0:1, 0:1] > 0.5 for m in range(group)]
    for m in range(group):
        for start, step in halves(share):

            def cells(ref, *where):
                return get_dense(ref, where, start, step, share, channels).astype(F32)

            here = slice(start, start + step)
            first, second = cells(moving, m, 0), cells(moving, m, 1)
            if m:
                prior = jnp.where(live[m - 1], cells(moving, m - 1, 1), cells(moving, m - 1, 0))
            else:
                prior = cells(edge, 0)
            later = cells(moving, m + 1, 0) if m + 1 < group else cells(edge, 1)
            rows = [
                arrange([prior, first, jnp.where(live[m], second, later)]),
                arrange([first, second, jnp.where(live[m], later, 0.0)]),
            ]
            mixed = jnp.dot(
                jnp.concatenate(rows, axis=0).astype(BF16), w_ref[...], preferred_element_type=F32
            )
            norms = []
            for f in range(frames):
                total = (cells(ordered, m, f) + mixed[f * step : (f + 1) * step]).astype(BF16)
                res_two_ref[m, f, here, :] = total
                v = total.astype(F32)
                v = v - jnp.mean(v, axis=1, keepdims=True)
                spread = jnp.mean(v * v, axis=1, keepdims=True)
                normed = v * lax.rsqrt(spread + EPS) * gain_ref[...]
                norms.append(normed)
                normed_ref[m, f, here, :] = normed.astype(BF16)
            picked = jnp.where(scalars[8 + group + m] > 0, norms[1], norms[0]).astype(BF16)
            put_dense(picks, (scalars[8 + 2 * group + m],), start, picked, share)
        for f in range(frames):
            flag_ref[m, f] = ordered[m, f, dense : dense + FLAG_ROWS, :].astype(F32)[0:8]
    both_ref, *part_refs = pick_refs
    both_ref[...] = picks[...]
    for i, ref in enumerate(part_refs):
        ref[...] = picks[2 * i : 2 * i + 2]


def pack_kernel(normed_ref, wq_ref, wkv_ref, packed_ref):
    group, frames, _, _ = normed_ref.shape
    wide = wq_ref.shape[1]
    for m in range(group):
        rows = jnp.concatenate([normed_ref[m, f] for f in range(frames)], axis=0)
        packed_ref[m, :, 0:wide] = jnp.dot(rows, wq_ref[...], preferred_element_type=F32).astype(BF16)
        packed_ref[m, :, wide:] = jnp.dot(rows, wkv_ref[...], preferred_element_type=F32).astype(BF16)


def head_maps(keys, channels, wide):
    column = np.arange(keys * wide)
    lane = column // wide * 8 + column % wide // HEAD_DIM
    hit = (lane[:, None] == np.arange(LANES)[None, :]) & (column % wide < channels)[:, None]
    return (hit * HEAD_DIM ** (-0.5)).astype(ml_dtypes.bfloat16), hit.T.astype(ml_dtypes.bfloat16)


def shared_kernel(buffers, contexts, base, share, scalars, *rest):
    sources, (wkv_ref, shared_ref, dense_context, context, sems) = rest[:buffers], rest[buffers:]
    channels = context.shape[1]
    for j in range(contexts):
        for b in range(buffers):

            @pl.when(scalars[base + 2 * j] == b)
            def _():
                pltpu.make_async_copy(
                    sources[b].at[scalars[base + 1 + 2 * j]], dense_context.at[j], sems.at[j]
                ).start()

    for j in range(contexts):
        pltpu.make_async_copy(sources[0].at[0], dense_context.at[j], sems.at[j]).wait()
        for start, count in halves(share):
            at = j * share + start
            context[at : at + count, :] = get_dense(dense_context, (j,), start, count, share, channels)
    half = contexts // 2 * share
    for s in (0, half):
        shared_ref[s : s + half, :] = jnp.dot(
            context[s : s + half, :], wkv_ref[...], preferred_element_type=F32
        ).astype(BF16)


def attend_kernel(contexts, who, scalars, shared, packed_ref, flag_ref, wout_ref, gather_ref, spread_ref, res_hbm, *rest):
    out_refs = rest[: len(who)]
    products, spreads, joined, res_ref, res_sems = rest[len(who) :]
    _, frames, share, channels = res_ref.shape
    heads = channels // HEAD_DIM
    wide = wout_ref.shape[0]
    keys = frames + contexts
    at_member = [scalars[8 + d] for d in who]
    res_copies = [
        pltpu.make_async_copy(res_hbm.at[at], res_ref.at[i], res_sems.at[i]) for i, at in enumerate(at_member)
    ]
    for copy in res_copies:
        copy.start()
    lane = lax.broadcasted_iota(jnp.int32, (1, LANES), 1)
    in_use = jnp.logical_and(lane % 8 < heads, lane // 8 < keys)

    piece = 32 if share % 32 == 0 else 16

    def key_value(m, j, s, part):
        if j < frames:
            at = j * share + s
            return packed_ref[at_member[m], at : at + piece, (1 + part) * wide : (2 + part) * wide]
        at = (j - frames) * share + s
        return shared[at : at + piece, part * wide : (part + 1) * wide]

    def multiply(m):
        for s in range(0, share, piece):
            queries = [packed_ref[at_member[m], f * share + s : f * share + s + piece, 0:wide] for f in range(frames)]
            for j in range(keys):
                key = key_value(m, j, s, 0)
                for f in range(frames):
                    at = f * share + s
                    products[m, at : at + piece, j * wide : (j + 1) * wide] = queries[f] * key

    def weigh(m):
        flags = flag_ref[at_member[m]]
        visible = in_use
        for f in range(frames):
            dead = jnp.logical_and(lane // 8 == f, flags[f, 0:1] < 0.5)
            visible = jnp.logical_and(visible, jnp.logical_not(dead))
        scores = scored[m]
        scores = jnp.where(visible, scores, MASKED)
        top = scores
        for shift in (8, 16, 32, 64):
            top = jnp.maximum(top, pltpu.roll(top, shift, 1))
        raised = jnp.exp(scores - top)
        total = raised
        for shift in (8, 16, 32, 64):
            total = total + pltpu.roll(total, shift, 1)
        weights = (raised / total).astype(BF16)
        spreads[m % 2] = jnp.dot(weights, spread_ref[...], preferred_element_type=F32)

    def combine(m):
        for s in range(0, share, piece):
            results = [jnp.zeros((piece, wide), F32) for _ in range(frames)]
            for j in range(keys):
                value = key_value(m, j, s, 1).astype(F32)
                for f in range(frames):
                    at = f * share + s
                    results[f] = results[f] + spreads[m % 2, at : at + piece, j * wide : (j + 1) * wide] * value
            for f in range(frames):
                joined[f * share + s : f * share + s + piece, :] = results[f].astype(BF16)
        added = jnp.dot(joined[...], wout_ref[...], preferred_element_type=F32)
        for f in range(frames):
            live = flag_ref[at_member[m], f, 0:1, 0:1] > 0.5
            total = res_ref[m, f].astype(F32) + added[f * share : (f + 1) * share]
            total = jnp.where(live, total, 0.0).astype(BF16)
            for start, count in halves(share):
                put_dense(out_refs[m], (f,), start, total[start : start + count], share)

    count = len(who)
    for m in range(count):
        multiply(m)
    rows = frames * share if count > 3 or frames * share % 64 else frames * share // 4
    scored = [
        jnp.concatenate(
            [
                jnp.dot(products[m, at : at + rows], gather_ref[...], preferred_element_type=F32)
                for at in range(0, frames * share, rows)
            ],
            axis=0,
        )
        for m in range(count)
    ]
    for copy in res_copies:
        copy.wait()
    for m in range(count):
        weigh(m)
        if m > 0:
            combine(m - 1)
    combine(count - 1)


def assemble_kernel(group, chunks, scalars, *rest):
    parts, out_ref = rest[:-1], rest[-1]
    frames, cells, channels = out_ref.shape
    share = cells // (chunks * group)
    for c in range(chunks):
        for d in range(group):
            place = (c * group + scalars[8 + d]) * share
            for f in range(frames):
                for start, count in halves(share):
                    out_ref[f, pl.ds(pl.multiple_of(place + start, 16), count), :] = get_dense(
                        parts[c * group + d], (f,), start, count, share, channels
                    )


def share_tile(stats, msg, source, cols):
    tiles = lax.axis_size("tile")
    if tiles == 2:
        got = lax.ppermute(msg, "tile", [(0, 1), (1, 0)])
        return stats, got, got
    down = [(i, i + 1) for i in range(tiles - 1)]
    up = [(i + 1, i) for i in range(tiles - 1)]
    pad = ((0, 0), (0, FLAG_ROWS), (0, 0))
    top = lax.ppermute(source[:, -cols:], "tile", down)
    bottom = lax.ppermute(source[:, :cols], "tile", up)
    return lax.psum(stats, "tile"), jnp.pad(top, pad), jnp.pad(bottom, pad)


def place_of(level, source, slot, levels):
    if levels != 4:
        hop = level - source
        return jnp.where(hop >= 0, hop, levels - 1 - hop), slot
    apart = level ^ source
    late = slot > 1
    outer = jnp.logical_or(level == 0, level == 3)
    from_outer = jnp.logical_or(source == 0, source == 3)
    whole = jnp.logical_or(apart < 2, jnp.logical_and(apart == 3, outer))
    two = jnp.where(late, jnp.where(from_outer, 5, 7), 4)
    three = jnp.where(outer, 2, jnp.where(late, 6, 3))
    buffer = jnp.where(apart < 2, apart, jnp.where(apart == 2, two, three))
    return buffer, jnp.where(jnp.logical_or(whole, jnp.logical_not(late)), slot, slot - 2)


def plan_kernel(group, frames, length, lengths_ref, context_ref, out_ref):
    contexts = context_ref.shape[0]
    levels = lax.axis_size("clip") // group
    clip = lax.axis_index("clip")
    level, member = lax.div(clip, group), lax.rem(clip, group)
    for i in range(length):
        out_ref[i] = 0
    out_ref[3] = lengths_ref[0]
    out_ref[4] = member
    out_ref[5] = lax.rem(level, 2)
    frame = [context_ref[j] for j in range(contexts)]
    owner = [lax.div(c, frames) for c in frame]
    source = [lax.div(c, group) for c in owner]

    def one(flag):
        return jnp.where(flag, 1, 0)

    for j in range(contexts):
        slot = 0
        for i in range(contexts):
            if i != j:
                slot = slot + one(jnp.logical_and(source[i] == source[j], owner[i] < owner[j]))
        buffer, place = place_of(level, source[j], slot, levels)
        out_ref[8 + 3 * group + 2 * j] = buffer
        out_ref[9 + 3 * group + 2 * j] = place
    named, second = [], []
    for m in range(group):
        mine = level * group + m
        hit, late = 0, 0
        for j in range(contexts):
            hit = jnp.maximum(hit, one(owner[j] == mine))
            late = jnp.maximum(late, one(frame[j] == mine * frames + 1))
        named.append(hit)
        second.append(late)
    before, empty = 0, sum(named)
    for m in range(group):
        out_ref[8 + m] = member ^ m
        out_ref[8 + group + m] = second[m]
        out_ref[8 + 2 * group + m] = jnp.where(named[m] > 0, before, empty)
        before, empty = before + named[m], empty + 1 - named[m]


def send(x, pairs, group):
    return lax.ppermute(x, "clip", [(a * group + i, b * group + i) for a, b in pairs for i in range(group)])


SWAP = [(0, 1), (1, 0), (2, 3), (3, 2)]


def turn_kernel(far_ref, far_high_ref, high_ref, on_ref, late_ref):
    on_ref[0:2] = far_ref[...]
    on_ref[2:4] = far_high_ref[...]
    late_ref[...] = high_ref[...]


def send_near(both, low, high, levels, group):
    if levels != 4:
        return (both,)
    return (
        send(low, [(0, 2), (2, 0), (1, 3), (3, 1)], group),
        send(high, [(0, 2), (3, 1)], group),
        send(low, [(1, 2), (2, 1)], group),
        send(both, [(0, 1), (1, 0), (2, 3), (3, 2)], group),
    )


def send_on(both, high, got, levels, group, wait):
    if levels != 4:
        lower, upper = [both], [both]
        for _ in range(levels - 1):
            lower.append(send(lower[-1], [(i, i + 1) for i in range(levels - 1)], group))
            upper.append(send(upper[-1], [(i + 1, i) for i in range(levels - 1)], group))
        return lower + upper[1:], got
    far, far_high, middle, near = got
    on, late = call(
        turn_kernel,
        [struct(both.shape), struct(high.shape)],
        [VMEM] * 3,
        [far, far_high, high],
        name="turn",
        wait=(near, middle, *wait),
    )
    outer = send(on, [(1, 0), (2, 3)], group)
    middle_late = send(late, [(1, 2), (2, 1)], group)
    far_late = send(late, [(1, 3), (2, 0)], group)
    return [both, near, outer, middle, far, far_high, middle_late, far_late], (on,)


def local(
    latents,
    lengths,
    context,
    gain_first,
    conv_first,
    gain_second,
    conv_second,
    time_weight,
    attn_gain,
    w_qkv,
    w_out,
):
    frames, rows, cols, channels = latents.shape
    cells = rows * cols
    tiles, clips = lax.axis_size("tile"), lax.axis_size("clip")
    group = 4
    chunks = 2 if rows % 2 == 0 and cells % (2 * group * 16) == 0 else 1
    levels = clips // group
    share = cells // (group * chunks)
    dense, _ = dense_rows(share)
    contexts = context.shape[0]
    total_cells = cells * tiles
    wide = (channels + LANES - 1) // LANES * LANES
    keys = frames + contexts

    length = 8 + 3 * group + 2 * contexts
    scalars = pl.pallas_call(
        functools.partial(plan_kernel, group, frames, length),
        out_shape=struct((length,), jnp.int32),
        in_specs=[SMEM] * 2,
        out_specs=SMEM,
        name="plan",
    )(lengths, context)

    x = latents.reshape(frames, cells, channels)
    message = struct((frames, cols + FLAG_ROWS, channels))
    sums = struct((frames, 8, channels), F32)
    whole = struct((frames, cells, channels))
    stats, msg = call(
        functools.partial(stats_kernel, cols), [sums, message], [VMEM], [x], name="first_sums"
    )
    stats, top, bottom = share_tile(stats, msg, x, cols)
    square = struct((3 * channels, 3 * channels))
    (wide_first,) = call(
        first_weights_kernel, [square], [VMEM], [conv_first.reshape(9, channels, channels)], name="first_weights"
    )
    gather, spread = (jnp.asarray(a) for a in head_maps(keys, channels, wide))

    part = struct((frames, dense + FLAG_ROWS, LANES))

    def conv(first_row, count, residual, outs, source, stats, top, bottom, gain, weight, *more):
        scratch = [
            pltpu.VMEM((frames, (count + 2) * cols, 3 * channels), BF16),
            pltpu.VMEM((frames, (count + 2) * cols, 3 * channels), F32),
        ]
        if residual:
            scratch += [
                pltpu.VMEM((frames, count * cols, channels), BF16),
                pltpu.SemaphoreType.DMA,
                pltpu.VMEM((group, *part.shape), BF16),
            ]
        block_rows = 11 if count == 20 else 8
        return call(
            functools.partial(conv_kernel, cols, total_cells, first_row, count, residual, block_rows),
            outs,
            [VMEM] * 6 + [HBM, SMEM][: len(more)],
            [source, stats, top, bottom, gain.reshape(1, channels), weight, *more],
            scratch,
            2 * frames * (count + 2) * cols * 9 * channels * channels,
            name="conv_two" if residual else "conv_one",
            mib=26,
        )

    hidden, stats, msg = conv(0, rows, False, [whole, sums, message], x, stats, top, bottom, gain_first, wide_first)
    wide_second, wide_time, wide_q, wide_kv, wide_out = call(
        weights_kernel,
        [
            square,
            struct((3 * channels, channels)),
            struct((channels, wide)),
            struct((channels, 2 * wide)),
            struct((wide, channels)),
        ],
        [VMEM] * 4,
        [conv_second.reshape(9, channels, channels), time_weight, w_qkv, w_out],
        name="weights",
        wait=(stats,),
    )
    stats, top, bottom = share_tile(stats, msg, hidden, cols)
    swaps = [[(i, i ^ d) for i in range(clips)] for d in range(group)]
    pairs = [[(i, i + 1) for i in range(a, levels - 1, 2)] for a in range(2)]
    beside = [
        [(u * group + i, v * group + i) for a, b in p for u, v in ((a, b), (b, a)) for i in range(group)] for p in pairs
    ]

    shares_of = []
    for c in range(chunks):
        shares = conv(
            c * rows // chunks,
            rows // chunks,
            True,
            [part] * group,
            hidden,
            stats,
            top,
            bottom,
            gain_second,
            wide_second,
            x,
            scalars,
        )
        shares_of.append(shares)

    def mix(own, *before):
        end = struct((dense, LANES))
        one, two = call(
            functools.partial(ends_kernel, group), [end, end], [SMEM] + [VMEM] * group, [scalars, *own], name="ends",
            wait=shares_of[-1][:1],
        )
        one = lax.ppermute(one, "clip", beside[0])
        two = lax.ppermute(two, "clip", beside[1])
        both = (group, frames, share, channels)
        res_two, normed, flags, *picked = call(
            functools.partial(time_kernel, group),
            [struct(both), struct(both), struct((group, frames, 8, LANES), F32), struct((group, dense, LANES))] + [struct((2, dense, LANES))] * (group // 2),
            [SMEM] + [VMEM] * (group + 4),
            [scalars, *own, one, two, wide_time, attn_gain.reshape(1, channels)],
            [
                pltpu.VMEM((group, frames, dense + FLAG_ROWS, LANES), BF16),
                pltpu.VMEM((group, frames, dense, LANES), BF16),
                pltpu.VMEM((2, dense, LANES), BF16),
                pltpu.VMEM((group, dense, LANES), BF16),
            ],
            2 * frames * group * share * 3 * channels * channels,
            name="time_mix",
            wait=before,
        )
        return res_two, normed, flags, *picked

    def exchange(shares):
        return [shares[0]] + [lax.ppermute(shares[d], "clip", swaps[d]) for d in range(1, group)]

    def shared_kv(sources):
        (shared,) = call(
            functools.partial(shared_kernel, len(sources), contexts, 8 + 3 * group, share),
            [struct((contexts * share, 2 * wide))],
            [SMEM] + [HBM] * len(sources) + [VMEM],
            [scalars, *sources, wide_kv],
            [
                pltpu.VMEM((contexts, dense, LANES), BF16),
                pltpu.VMEM((contexts * share, channels), BF16),
                pltpu.SemaphoreType.DMA((contexts,)),
            ],
            name="shared",
        )
        return shared

    def pack(normed):
        (packed,) = call(
            pack_kernel,
            [struct((group, frames * share, 3 * wide))],
            [VMEM] * 3,
            [normed, wide_q, wide_kv],
            name="pack",
        )
        return packed

    def attention(res_two, flags, packed, shared, who, wait=()):
        return call(
            functools.partial(attend_kernel, contexts, who),
            [struct((frames, dense, LANES))] * len(who),
            [SMEM] + [VMEM] * 6 + [HBM],
            [scalars, shared, packed, flags, wide_out, gather, spread, res_two],
            [
                pltpu.VMEM((len(who), frames * share, keys * wide), BF16),
                pltpu.VMEM((2, frames * share, keys * wide), F32),
                pltpu.VMEM((frames * share, wide), BF16),
                pltpu.VMEM((len(who), frames, share, channels), BF16),
                pltpu.SemaphoreType.DMA((len(who),)),
            ],
            name="attend",
            mib=26,
            wait=wait,
        )

    def give_back(who, outs):
        return [lax.ppermute(out, "clip", swaps[d]) if d else out for d, out in zip(who, outs, strict=True)]

    def across(normed, both, low, high, wait=()):
        got = send_near(both, low, high, levels, group)
        packed = pack(normed)
        return packed, *send_on(both, high, got, levels, group, (packed, *wait))

    own = exchange(shares_of[0])
    later = [exchange(shares) for shares in shares_of[1:]]
    res_two, normed, flags, *picked = mix(own)
    packed, buffers, turned = across(normed, *picked)
    parts = []
    for own in later:
        shared = shared_kv(buffers)
        far_outs = attention(res_two, flags, packed, shared, (2, 3))
        next_res_two, normed, next_flags, *picked = mix(own, *turned)
        next_packed, buffers, turned = across(normed, *picked, far_outs[:1])
        near_outs = attention(res_two, flags, packed, shared, (0, 1), turned)
        parts += give_back((0, 1), near_outs) + give_back((2, 3), far_outs)
        res_two, flags, packed = next_res_two, next_flags, next_packed
    shared = shared_kv(buffers)
    most = attention(res_two, flags, packed, shared, (1, 2, 3))
    parts += attention(res_two, flags, packed, shared, (0,), most[:1])
    parts += give_back((1, 2, 3), most)
    (result,) = call(
        functools.partial(assemble_kernel, group, chunks),
        [whole],
        [SMEM] + [VMEM] * len(parts),
        [scalars, *parts],
        name="assemble",
    )
    return result.reshape(frames, rows, cols, channels)


def solution(mesh):
    placed = (P("clip", "tile", None, None), P("clip"), P(), P(), P(), P(), P(), P(), P(), P(), P())
    return jax.shard_map(
        local, mesh=mesh, in_specs=placed, out_specs=P("clip", "tile", None, None), check_vma=False
    )
```

```python
import functools
import math

import jax
import jax.numpy as jnp
import ml_dtypes
import numpy as np
from jax import lax
from jax.experimental import pallas as pl
from jax.experimental.pallas import tpu as pltpu
from jax.sharding import PartitionSpec as P

HEAD_DIM = 64
GROUPS = 32
H = 40
W = 64
EPS = 1e-05
MASKED = -1e30
LANES = 128
FLAG_ROWS = 16
F32 = jnp.float32
BF16 = jnp.bfloat16

SMEM = pl.BlockSpec(memory_space=pltpu.SMEM)
VMEM = pl.BlockSpec(memory_space=pltpu.VMEM)
ANY = pl.BlockSpec(memory_space=pl.ANY)
HBM = pl.BlockSpec(memory_space=pltpu.HBM)


def call(kernel, out_shape, in_specs, args, scratch=(), flops=0, name=None, mib=8, wait=()):
    count = len(args)

    def body(*refs):
        kernel(*refs[:count], *refs[count + len(wait) :])

    return pl.pallas_call(
        body,
        out_shape=out_shape,
        in_specs=[*in_specs, *[ANY] * len(wait)],
        out_specs=[VMEM] * len(out_shape),
        scratch_shapes=list(scratch),
        compiler_params=pltpu.CompilerParams(vmem_limit_bytes=mib * 1024 * 1024),
        cost_estimate=pl.CostEstimate(flops=1, bytes_accessed=1, transcendentals=0),
        name=name,
    )(*args, *wait)


def struct(shape, dtype=BF16):
    return jax.ShapeDtypeStruct(shape, dtype)


def silu(x):
    return 0.5 * x * (1.0 + jnp.tanh(0.5 * x))


def column_sums(v):
    folded = v.reshape(v.shape[0] // 8, 8, v.shape[1])
    return jnp.sum(folded, axis=0), jnp.sum(folded * folded, axis=0)


def split3(x):
    high = x.astype(BF16)
    rest = x - high.astype(F32)
    mid = rest.astype(BF16)
    return high, mid, (rest - mid.astype(F32)).astype(BF16)


def put_stats(f, sums, stats_ref, msg_ref, cols):
    channels = sums.shape[1]
    stats_ref[f] = jnp.concatenate([sums, jnp.zeros((6, channels), F32)], axis=0)
    high, mid, low = split3(sums)
    parts = [high, mid, low, jnp.zeros((FLAG_ROWS - 6, channels), BF16)]
    packed = jnp.concatenate([p.astype(F32) for p in parts], axis=0)
    msg_ref[f, pl.ds(cols, FLAG_ROWS), :] = packed.astype(BF16)


def edge_start(cells, cols):
    return pl.multiple_of(jnp.where(lax.axis_index("tile") == 0, cells - cols, 0), cols)


def stats_kernel(cols, x_ref, stats_ref, msg_ref):
    frames, cells, channels = x_ref.shape
    step = 2 * cols if cells % (2 * cols) == 0 else cols
    for f in range(frames):

        def body(i, carry):
            v = x_ref[f, pl.ds(pl.multiple_of(i * step, step), step), :].astype(F32)
            s, q = column_sums(v)
            return carry[0] + s, carry[1] + q

        zero = jnp.zeros((8, channels), F32)
        s, q = lax.fori_loop(0, cells // step, body, (zero, zero))
        sums = jnp.concatenate(
            [jnp.sum(s, axis=0, keepdims=True), jnp.sum(q, axis=0, keepdims=True)], axis=0
        )
        put_stats(f, sums, stats_ref, msg_ref, cols)
        edge = edge_start(cells, cols)
        msg_ref[f, pl.ds(0, cols), :] = x_ref[f, pl.ds(edge, cols), :]


def arrange(pieces):
    big = pieces[0].shape[1] // 256 * 256
    return jnp.concatenate([p[:, :big] for p in pieces] + [p[:, big:] for p in pieces], axis=1)


def spans(index, channels):
    big = channels // 256 * 256
    return ((index * big, big, 0), (3 * big + index * (channels - big), channels - big, big))


def lay_conv(source, target):
    channels = source.shape[1]
    for a in range(3):
        for b in range(3):
            for row, height, from_row in spans(b, channels):
                for col, width, from_col in spans(a, channels):
                    target[row : row + height, col : col + width] = source[
                        3 * a + b, from_row : from_row + height, from_col : from_col + width
                    ]


def first_weights_kernel(first_ref, wide_first):
    lay_conv(first_ref, wide_first)


def weights_kernel(second_ref, time_ref, qkv_ref, out_ref, wide_second, wide_time, wide_q, wide_kv, wide_out):
    channels = out_ref.shape[0]
    lay_conv(second_ref, wide_second)
    for b in range(3):
        for row, height, from_row in spans(b, channels):
            wide_time[row : row + height, :] = time_ref[b, from_row : from_row + height, :]
    wide = wide_out.shape[0]
    wide_q[...] = jnp.zeros_like(wide_q)
    wide_kv[...] = jnp.zeros_like(wide_kv)
    wide_q[:, 0:channels] = qkv_ref[:, 0:channels]
    for part in range(2):
        wide_kv[:, part * wide : part * wide + channels] = qkv_ref[:, (part + 1) * channels : (part + 2) * channels]
    wide_out[...] = jnp.zeros_like(wide_out)
    wide_out[0:channels, :] = out_ref[...]


def conv_kernel(cols, total_cells, first_row, rows, residual, block_rows, x_ref, stats_ref, top_ref, bottom_ref, gain_ref, w_ref, *rest):
    if residual:
        res_in_ref, scalars, *share_refs, wide_x, wide_y, res_rows, res_sem, share_ref = rest
        here = pl.ds(first_row * cols, rows * cols)
        res_copy = pltpu.make_async_copy(res_in_ref.at[:, here], res_rows, res_sem)
        res_copy.start()
        share = cols * rows // share_ref.shape[0]
    else:
        out_ref, out_stats_ref, msg_ref, wide_x, wide_y = rest
    frames, cells, channels = x_ref.shape
    tile_rows = cells // cols
    big = channels // 256 * 256
    small = channels - big
    group_width = channels // GROUPS
    row_group = lax.broadcasted_iota(jnp.int32, (channels, channels), 0) // group_width
    col_group = lax.broadcasted_iota(jnp.int32, (channels, channels), 1) // group_width
    same = (row_group == col_group).astype(F32)
    column = lax.broadcasted_iota(jnp.int32, (cols, 1), 0)
    leftmost, rightmost = column == 0, column == cols - 1

    scales = []
    for f in range(frames):
        other = top_ref[f, pl.ds(cols, FLAG_ROWS), :].astype(F32)
        sums = stats_ref[f, 0:2, :] + other[0:2] + other[2:4] + other[4:6]
        sums = jnp.concatenate([sums, jnp.zeros((6, channels), F32)], axis=0)
        means = jnp.dot(
            sums, same, preferred_element_type=F32, precision=lax.Precision.HIGHEST
        ) / (total_cells * group_width)
        centre = means[0:1]
        scale = lax.rsqrt(means[1:2] - centre * centre + EPS) * gain_ref[...]
        scales.append((scale, -centre * scale))

    def widen(f, padded_row):
        row = first_row + padded_row - 1
        if row < 0:
            raw, keep = top_ref[f, 0:cols, :], lax.axis_index("tile") > 0
        elif row >= tile_rows:
            raw, keep = bottom_ref[f, 0:cols, :], lax.axis_index("tile") < lax.axis_size("tile") - 1
        else:
            raw, keep = x_ref[f, row * cols : (row + 1) * cols, :], None
        scale, shift = scales[f]
        y = silu(raw.astype(F32) * scale + shift)
        if keep is not None:
            y = jnp.where(keep, y, 0.0)
        left = jnp.where(leftmost, 0.0, pltpu.roll(y, 1, 0))
        right = jnp.where(rightmost, 0.0, pltpu.roll(y, cols - 1, 0))
        wide_x[f, padded_row * cols : (padded_row + 1) * cols, :] = arrange([left, y, right]).astype(BF16)

    def multiply(f, start, stop):
        here = slice(start * cols, stop * cols)
        wide_y[f, here, :] = jnp.dot(wide_x[f, here, :], w_ref[...], preferred_element_type=F32)

    totals = [[jnp.zeros((8, channels), F32)] * 2 for _ in range(frames)]

    def finish(f, r):
        parts = []
        for base, width in ((0, big), (3 * big, small)):
            parts.append(
                wide_y[f, r * cols : (r + 1) * cols, base : base + width]
                + wide_y[f, (r + 1) * cols : (r + 2) * cols, base + width : base + 2 * width]
                + wide_y[f, (r + 2) * cols : (r + 3) * cols, base + 2 * width : base + 3 * width]
            )
        total = jnp.concatenate(parts, axis=1)
        here = slice(r * cols, (r + 1) * cols)
        if residual:
            total = (res_rows[f, here, :].astype(F32) + total).astype(BF16)
            put_share(scalars, share_ref, f, r * cols, total, share)
        else:
            total = total.astype(BF16)
            out_ref[f, here, :] = total
            s, q = column_sums(total.astype(F32))
            totals[f] = [totals[f][0] + s, totals[f][1] + q]

    blocks = []
    for f in range(frames):
        edges = list(range(0, rows + 2, block_rows)) + [rows + 2]
        blocks += [(f, edges[i], edges[i + 1]) for i in range(len(edges) - 1)]

    def act(block):
        for p in range(block[1], block[2]):
            widen(block[0], p)

    def end(block):
        for p in range(block[1], block[2]):
            if p >= 2:
                finish(block[0], p - 2)

    act(blocks[0])
    if residual:
        res_copy.wait()
    for i, block in enumerate(blocks):
        multiply(*block)
        if i + 1 < len(blocks):
            act(blocks[i + 1])
        if i > 0:
            end(blocks[i - 1])
    end(blocks[-1])
    if residual:
        for f in range(frames):
            flag = jnp.full((FLAG_ROWS, LANES), jnp.where(f < scalars[3], 1.0, 0.0), F32)
            for d in range(share_ref.shape[0]):
                share_ref[d, f, pl.ds(dense_rows(share)[0], FLAG_ROWS), :] = flag.astype(BF16)
        for d, ref in enumerate(share_refs):
            ref[...] = share_ref[d]
    else:
        for f in range(frames):
            sums = jnp.concatenate([jnp.sum(t, axis=0, keepdims=True) for t in totals[f]], axis=0)
            put_stats(f, sums, out_stats_ref, msg_ref, cols)
            edge = edge_start(cells, cols)
            msg_ref[f, pl.ds(0, cols), :] = out_ref[f, pl.ds(edge, cols), :]


def dense_rows(share):
    half = (share // 2 + 15) // 16 * 16
    return 2 * share + half, half


def put_dense(ref, where, start, x, share):
    _, half = dense_rows(share)
    count = x.shape[0]
    ref[(*where, slice(start, start + count), slice(None))] = x[:, 0:LANES]
    ref[(*where, slice(share + start, share + start + count), slice(None))] = x[:, LANES : 2 * LANES]
    rest = x.shape[1] - 2 * LANES
    side, row = (0, start) if start < half else (1, start - half)
    row += 2 * share
    ref[(*where, slice(row, row + count), slice(side * rest, (side + 1) * rest))] = x[:, 2 * LANES :]


def get_dense(ref, where, start, count, share, channels):
    _, half = dense_rows(share)
    rest = channels - 2 * LANES
    side, row = (0, start) if start < half else (1, start - half)
    row += 2 * share
    third = ref[(*where, slice(row, row + count), slice(None))]
    return jnp.concatenate(
        [
            ref[(*where, slice(start, start + count), slice(None))],
            ref[(*where, slice(share + start, share + start + count), slice(None))],
            third[:, side * rest : (side + 1) * rest],
        ],
        axis=1,
    )


def halves(share):
    _, half = dense_rows(share)
    return ((0, half), (half, share - half))


def put_share(scalars, out_ref, f, start, total, share):
    piece = math.gcd(math.gcd(share, total.shape[0]), dense_rows(share)[1])
    for p in range(0, total.shape[0], piece):
        owner, inside = divmod(start + p, share)
        put_dense(out_ref, (scalars[8 + owner], f), inside, total[p : p + piece], share)


def ends_kernel(group, scalars, *rest):
    own, (one_ref, two_ref) = rest[:group], rest[group:]
    dense = one_ref.shape[0]
    odd = scalars[5] > 0
    for d in range(group):
        for ref, upper in ((one_ref, odd), (two_ref, jnp.logical_not(odd))):

            @pl.when(jnp.logical_and(jnp.logical_not(upper), scalars[4] ^ d == group - 1))
            def _():
                live = own[d][1, pl.ds(dense, FLAG_ROWS), :].astype(F32)[0:1] > 0.5
                ref[...] = jnp.where(
                    live, own[d][1, 0:dense, :].astype(F32), own[d][0, 0:dense, :].astype(F32)
                ).astype(BF16)

            @pl.when(jnp.logical_and(upper, scalars[4] == d))
            def _():
                ref[...] = own[d][0, 0:dense, :]


def time_kernel(group, scalars, *rest):
    own, (one_ref, two_ref, w_ref, gain_ref) = rest[:group], rest[group : group + 4]
    res_two_ref, normed_ref, flag_ref, *pick_refs, ordered, moving, edge, picks = rest[group + 4 :]
    _, frames, share, channels = res_two_ref.shape
    dense = one_ref.shape[0]
    odd = scalars[5] > 0
    for d in range(group):
        ordered[scalars[8 + d]] = own[d][...]

    def lively(x):
        return silu(x.astype(F32)).astype(BF16)

    for m in range(group):
        for f in range(frames):
            moving[m, f] = lively(ordered[m, f, 0:dense, :])
    one, two = one_ref[...].astype(F32), two_ref[...].astype(F32)
    edge[0] = lively(jnp.where(odd, one, two))
    edge[1] = lively(jnp.where(odd, two, one))
    live = [ordered[m, 1, dense : dense + FLAG_ROWS, :].astype(F32)[0:1, 0:1] > 0.5 for m in range(group)]
    for m in range(group):
        for start, step in halves(share):

            def cells(ref, *where):
                return get_dense(ref, where, start, step, share, channels).astype(F32)

            here = slice(start, start + step)
            first, second = cells(moving, m, 0), cells(moving, m, 1)
            if m:
                prior = jnp.where(live[m - 1], cells(moving, m - 1, 1), cells(moving, m - 1, 0))
            else:
                prior = cells(edge, 0)
            later = cells(moving, m + 1, 0) if m + 1 < group else cells(edge, 1)
            rows = [
                arrange([prior, first, jnp.where(live[m], second, later)]),
                arrange([first, second, jnp.where(live[m], later, 0.0)]),
            ]
            mixed = jnp.dot(
                jnp.concatenate(rows, axis=0).astype(BF16), w_ref[...], preferred_element_type=F32
            )
            norms = []
            for f in range(frames):
                total = (cells(ordered, m, f) + mixed[f * step : (f + 1) * step]).astype(BF16)
                res_two_ref[m, f, here, :] = total
                v = total.astype(F32)
                v = v - jnp.mean(v, axis=1, keepdims=True)
                spread = jnp.mean(v * v, axis=1, keepdims=True)
                normed = v * lax.rsqrt(spread + EPS) * gain_ref[...]
                norms.append(normed)
                normed_ref[m, f, here, :] = normed.astype(BF16)
            picked = jnp.where(scalars[8 + group + m] > 0, norms[1], norms[0]).astype(BF16)
            put_dense(picks, (scalars[8 + 2 * group + m],), start, picked, share)
        for f in range(frames):
            flag_ref[m, f] = ordered[m, f, dense : dense + FLAG_ROWS, :].astype(F32)[0:8]
    both_ref, *part_refs = pick_refs
    both_ref[...] = picks[...]
    for i, ref in enumerate(part_refs):
        ref[...] = picks[2 * i : 2 * i + 2]


def pack_kernel(normed_ref, wq_ref, wkv_ref, packed_ref):
    group, frames, _, _ = normed_ref.shape
    wide = wq_ref.shape[1]
    for m in range(group):
        rows = jnp.concatenate([normed_ref[m, f] for f in range(frames)], axis=0)
        packed_ref[m, :, 0:wide] = jnp.dot(rows, wq_ref[...], preferred_element_type=F32).astype(BF16)
        packed_ref[m, :, wide:] = jnp.dot(rows, wkv_ref[...], preferred_element_type=F32).astype(BF16)


def head_maps(keys, channels, wide):
    column = np.arange(keys * wide)
    lane = column // wide * 8 + column % wide // HEAD_DIM
    hit = (lane[:, None] == np.arange(LANES)[None, :]) & (column % wide < channels)[:, None]
    return (hit * HEAD_DIM ** (-0.5)).astype(ml_dtypes.bfloat16), hit.T.astype(ml_dtypes.bfloat16)


def shared_kernel(buffers, contexts, base, share, scalars, *rest):
    sources, (wkv_ref, shared_ref, dense_context, context, sems) = rest[:buffers], rest[buffers:]
    channels = context.shape[1]
    for j in range(contexts):
        for b in range(buffers):

            @pl.when(scalars[base + 2 * j] == b)
            def _():
                pltpu.make_async_copy(
                    sources[b].at[scalars[base + 1 + 2 * j]], dense_context.at[j], sems.at[j]
                ).start()

    for j in range(contexts):
        pltpu.make_async_copy(sources[0].at[0], dense_context.at[j], sems.at[j]).wait()
        for start, count in halves(share):
            at = j * share + start
            context[at : at + count, :] = get_dense(dense_context, (j,), start, count, share, channels)
    half = contexts // 2 * share
    for s in (0, half):
        shared_ref[s : s + half, :] = jnp.dot(
            context[s : s + half, :], wkv_ref[...], preferred_element_type=F32
        ).astype(BF16)


def attend_kernel(contexts, who, scalars, shared, packed_ref, flag_ref, wout_ref, gather_ref, spread_ref, res_hbm, *rest):
    out_refs = rest[: len(who)]
    products, spreads, joined, res_ref, res_sems = rest[len(who) :]
    _, frames, share, channels = res_ref.shape
    heads = channels // HEAD_DIM
    wide = wout_ref.shape[0]
    keys = frames + contexts
    at_member = [scalars[8 + d] for d in who]
    res_copies = [
        pltpu.make_async_copy(res_hbm.at[at], res_ref.at[i], res_sems.at[i]) for i, at in enumerate(at_member)
    ]
    for copy in res_copies:
        copy.start()
    lane = lax.broadcasted_iota(jnp.int32, (1, LANES), 1)
    in_use = jnp.logical_and(lane % 8 < heads, lane // 8 < keys)

    piece = 32 if share % 32 == 0 else 16

    def key_value(m, j, s, part):
        if j < frames:
            at = j * share + s
            return packed_ref[at_member[m], at : at + piece, (1 + part) * wide : (2 + part) * wide]
        at = (j - frames) * share + s
        return shared[at : at + piece, part * wide : (part + 1) * wide]

    def multiply(m):
        for s in range(0, share, piece):
            queries = [packed_ref[at_member[m], f * share + s : f * share + s + piece, 0:wide] for f in range(frames)]
            for j in range(keys):
                key = key_value(m, j, s, 0)
                for f in range(frames):
                    at = f * share + s
                    products[m, at : at + piece, j * wide : (j + 1) * wide] = queries[f] * key

    def weigh(m):
        flags = flag_ref[at_member[m]]
        visible = in_use
        for f in range(frames):
            dead = jnp.logical_and(lane // 8 == f, flags[f, 0:1] < 0.5)
            visible = jnp.logical_and(visible, jnp.logical_not(dead))
        scores = scored[m]
        scores = jnp.where(visible, scores, MASKED)
        top = scores
        for shift in (8, 16, 32, 64):
            top = jnp.maximum(top, pltpu.roll(top, shift, 1))
        raised = jnp.exp(scores - top)
        total = raised
        for shift in (8, 16, 32, 64):
            total = total + pltpu.roll(total, shift, 1)
        weights = (raised / total).astype(BF16)
        spreads[m % 2] = jnp.dot(weights, spread_ref[...], preferred_element_type=F32)

    def combine(m):
        for s in range(0, share, piece):
            results = [jnp.zeros((piece, wide), F32) for _ in range(frames)]
            for j in range(keys):
                value = key_value(m, j, s, 1).astype(F32)
                for f in range(frames):
                    at = f * share + s
                    results[f] = results[f] + spreads[m % 2, at : at + piece, j * wide : (j + 1) * wide] * value
            for f in range(frames):
                joined[f * share + s : f * share + s + piece, :] = results[f].astype(BF16)
        added = jnp.dot(joined[...], wout_ref[...], preferred_element_type=F32)
        for f in range(frames):
            live = flag_ref[at_member[m], f, 0:1, 0:1] > 0.5
            total = res_ref[m, f].astype(F32) + added[f * share : (f + 1) * share]
            total = jnp.where(live, total, 0.0).astype(BF16)
            for start, count in halves(share):
                put_dense(out_refs[m], (f,), start, total[start : start + count], share)

    count = len(who)
    for m in range(count):
        multiply(m)
    rows = frames * share if count > 3 or frames * share % 64 else frames * share // 4
    scored = [
        jnp.concatenate(
            [
                jnp.dot(products[m, at : at + rows], gather_ref[...], preferred_element_type=F32)
                for at in range(0, frames * share, rows)
            ],
            axis=0,
        )
        for m in range(count)
    ]
    for copy in res_copies:
        copy.wait()
    for m in range(count):
        weigh(m)
        if m > 0:
            combine(m - 1)
    combine(count - 1)


def assemble_kernel(group, chunks, scalars, *rest):
    parts, out_ref = rest[:-1], rest[-1]
    frames, cells, channels = out_ref.shape
    share = cells // (chunks * group)
    for c in range(chunks):
        for d in range(group):
            place = (c * group + scalars[8 + d]) * share
            for f in range(frames):
                for start, count in halves(share):
                    out_ref[f, pl.ds(pl.multiple_of(place + start, 16), count), :] = get_dense(
                        parts[c * group + d], (f,), start, count, share, channels
                    )


def share_tile(stats, msg, source, cols):
    tiles = lax.axis_size("tile")
    if tiles == 2:
        got = lax.ppermute(msg, "tile", [(0, 1), (1, 0)])
        return stats, got, got
    down = [(i, i + 1) for i in range(tiles - 1)]
    up = [(i + 1, i) for i in range(tiles - 1)]
    pad = ((0, 0), (0, FLAG_ROWS), (0, 0))
    top = lax.ppermute(source[:, -cols:], "tile", down)
    bottom = lax.ppermute(source[:, :cols], "tile", up)
    return lax.psum(stats, "tile"), jnp.pad(top, pad), jnp.pad(bottom, pad)


def place_of(level, source, slot, levels):
    if levels != 4:
        hop = level - source
        return jnp.where(hop >= 0, hop, levels - 1 - hop), slot
    apart = level ^ source
    late = slot > 1
    outer = jnp.logical_or(level == 0, level == 3)
    from_outer = jnp.logical_or(source == 0, source == 3)
    whole = jnp.logical_or(apart < 2, jnp.logical_and(apart == 3, outer))
    two = jnp.where(late, jnp.where(from_outer, 5, 7), 4)
    three = jnp.where(outer, 2, jnp.where(late, 6, 3))
    buffer = jnp.where(apart < 2, apart, jnp.where(apart == 2, two, three))
    return buffer, jnp.where(jnp.logical_or(whole, jnp.logical_not(late)), slot, slot - 2)


def plan_kernel(group, frames, length, lengths_ref, context_ref, out_ref):
    contexts = context_ref.shape[0]
    levels = lax.axis_size("clip") // group
    clip = lax.axis_index("clip")
    level, member = lax.div(clip, group), lax.rem(clip, group)
    for i in range(length):
        out_ref[i] = 0
    out_ref[3] = lengths_ref[0]
    out_ref[4] = member
    out_ref[5] = lax.rem(level, 2)
    frame = [context_ref[j] for j in range(contexts)]
    owner = [lax.div(c, frames) for c in frame]
    source = [lax.div(c, group) for c in owner]

    def one(flag):
        return jnp.where(flag, 1, 0)

    for j in range(contexts):
        slot = 0
        for i in range(contexts):
            if i != j:
                slot = slot + one(jnp.logical_and(source[i] == source[j], owner[i] < owner[j]))
        buffer, place = place_of(level, source[j], slot, levels)
        out_ref[8 + 3 * group + 2 * j] = buffer
        out_ref[9 + 3 * group + 2 * j] = place
    named, second = [], []
    for m in range(group):
        mine = level * group + m
        hit, late = 0, 0
        for j in range(contexts):
            hit = jnp.maximum(hit, one(owner[j] == mine))
            late = jnp.maximum(late, one(frame[j] == mine * frames + 1))
        named.append(hit)
        second.append(late)
    before, empty = 0, sum(named)
    for m in range(group):
        out_ref[8 + m] = member ^ m
        out_ref[8 + group + m] = second[m]
        out_ref[8 + 2 * group + m] = jnp.where(named[m] > 0, before, empty)
        before, empty = before + named[m], empty + 1 - named[m]


def send(x, pairs, group):
    return lax.ppermute(x, "clip", [(a * group + i, b * group + i) for a, b in pairs for i in range(group)])


SWAP = [(0, 1), (1, 0), (2, 3), (3, 2)]


def turn_kernel(far_ref, far_high_ref, high_ref, on_ref, late_ref):
    on_ref[0:2] = far_ref[...]
    on_ref[2:4] = far_high_ref[...]
    late_ref[...] = high_ref[...]


def send_near(both, low, high, levels, group):
    if levels != 4:
        return (both,)
    return (
        send(low, [(0, 2), (2, 0), (1, 3), (3, 1)], group),
        send(high, [(0, 2), (3, 1)], group),
        send(low, [(1, 2), (2, 1)], group),
        send(both, [(0, 1), (1, 0), (2, 3), (3, 2)], group),
    )


def send_on(both, high, got, levels, group, wait):
    if levels != 4:
        lower, upper = [both], [both]
        for _ in range(levels - 1):
            lower.append(send(lower[-1], [(i, i + 1) for i in range(levels - 1)], group))
            upper.append(send(upper[-1], [(i + 1, i) for i in range(levels - 1)], group))
        return lower + upper[1:], got
    far, far_high, middle, near = got
    on, late = call(
        turn_kernel,
        [struct(both.shape), struct(high.shape)],
        [VMEM] * 3,
        [far, far_high, high],
        name="turn",
        wait=(near, middle, *wait),
    )
    outer = send(on, [(1, 0), (2, 3)], group)
    middle_late = send(late, [(1, 2), (2, 1)], group)
    far_late = send(late, [(1, 3), (2, 0)], group)
    return [both, near, outer, middle, far, far_high, middle_late, far_late], (on,)


def local(
    latents,
    lengths,
    context,
    gain_first,
    conv_first,
    gain_second,
    conv_second,
    time_weight,
    attn_gain,
    w_qkv,
    w_out,
):
    frames, rows, cols, channels = latents.shape
    cells = rows * cols
    tiles, clips = lax.axis_size("tile"), lax.axis_size("clip")
    group = 4
    chunks = 2 if rows % 2 == 0 and cells % (2 * group * 16) == 0 else 1
    levels = clips // group
    share = cells // (group * chunks)
    dense, _ = dense_rows(share)
    contexts = context.shape[0]
    total_cells = cells * tiles
    wide = (channels + LANES - 1) // LANES * LANES
    keys = frames + contexts

    length = 8 + 3 * group + 2 * contexts
    scalars = pl.pallas_call(
        functools.partial(plan_kernel, group, frames, length),
        out_shape=struct((length,), jnp.int32),
        in_specs=[SMEM] * 2,
        out_specs=SMEM,
        compiler_params=pltpu.CompilerParams(vmem_limit_bytes=1024 * 1024),
        name="plan",
    )(lengths, context)

    x = latents.reshape(frames, cells, channels)
    message = struct((frames, cols + FLAG_ROWS, channels))
    sums = struct((frames, 8, channels), F32)
    whole = struct((frames, cells, channels))
    stats, msg = call(
        functools.partial(stats_kernel, cols), [sums, message], [VMEM], [x], name="first_sums"
    )
    stats, top, bottom = share_tile(stats, msg, x, cols)
    square = struct((3 * channels, 3 * channels))
    (wide_first,) = call(
        first_weights_kernel, [square], [VMEM], [conv_first.reshape(9, channels, channels)], name="first_weights"
    )
    gather, spread = (jnp.asarray(a) for a in head_maps(keys, channels, wide))

    part = struct((frames, dense + FLAG_ROWS, LANES))

    def conv(first_row, count, residual, outs, source, stats, top, bottom, gain, weight, *more):
        scratch = [
            pltpu.VMEM((frames, (count + 2) * cols, 3 * channels), BF16),
            pltpu.VMEM((frames, (count + 2) * cols, 3 * channels), F32),
        ]
        if residual:
            scratch += [
                pltpu.VMEM((frames, count * cols, channels), BF16),
                pltpu.SemaphoreType.DMA,
                pltpu.VMEM((group, *part.shape), BF16),
            ]
        block_rows = 11 if count == 20 else 8
        return call(
            functools.partial(conv_kernel, cols, total_cells, first_row, count, residual, block_rows),
            outs,
            [VMEM] * 6 + [HBM, SMEM][: len(more)],
            [source, stats, top, bottom, gain.reshape(1, channels), weight, *more],
            scratch,
            2 * frames * (count + 2) * cols * 9 * channels * channels,
            name="conv_two" if residual else "conv_one",
            mib=17 if residual else 22,
        )

    hidden, stats, msg = conv(0, rows, False, [whole, sums, message], x, stats, top, bottom, gain_first, wide_first)
    wide_second, wide_time, wide_q, wide_kv, wide_out = call(
        weights_kernel,
        [
            square,
            struct((3 * channels, channels)),
            struct((channels, wide)),
            struct((channels, 2 * wide)),
            struct((wide, channels)),
        ],
        [VMEM] * 4,
        [conv_second.reshape(9, channels, channels), time_weight, w_qkv, w_out],
        name="weights",
        wait=(stats,),
    )
    stats, top, bottom = share_tile(stats, msg, hidden, cols)
    swaps = [[(i, i ^ d) for i in range(clips)] for d in range(group)]
    pairs = [[(i, i + 1) for i in range(a, levels - 1, 2)] for a in range(2)]
    beside = [
        [(u * group + i, v * group + i) for a, b in p for u, v in ((a, b), (b, a)) for i in range(group)] for p in pairs
    ]

    shares_of = []
    for c in range(chunks):
        shares = conv(
            c * rows // chunks,
            rows // chunks,
            True,
            [part] * group,
            hidden,
            stats,
            top,
            bottom,
            gain_second,
            wide_second,
            x,
            scalars,
        )
        shares_of.append(shares)

    def mix(own, *before):
        end = struct((dense, LANES))
        one, two = call(
            functools.partial(ends_kernel, group), [end, end], [SMEM] + [VMEM] * group, [scalars, *own], name="ends",
            wait=shares_of[-1][:1],
        )
        one = lax.ppermute(one, "clip", beside[0])
        two = lax.ppermute(two, "clip", beside[1])
        both = (group, frames, share, channels)
        res_two, normed, flags, *picked = call(
            functools.partial(time_kernel, group),
            [struct(both), struct(both), struct((group, frames, 8, LANES), F32), struct((group, dense, LANES))] + [struct((2, dense, LANES))] * (group // 2),
            [SMEM] + [VMEM] * (group + 4),
            [scalars, *own, one, two, wide_time, attn_gain.reshape(1, channels)],
            [
                pltpu.VMEM((group, frames, dense + FLAG_ROWS, LANES), BF16),
                pltpu.VMEM((group, frames, dense, LANES), BF16),
                pltpu.VMEM((2, dense, LANES), BF16),
                pltpu.VMEM((group, dense, LANES), BF16),
            ],
            2 * frames * group * share * 3 * channels * channels,
            name="time_mix",
            wait=before,
        )
        return res_two, normed, flags, *picked

    def exchange(shares):
        return [shares[0]] + [lax.ppermute(shares[d], "clip", swaps[d]) for d in range(1, group)]

    def shared_kv(sources):
        (shared,) = call(
            functools.partial(shared_kernel, len(sources), contexts, 8 + 3 * group, share),
            [struct((contexts * share, 2 * wide))],
            [SMEM] + [HBM] * len(sources) + [VMEM],
            [scalars, *sources, wide_kv],
            [
                pltpu.VMEM((contexts, dense, LANES), BF16),
                pltpu.VMEM((contexts * share, channels), BF16),
                pltpu.SemaphoreType.DMA((contexts,)),
            ],
            name="shared",
        )
        return shared

    def pack(normed):
        (packed,) = call(
            pack_kernel,
            [struct((group, frames * share, 3 * wide))],
            [VMEM] * 3,
            [normed, wide_q, wide_kv],
            name="pack",
        )
        return packed

    def attention(res_two, flags, packed, shared, who, wait=()):
        return call(
            functools.partial(attend_kernel, contexts, who),
            [struct((frames, dense, LANES))] * len(who),
            [SMEM] + [VMEM] * 6 + [HBM],
            [scalars, shared, packed, flags, wide_out, gather, spread, res_two],
            [
                pltpu.VMEM((len(who), frames * share, keys * wide), BF16),
                pltpu.VMEM((2, frames * share, keys * wide), F32),
                pltpu.VMEM((frames * share, wide), BF16),
                pltpu.VMEM((len(who), frames, share, channels), BF16),
                pltpu.SemaphoreType.DMA((len(who),)),
            ],
            name="attend",
            mib=22,
            wait=wait,
        )

    def give_back(who, outs):
        return [lax.ppermute(out, "clip", swaps[d]) if d else out for d, out in zip(who, outs, strict=True)]

    def across(normed, both, low, high, wait=()):
        got = send_near(both, low, high, levels, group)
        packed = pack(normed)
        return packed, *send_on(both, high, got, levels, group, (packed, *wait))

    own = exchange(shares_of[0])
    later = [exchange(shares) for shares in shares_of[1:]]
    res_two, normed, flags, *picked = mix(own)
    packed, buffers, turned = across(normed, *picked)
    parts = []
    for own in later:
        shared = shared_kv(buffers)
        far_outs = attention(res_two, flags, packed, shared, (2, 3))
        next_res_two, normed, next_flags, *picked = mix(own, *turned)
        next_packed, buffers, turned = across(normed, *picked, far_outs[:1])
        near_outs = attention(res_two, flags, packed, shared, (0, 1), turned)
        parts += give_back((0, 1), near_outs) + give_back((2, 3), far_outs)
        res_two, flags, packed = next_res_two, next_flags, next_packed
    shared = shared_kv(buffers)
    most = attention(res_two, flags, packed, shared, (1, 2, 3))
    parts += attention(res_two, flags, packed, shared, (0,), most[:1])
    parts += give_back((1, 2, 3), most)
    (result,) = call(
        functools.partial(assemble_kernel, group, chunks),
        [whole],
        [SMEM] + [VMEM] * len(parts),
        [scalars, *parts],
        name="assemble",
    )
    return result.reshape(frames, rows, cols, channels)


def solution(mesh):
    placed = (P("clip", "tile", None, None), P("clip"), P(), P(), P(), P(), P(), P(), P(), P(), P())
    return jax.shard_map(
        local, mesh=mesh, in_specs=placed, out_specs=P("clip", "tile", None, None), check_vma=False
    )
```
